32 devices in a mesh: space: 8 (over y, x, core), modes: 4 (over z).
Axes of the slice: x: 2, y: 2, z: 4, core: 2. Of those that a mesh axis runs over, the one named last changes fastest.
Arguments:
- voltage_expansion: float32 [220, 8, 2048], P('modes', 'space'), may hold values from -6 to 6
- current_injection: float32 [220, 8, 2048], P('modes', 'space'), may hold values from -48 to 48
- thermal_state: float32 [220, 8, 2048], P('modes', 'space'), may hold values from -6 to 6
- average_electric_transport: float32 [8, 2048], P('space'), may hold values from 0.5 to 4
- material_zone: int32 [8, 2048], P('space'), may hold values from 0 to 3
- zone_relative_response: float32 [4, 9], replicated, may hold values from 0.02 to 0.12
- polynomial_exponent_rows: int32 [220, 9], replicated, may hold values from 0 to 3, as said below
- quadrature_abscissa_choice: int32 [512, 9], replicated, may hold values from 0 to 4
- quadrature_integer_share: int32 [512], replicated, may hold values from 1 to 1024
Outputs:
- relaxed_voltage: float32 [220, 8, 2048], P('modes', 'space')
- advanced_thermal_state: float32 [220, 8, 2048], P('modes', 'space')
The draws below stay inside these ranges and needn't reach their ends.
Inputs may be any that keep to these rules, and one draw needn't show every extreme that they name: `polynomial_exponent_rows`: the rows are the 220 multi-indices of total degree at most 3 over 9 parameters, each once.
All inputs are finite; a program needn't handle non-finite values.
Results may differ from the reference program's by a relative error of at most 0.0003.
Values sent between devices are 32-bit elements; how exact they have to be, the bound alone decides.
No kernel may reach another device: no remote copies, remote signals or barrier semaphores. Data moves between devices by JAX's collectives and lax.ppermute only.
A program may use at most 64 MiB of HBM per device.

```python
import math
import jax
import jax.numpy as jnp
import numpy as np
from jax import lax

NPAR = 9
EXPANSION_TERMS = 220
NQ = 512
NREG = 4
NY = 256
NZ = 8
VOXELS_SLICE = 2048
VOXELS_LEADING = 8


def draw_polynomial_exponent_rows(key, part):
    listing = [[0] * NPAR]
    for first in range(NPAR):
        entry = [0] * NPAR
        entry[first] += 1
        listing.append(entry)
    for first in range(NPAR):
        for second in range(first, NPAR):
            entry = [0] * NPAR
            entry[first] += 1
            entry[second] += 1
            listing.append(entry)
    for first in range(NPAR):
        for second in range(first, NPAR):
            for third in range(second, NPAR):
                entry = [0] * NPAR
                entry[first] += 1
                entry[second] += 1
                entry[third] += 1
                listing.append(entry)
    table = jnp.asarray(np.array(listing, dtype=np.int32))
    order = jax.random.permutation(jax.random.fold_in(key, 7), table.shape[0])
    return table[order].astype(jnp.int32)


def touch_ends(result, own_key, smallest, high):
    place = [jax.random.randint(jax.random.fold_in(own_key, axis), (), 0, length) for axis, length in enumerate(result.shape)]
    longest = result.shape.index(max(result.shape))
    neighbour = place[:longest] + [(place[longest] + 1) % result.shape[longest]] + place[longest + 1:]
    return result.at[tuple(place)].set(smallest).at[tuple(neighbour)].set(high)


def level_of(rng, shape, cuts, least, largest):
    factor_of, own = 1.0, jax.random.fold_in(rng, 6)
    for dim, shards_of in cuts:
        steps = jnp.exp(jax.random.uniform(jax.random.fold_in(own, dim), (shards_of,), jnp.float32, least / len(cuts), largest / len(cuts)))
        factor_of = factor_of * jnp.repeat(steps, shape[dim] // shards_of).reshape([-1 if axis == dim else 1 for axis in range(len(shape))])
    return factor_of


def normal_values(rng, extent, width, reach, shards=(), held_as=jnp.bfloat16):
    gain = level_of(rng, extent, shards, -0.22, 0.18) if shards else 1.0
    entries = jax.random.normal(rng, extent, jnp.float32) * width * gain
    return jnp.minimum(jnp.maximum(entries, -reach), reach).astype(held_as)


def setup_inputs(seed: int = 0) -> dict:
    splits = jax.random.split(jax.random.key(seed), 10)
    return {
        "voltage_expansion": normal_values(splits[0], (EXPANSION_TERMS, VOXELS_LEADING, VOXELS_SLICE), 1.0, 6.0, ((0, 4), (1, 8)), jnp.float32),
        "current_injection": normal_values(splits[1], (EXPANSION_TERMS, VOXELS_LEADING, VOXELS_SLICE), 8.0, 48.0, ((0, 4), (1, 8)), jnp.float32),
        "thermal_state": normal_values(splits[2], (EXPANSION_TERMS, VOXELS_LEADING, VOXELS_SLICE), 1.0, 6.0, ((0, 4), (1, 8)), jnp.float32),
        "average_electric_transport": jnp.clip(jnp.exp(math.log(4.0) - 2.0794415 * jax.random.uniform(splits[3], (VOXELS_LEADING, VOXELS_SLICE), jnp.float32) ** level_of(splits[3], (VOXELS_LEADING, VOXELS_SLICE), ((0, 8),), -0.2, 0.2)), 0.5, 4.0),
        "material_zone": touch_ends(jax.random.randint(splits[4], (VOXELS_LEADING, VOXELS_SLICE), 0, NREG), jax.random.fold_in(splits[4], 1), 0, NREG - 1).astype(jnp.int32),
        "zone_relative_response": jnp.clip(jax.random.uniform(splits[5], (NREG, NPAR), jnp.float32, 0.02, 0.12), 0.02, 0.12),
        "polynomial_exponent_rows": draw_polynomial_exponent_rows(jax.random.fold_in(splits[9], 71), 0),
        "quadrature_abscissa_choice": touch_ends(jax.random.randint(splits[7], (NQ, NPAR), 0, 5), jax.random.fold_in(splits[7], 1), 0, 4).astype(jnp.int32),
        "quadrature_integer_share": touch_ends(jax.random.randint(splits[8], (NQ,), 1, 1025), jax.random.fold_in(splits[8], 1), 1, 1024).astype(jnp.int32),
    }


HERMITE_NODES = (0.0, 1.355626179974266, -1.355626179974266, 2.8569700138728056, -2.8569700138728056)

def neighbours(field):
    column_ids = jnp.arange(field.shape[-1])
    depth_pos = column_ids % NZ
    row_pos = column_ids // NZ
    z_next = jnp.where(depth_pos < NZ - 1, jnp.roll(field, -1, -1), 0.0)
    z_prev = jnp.where(depth_pos > 0, jnp.roll(field, 1, -1), 0.0)
    y_next = jnp.where(row_pos < NY - 1, jnp.roll(field, -NZ, -1), 0.0)
    y_prev = jnp.where(row_pos > 0, jnp.roll(field, NZ, -1), 0.0)
    return (z_next, z_prev, y_next, y_prev)

def diffusion_operator_weights(padded):
    center = padded[..., 1:-1, :]
    z_next, z_prev, y_next, y_prev = neighbours(center)
    return 6.0 * center - padded[..., 2:, :] - padded[..., :-2, :] - z_next - z_prev - y_next - y_prev

def gradient(padded):
    center = padded[..., 1:-1, :]
    z_next, z_prev, y_next, y_prev = neighbours(center)
    along_x = (padded[..., 2:, :] - padded[..., :-2, :]) * 0.5
    along_y = (y_next - y_prev) * 0.5
    along_z = (z_next - z_prev) * 0.5
    return jnp.stack([along_x, along_y, along_z])

def coupling(row_table, col_table):
    offsets = row_table[:, None, :] - col_table[None, :, :]
    differ_count = lax.optimization_barrier(jnp.sum((offsets != 0).astype(jnp.int32), axis=2))
    layers = [jnp.where(differ_count == 0, 1.0, 0.0).astype(jnp.float32)]
    for which_param in range(row_table.shape[1]):
        larger = jnp.maximum(row_table[:, None, which_param], col_table[None, :, which_param]).astype(jnp.float32)
        linked = (jnp.abs(offsets[:, :, which_param]) == 1) & (differ_count == 1)
        layers.append(jnp.where(linked, jnp.sqrt(larger), 0.0).astype(jnp.float32))
    return jnp.stack(layers)

def node_values(quadrature_abscissa_choice):
    node_vals = jnp.zeros(quadrature_abscissa_choice.shape, jnp.float32)
    for which_node in range(5):
        node_vals = node_vals + jnp.where(quadrature_abscissa_choice == which_node, HERMITE_NODES[which_node], 0.0)
    return node_vals

def basis_values(polynomial_exponent_rows, node_vals):
    poly_terms = [jnp.ones_like(node_vals), node_vals, (node_vals * node_vals - 1.0) / jnp.sqrt(2.0), (node_vals * node_vals * node_vals - 3.0 * node_vals) / jnp.sqrt(6.0)]
    basis_vals = jnp.ones((node_vals.shape[0], polynomial_exponent_rows.shape[0]), jnp.float32)
    for which_param in range(polynomial_exponent_rows.shape[1]):
        degree = polynomial_exponent_rows[:, which_param]
        factor = jnp.zeros_like(basis_vals)
        for which_deg in range(4):
            factor = factor + jnp.where(degree[None, :] == which_deg, poly_terms[which_deg][:, which_param][:, None], 0.0)
        basis_vals = basis_vals * factor
    return basis_vals

def border_slices(field):
    return jnp.pad(field, ((0, 0), (1, 1), (0, 0)))

def reference(voltage_expansion, current_injection, thermal_state, average_electric_transport, material_zone, zone_relative_response, polynomial_exponent_rows, quadrature_abscissa_choice, quadrature_integer_share):
    hp = lax.Precision.HIGHEST
    nreg = zone_relative_response.shape[0]
    sens_cell = jnp.zeros((zone_relative_response.shape[1],) + material_zone.shape, jnp.float32)
    for which_region in range(nreg):
        sens_cell = sens_cell + jnp.where(material_zone[None] == which_region, zone_relative_response[which_region][:, None, None], 0.0)
    coeff = jnp.concatenate([jnp.ones((1,) + material_zone.shape, jnp.float32), sens_cell]) * average_electric_transport
    coup = coupling(polynomial_exponent_rows, polynomial_exponent_rows)
    rough = jnp.moveaxis(diffusion_operator_weights(border_slices(voltage_expansion)), 1, 0)
    coeff_planes = jnp.moveaxis(coeff, 1, 0)

    def couple_plane(pair):
        plane_rough, plane_coeff = pair
        mixed = jnp.einsum('mij,jc->mic', coup, plane_rough, precision=hp)
        return lax.optimization_barrier(jnp.sum(plane_coeff[:, None, :] * mixed, axis=0))
    applied = jnp.moveaxis(lax.map(couple_plane, (rough, coeff_planes)), 0, 1)
    relaxed_voltage = voltage_expansion + 0.8 * (current_injection - applied) / (6.0 * average_electric_transport)
    node_vals = node_values(quadrature_abscissa_choice)
    basis_vals = basis_values(polynomial_exponent_rows, node_vals)
    cond_lift = 1.0 + jnp.dot(zone_relative_response, node_vals.T, precision=hp)
    weighted = basis_vals.T * quadrature_integer_share[None, :].astype(jnp.float32) / (512.0 * NQ * EXPANSION_TERMS)
    padded = border_slices(relaxed_voltage)

    def heat_plane(plane):
        window = lax.dynamic_slice_in_dim(padded, plane, 3, 1)
        grads = gradient(window)[:, :, 0, :]
        point_grads = jnp.einsum('qi,kin->kqn', basis_vals, grads, precision=hp)
        plane_cond = lax.dynamic_index_in_dim(average_electric_transport, plane, 0, keepdims=False)
        plane_region = lax.dynamic_index_in_dim(material_zone, plane, 0, keepdims=False)
        spread = jnp.zeros((cond_lift.shape[1], plane_cond.shape[0]), jnp.float32)
        for which_region in range(nreg):
            spread = spread + jnp.where(plane_region[None, :] == which_region, cond_lift[which_region][:, None], 0.0)
        joule_heat = plane_cond * spread * lax.optimization_barrier(jnp.sum(point_grads * point_grads, axis=0))
        return jnp.dot(weighted, joule_heat, precision=hp)
    thermal_expansion_terms = jnp.moveaxis(lax.map(heat_plane, jnp.arange(VOXELS_LEADING)), 0, 1)
    advanced_thermal_state = thermal_state + 0.1 * (thermal_expansion_terms - 1.5 * diffusion_operator_weights(border_slices(thermal_state)))
    return (relaxed_voltage, advanced_thermal_state)
```

```python
import functools

import jax
import jax.numpy as jnp
from jax import lax
from jax.experimental import pallas as pl
from jax.experimental.pallas import tpu as pltpu
from jax.sharding import PartitionSpec as P

NZ = 8
LANES = 128
SUB = 8
TILE16 = 16
VMEM_LIMIT = 40 * 1024 * 1024

HERMITE_NODES = (
    0.0,
    1.355626179974266,
    -1.355626179974266,
    2.8569700138728056,
    -2.8569700138728056,
)

F32 = jnp.float32
BF16 = jnp.bfloat16


def split2(x):
    high = x.astype(BF16)
    return high, (x - high.astype(F32)).astype(BF16)


def dot(a, b):
    return jnp.dot(a, b, preferred_element_type=F32)


def dot_nt(a, b):
    return lax.dot_general(a, b, (((1,), (1,)), ((), ())), preferred_element_type=F32)


def dot3(a_high, a_low, b_high, b_low):
    return dot(a_high, b_high) + (dot(a_high, b_low) + dot(a_low, b_high))


def lane_ids(shape):
    return lax.broadcasted_iota(jnp.int32, shape, len(shape) - 1)


def load_group(ref, group, modes, groups):
    return ref[pl.ds(group, modes, stride=groups), :]


def pad_rows(x, rows):
    if x.shape[0] == rows:
        return x
    return jnp.concatenate([x, jnp.zeros((rows - x.shape[0], x.shape[1]), x.dtype)], axis=0)


def emit_slots(me, parts, grouped, outs, padded):
    groups = grouped.shape[0] // padded
    per = groups // parts
    lane = lane_ids((padded, LANES))
    for k, out in enumerate(outs):
        q = lax.rem(me + k, parts)
        start = pl.multiple_of(q * (per * padded), SUB)
        out[: per * padded, :] = grouped[pl.ds(start, per * padded), :]
        before = pl.multiple_of(jnp.maximum(q * per - 1, 0) * padded, SUB)
        after = pl.multiple_of(jnp.minimum(q * per + per, groups - 1) * padded, SUB)
        low = pltpu.roll(grouped[pl.ds(before, padded), :], NZ, 1)
        high = pltpu.roll(grouped[pl.ds(after, padded), :], NZ, 1)
        rim = jnp.where((lane < NZ) & (q > 0), low, 0.0)
        rim = jnp.where((lane >= NZ) & (lane < 2 * NZ) & (q < parts - 1), high, rim)
        packed = rim[:SUB]
        for tile in range(1, padded // SUB):
            packed = packed + pltpu.roll(rim[tile * SUB : (tile + 1) * SUB], 2 * NZ * tile, 1)
        out[per * padded :, :] = packed


def source_kernel(parts, modes, padded, v_ref, j_ref, a_ref, *rest):
    outs, grouped = rest[:-1], rest[-1]
    me = lax.axis_index("modes")
    groups = a_ref.shape[0]
    factor = 0.8 / (6.0 * a_ref[...])
    for g in range(groups):
        w = load_group(v_ref, g, modes, groups)
        w = w + load_group(j_ref, g, modes, groups) * factor[g : g + 1]
        grouped[g * padded : (g + 1) * padded, :] = pad_rows(w, padded)
    emit_slots(me, parts, grouped, outs, padded)


def stencil_groups(x_ref, lo_ref, hi_ref, modes, groups, padded, emit):
    lane = lane_ids((padded, LANES))
    depth = lane % NZ
    fields = [pad_rows(load_group(x_ref, g, modes, groups), padded) for g in range(groups)]
    for g in range(groups):
        x = fields[g]
        total = 6.0 * x - pad_rows(load_group(lo_ref, g, modes, groups), padded)
        total = total - pad_rows(load_group(hi_ref, g, modes, groups), padded)
        total = total - jnp.where(depth < NZ - 1, pltpu.roll(x, LANES - 1, 1), 0.0)
        total = total - jnp.where(depth > 0, pltpu.roll(x, 1, 1), 0.0)
        right = fields[g + 1] if g + 1 < groups else jnp.zeros_like(x)
        left = fields[g - 1] if g > 0 else jnp.zeros_like(x)
        total = total - pltpu.roll(jnp.where(lane < NZ, right, x), LANES - NZ, 1)
        total = total - pltpu.roll(jnp.where(lane >= LANES - NZ, left, x), NZ, 1)
        emit(g, x, total)


def rough_kernel(parts, modes, padded, groups, v_ref, lo_ref, hi_ref, *rest):
    outs, grouped = rest[:-1], rest[-1]
    me = lax.axis_index("modes")

    def emit(g, _, total):
        grouped[g * padded : (g + 1) * padded, :] = total

    stencil_groups(v_ref, lo_ref, hi_ref, modes, groups, padded, emit)
    emit_slots(me, parts, grouped, outs, padded)


def thermal_kernel(modes, padded, groups, t_ref, lo_ref, hi_ref, out_ref):
    def emit(g, x, total):
        out_ref[g * padded : (g + 1) * padded, :] = x - 0.15 * total

    stencil_groups(t_ref, lo_ref, hi_ref, modes, groups, padded, emit)


def tables_kernel(
    parts, modes, padded, table_ref, nodes_ref, share_ref, z_ref, zone_ref,
    ah_ref, al_ref, bh_ref, bl_ref, wh_ref, wl_ref, lift_ref, zones_ref,
    cols, basis_t,
):
    nreg, npar = z_ref.shape
    all_modes = parts * modes
    rows = parts * padded
    points = nodes_ref.shape[1]
    me = lax.axis_index("modes")

    slot = lax.broadcasted_iota(jnp.int32, (rows, all_modes), 0)
    mode = lax.broadcasted_iota(jnp.int32, (rows, all_modes), 1)
    within = slot % padded
    pick = (within < modes) & (mode == slot // padded * modes + within)
    pick = jnp.where(pick, 1.0, 0.0).astype(BF16)
    table = table_ref[...].astype(F32).astype(BF16)
    along = dot_nt(table, pick)
    lane_pad = lane_ids(along.shape) % padded >= modes
    along = jnp.where(lane_pad, -50.0, along)
    down = dot_nt(pick, table)
    row_pad = lax.broadcasted_iota(jnp.int32, down.shape, 0) % padded >= modes
    cols[...] = jnp.where(row_pad, -50.0, down)

    nodes = nodes_ref[...]
    t = jnp.zeros(nodes.shape, F32)
    for which in range(1, len(HERMITE_NODES)):
        t = jnp.where(nodes == which, HERMITE_NODES[which], t)
    h2 = (t * t - 1.0) * (1.0 / 2.0**0.5)
    h3 = (t * t * t - 3.0 * t) * (1.0 / 6.0**0.5)
    share = share_ref[...].astype(F32) * (0.25 / (512.0 * points * all_modes))

    def block(b, carry):
        at = pl.multiple_of(b * TILE16, TILE16)
        mine = cols[pl.ds(at, TILE16), :]
        count = jnp.zeros((TILE16, rows), F32)
        larger = jnp.zeros((TILE16, rows), F32)
        weight = [jnp.zeros((TILE16, rows), F32) for _ in range(nreg)]
        basis = jnp.ones((TILE16, points), F32)
        for m in range(npar):
            own = mine[:, m : m + 1]
            other = along[m : m + 1, :]
            gap = jnp.abs(own - other)
            count = count + jnp.where(gap != 0.0, 1.0, 0.0)
            one = gap == 1.0
            larger = jnp.where(one, jnp.maximum(own, other), larger)
            weight = [jnp.where(one, z_ref[r, m], weight[r]) for r in range(nreg)]
            factor = jnp.where(own == 0.0, 1.0, 0.0) + jnp.where(own == 1.0, t[m : m + 1], 0.0)
            factor = factor + jnp.where(own == 2.0, h2[m : m + 1], 0.0)
            factor = factor + jnp.where(own == 3.0, h3[m : m + 1], 0.0)
            basis = basis * factor
        root = jnp.where(count == 1.0, jnp.sqrt(larger), 0.0)
        for r in range(nreg):
            high, low = split2(jnp.where(count == 0.0, 1.0, root * weight[r]))
            spot = pl.multiple_of(r * rows + at, TILE16)
            ah_ref[pl.ds(spot, TILE16), :] = high
            al_ref[pl.ds(spot, TILE16), :] = low
        basis_t[pl.ds(at, TILE16), :] = basis
        high, low = split2(basis * share)
        wh_ref[pl.ds(at, TILE16), :] = high
        wl_ref[pl.ds(at, TILE16), :] = low
        return carry

    lax.fori_loop(0, rows // TILE16, block, 0)
    high, low = split2(basis_t[...].T)
    bh_ref[...] = high
    bl_ref[...] = low

    terms = []
    for r in range(nreg):
        lift = jnp.ones((1, points), F32)
        for m in range(npar):
            lift = lift + z_ref[r, m] * t[m : m + 1]
        terms.append(lift)
    lift = jnp.concatenate(terms, axis=0)
    high = lift.astype(BF16).astype(F32)
    mid = (lift - high).astype(BF16).astype(F32)
    low = lift - high - mid
    stacked = jnp.concatenate(
        [high, mid, low, jnp.zeros((LANES - 3 * nreg, points), F32)], axis=0
    )
    lift_ref[...] = stacked.T.astype(BF16)

    groups = zone_ref.shape[0]
    per = groups // parts
    zone = zone_ref[...]
    row = lax.broadcasted_iota(jnp.int32, zone.shape, 0)

    def pick_row(g):
        return jnp.sum(jnp.where(row == g, zone, 0), axis=0, keepdims=True)

    for s in range(per):
        zones_ref[:, s * LANES : (s + 1) * LANES] = pick_row(me * per + s)
    low = pltpu.roll(pick_row(jnp.maximum(me * per - 1, 0)), NZ, 1)
    high = pltpu.roll(pick_row(jnp.minimum(me * per + per, groups - 1)), NZ, 1)
    zones_ref[:, per * LANES :] = jnp.where(lane_ids(low.shape) < NZ, low, high)


def couple_kernel(
    parts, padded, per, nreg, *refs
):
    w_refs = refs[:parts]
    r_refs = refs[parts : 2 * parts]
    ah_ref, al_ref, zones_ref = refs[2 * parts : 2 * parts + 3]
    rel_ref, rim_ref = refs[2 * parts + 3 : 2 * parts + 5]
    outs = refs[2 * parts + 5 : -2]
    w_all, r_all = refs[-2:]
    me = lax.axis_index("modes")
    rows = parts * padded
    width = per * LANES
    for k in range(parts):
        source = lax.rem(me + (parts - k), parts)
        at = pl.multiple_of(source * padded, SUB)
        for chunk, dest in ((w_refs[k], w_all), (r_refs[k], r_all)):
            for s in range(per):
                dest[pl.ds(at, padded), s * LANES : (s + 1) * LANES] = chunk[
                    s * padded : (s + 1) * padded, :
                ]
            packed = chunk[per * padded :, :]
            for tile in range(padded // SUB):
                spot = pl.multiple_of(at + tile * SUB, SUB)
                shift = (LANES - 2 * NZ * tile) % LANES
                part = pltpu.roll(packed, shift, 1) if shift else packed
                dest[pl.ds(spot, SUB), width:] = part
    r_high, r_low = split2(r_all[...])
    zones = zones_ref[...]
    applied = jnp.zeros(r_all.shape, F32)
    for r in range(nreg):
        a_high = ah_ref[r * rows : (r + 1) * rows, :]
        a_low = al_ref[r * rows : (r + 1) * rows, :]
        applied = jnp.where(zones == r, dot3(a_high, a_low, r_high, r_low), applied)
    w_all[...] = w_all[...] - (0.8 / 6.0) * applied
    rel_ref[...] = w_all[:, :width]
    rim_ref[...] = w_all[:, width:]
    for k, out in enumerate(outs):
        target = lax.rem(me + k, parts)
        at = pl.multiple_of(target * padded, SUB)
        for s in range(per):
            out[s * padded : (s + 1) * padded, :] = w_all[
                pl.ds(at, padded), s * LANES : (s + 1) * LANES
            ]


def joule_kernel(
    parts, padded, per, nreg, rel_ref, rim_ref, lo_ref, hi_ref, a_ref, zones_ref,
    bh_ref, bl_ref, wh_ref, wl_ref, lift_ref, *rest,
):
    outs, heat_ref = rest[:-1], rest[-1]
    me = lax.axis_index("modes")
    width = per * LANES
    rel = rel_ref[...]
    rim = rim_ref[...]
    lane = lane_ids(rel.shape)
    depth = lane % NZ
    wide = jnp.concatenate([rim] + [jnp.zeros_like(rim)] * (per - 1), axis=1)
    along_z = jnp.where(depth < NZ - 1, pltpu.roll(rel, width - 1, 1), 0.0)
    along_z = along_z - jnp.where(depth > 0, pltpu.roll(rel, 1, 1), 0.0)
    after = pltpu.roll(wide, width - 2 * NZ, 1)
    along_y = jnp.where(lane >= width - NZ, after, pltpu.roll(rel, width - NZ, 1))
    along_y = along_y - jnp.where(lane < NZ, wide, pltpu.roll(rel, NZ, 1))
    along_x = hi_ref[...] - lo_ref[...]
    b_high, b_low = bh_ref[...], bl_ref[...]
    total = None
    for grad in (along_y, along_z, along_x):
        g_high, g_low = split2(grad)
        at_point = dot3(b_high, b_low, g_high, g_low)
        total = at_point * at_point if total is None else total + at_point * at_point
    zones = zones_ref[:, :width]
    row = lax.broadcasted_iota(jnp.int32, (LANES, width), 0)
    hot = (row < 3 * nreg) & (row % nreg == zones)
    spread = dot(lift_ref[...], jnp.where(hot, 1.0, 0.0).astype(BF16))
    j_high, j_low = split2(spread * total)
    heat = dot3(wh_ref[...], wl_ref[...], j_high, j_low)
    for s in range(per):
        heat_ref[:, s * LANES : (s + 1) * LANES] = (
            heat[:, s * LANES : (s + 1) * LANES] * a_ref[pl.ds(me * per + s, 1), :]
        )
    for k, out in enumerate(outs):
        target = lax.rem(me + k, parts)
        at = pl.multiple_of(target * padded, SUB)
        for s in range(per):
            out[s * padded : (s + 1) * padded, :] = heat_ref[
                pl.ds(at, padded), s * LANES : (s + 1) * LANES
            ]


def gather_kernel(parts, modes, padded, per, *refs):
    chunks, out = refs[:parts], refs[parts]
    me = lax.axis_index("modes")
    for k in range(parts):
        q = lax.rem(me + (parts - k), parts)
        for s in range(per):
            rows = chunks[k][s * padded : s * padded + modes, :]
            out[pl.ds(q * per + s, modes, stride=parts * per), :] = rows


def final_kernel(parts, modes, padded, per, *refs):
    chunks, base, out = refs[:parts], refs[parts], refs[parts + 1]
    me = lax.axis_index("modes")
    for k in range(parts):
        q = lax.rem(me + (parts - k), parts)
        for s in range(per):
            at = pl.multiple_of((q * per + s) * padded, SUB)
            rows = base[pl.ds(at, padded), :] + 0.1 * chunks[k][s * padded : (s + 1) * padded, :]
            out[pl.ds(q * per + s, modes, stride=parts * per), :] = rows[:modes]


def call(kernel, out_shape, args, scratch=(), smem=(), flops=0):
    specs = [
        pl.BlockSpec(memory_space=pltpu.SMEM if i in smem else pltpu.VMEM)
        for i in range(len(args))
    ]
    many = isinstance(out_shape, (list, tuple))
    vmem = pl.BlockSpec(memory_space=pltpu.VMEM)
    nbytes = sum(x.size * x.dtype.itemsize for x in args)
    return pl.pallas_call(
        kernel,
        out_shape=out_shape,
        in_specs=specs,
        out_specs=[vmem] * len(out_shape) if many else vmem,
        scratch_shapes=list(scratch),
        compiler_params=pltpu.CompilerParams(vmem_limit_bytes=VMEM_LIMIT),
        cost_estimate=pl.CostEstimate(flops=flops, bytes_accessed=nbytes, transcendentals=0),
    )(*args)


def exchange(chunks):
    parts = lax.axis_size("modes")
    received = [chunks[0]]
    for k in range(1, parts):
        pairs = [(i, (i + k) % parts) for i in range(parts)]
        received.append(lax.ppermute(chunks[k], "modes", pairs))
    return received


def halo(x):
    count = lax.axis_size("space")
    forward = [(i, i + 1) for i in range(count - 1)]
    backward = [(i + 1, i) for i in range(count - 1)]
    return lax.ppermute(x, "space", forward), lax.ppermute(x, "space", backward)


def on_device(
    voltage_expansion,
    current_injection,
    thermal_state,
    average_electric_transport,
    material_zone,
    zone_relative_response,
    polynomial_exponent_rows,
    quadrature_abscissa_choice,
    quadrature_integer_share,
):
    parts = lax.axis_size("modes")
    modes, planes, columns = voltage_expansion.shape
    nreg = zone_relative_response.shape[0]
    points = quadrature_integer_share.shape[0]
    groups = columns // LANES
    per = groups // parts
    padded = -(-modes // SUB) * SUB
    rows = parts * padded
    assert planes == 1 and groups * LANES == columns and per * parts == groups
    assert rows % TILE16 == 0 and 2 * NZ * padded <= SUB * LANES and 3 * nreg <= LANES

    def flat(x):
        return x.reshape(modes * groups, LANES)

    def struct(*shape, dtype=F32):
        return jax.ShapeDtypeStruct(shape, dtype)

    v, cur, temp = flat(voltage_expansion), flat(current_injection), flat(thermal_state)
    avg = average_electric_transport.reshape(groups, LANES)
    zone = material_zone.reshape(groups, LANES)
    chunk = struct(per * padded, LANES)
    rimmed = struct(per * padded + SUB, LANES)
    grouped = pltpu.VMEM((groups * padded, LANES), F32)

    v_low, v_high = halo(v)
    source = call(
        functools.partial(source_kernel, parts, modes, padded),
        [rimmed] * parts, [v, cur, avg], [grouped],
    )
    source = exchange(source)
    rough = call(
        functools.partial(rough_kernel, parts, modes, padded, groups),
        [rimmed] * parts, [v, v_low, v_high], [grouped],
    )
    rough = exchange(rough)
    a_high, a_low, b_high, b_low, w_high, w_low, lift, zones = call(
        functools.partial(tables_kernel, parts, modes, padded),
        [
            struct(nreg * rows, rows, dtype=BF16),
            struct(nreg * rows, rows, dtype=BF16),
            struct(points, rows, dtype=BF16),
            struct(points, rows, dtype=BF16),
            struct(rows, points, dtype=BF16),
            struct(rows, points, dtype=BF16),
            struct(points, LANES, dtype=BF16),
            struct(1, (per + 1) * LANES, dtype=jnp.int32),
        ],
        [
            polynomial_exponent_rows.T,
            quadrature_abscissa_choice.T,
            quadrature_integer_share.reshape(1, points),
            zone_relative_response,
            zone,
        ],
        [pltpu.VMEM((rows, polynomial_exponent_rows.shape[1]), F32), pltpu.VMEM((rows, points), F32)],
        smem=(3,),
    )
    t_low, t_high = halo(temp)
    base = call(
        functools.partial(thermal_kernel, modes, padded, groups),
        struct(groups * padded, LANES), [temp, t_low, t_high],
    )
    wide = (per + 1) * LANES
    relaxed, rim, *back = call(
        functools.partial(couple_kernel, parts, padded, per, nreg),
        [struct(rows, per * LANES), struct(rows, LANES)] + [chunk] * parts,
        [*source, *rough, a_high, a_low, zones],
        [pltpu.VMEM((rows, wide), F32), pltpu.VMEM((rows, wide), F32)],
    )
    x_low, x_high = halo(relaxed)
    back = exchange(back)
    heat = call(
        functools.partial(joule_kernel, parts, padded, per, nreg),
        [chunk] * parts,
        [relaxed, rim, x_low, x_high, avg, zones, b_high, b_low, w_high, w_low, lift],
        [pltpu.VMEM((rows, per * LANES), F32)],
    )
    heat = exchange(heat)
    relaxed_voltage = call(
        functools.partial(gather_kernel, parts, modes, padded, per),
        struct(modes * groups, LANES), back,
    )
    advanced = call(
        functools.partial(final_kernel, parts, modes, padded, per),
        struct(modes * groups, LANES), [*heat, base],
    )
    shape = voltage_expansion.shape
    return relaxed_voltage.reshape(shape), advanced.reshape(shape)


def solution(mesh):
    in_specs = (
        P("modes", "space", None),
        P("modes", "space", None),
        P("modes", "space", None),
        P("space", None),
        P("space", None),
        P(),
        P(),
        P(),
        P(),
    )
    out_specs = (P("modes", "space", None), P("modes", "space", None))
    return jax.shard_map(
        on_device, mesh=mesh, in_specs=in_specs, out_specs=out_specs, check_vma=False
    )
```

```python
import functools

import jax
import jax.numpy as jnp
from jax import lax
from jax.experimental import pallas as pl
from jax.experimental.pallas import tpu as pltpu
from jax.sharding import PartitionSpec as P

NZ = 8
LANES = 128
SUB = 8
TILE16 = 16
VMEM_LIMIT = 40 * 1024 * 1024

HERMITE_NODES = (
    0.0,
    1.355626179974266,
    -1.355626179974266,
    2.8569700138728056,
    -2.8569700138728056,
)

F32 = jnp.float32
BF16 = jnp.bfloat16


def split2(x):
    high = x.astype(BF16)
    return high, (x - high.astype(F32)).astype(BF16)


def dot(a, b):
    return jnp.dot(a, b, preferred_element_type=F32)


def dot_nt(a, b):
    return lax.dot_general(a, b, (((1,), (1,)), ((), ())), preferred_element_type=F32)


def dot3(a_high, a_low, b_high, b_low):
    return dot(a_high, b_high) + (dot(a_high, b_low) + dot(a_low, b_high))


def lane_ids(shape):
    return lax.broadcasted_iota(jnp.int32, shape, len(shape) - 1)


def load_group(ref, group, modes, groups):
    return ref[pl.ds(group, modes, stride=groups), :]


def pad_rows(x, rows):
    if x.shape[0] == rows:
        return x
    return jnp.concatenate([x, jnp.zeros((rows - x.shape[0], x.shape[1]), x.dtype)], axis=0)


def emit_slots(me, parts, grouped, outs, padded):
    groups = grouped.shape[0] // padded
    per = groups // parts
    lane = lane_ids((padded, LANES))
    for k, out in enumerate(outs):
        q = lax.rem(me + k, parts)
        start = pl.multiple_of(q * (per * padded), SUB)
        out[: per * padded, :] = grouped[pl.ds(start, per * padded), :]
        before = pl.multiple_of(jnp.maximum(q * per - 1, 0) * padded, SUB)
        after = pl.multiple_of(jnp.minimum(q * per + per, groups - 1) * padded, SUB)
        low = pltpu.roll(grouped[pl.ds(before, padded), :], NZ, 1)
        high = pltpu.roll(grouped[pl.ds(after, padded), :], NZ, 1)
        rim = jnp.where((lane < NZ) & (q > 0), low, 0.0)
        rim = jnp.where((lane >= NZ) & (lane < 2 * NZ) & (q < parts - 1), high, rim)
        packed = rim[:SUB]
        for tile in range(1, padded // SUB):
            packed = packed + pltpu.roll(rim[tile * SUB : (tile + 1) * SUB], 2 * NZ * tile, 1)
        out[per * padded :, :] = packed


def source_kernel(parts, modes, padded, v_hbm, j_hbm, a_hbm, *rest):
    outs, (grouped, v_ref, j_ref, a_ref, sems) = rest[:-5], rest[-5:]
    pairs = ((v_hbm, v_ref), (j_hbm, j_ref), (a_hbm, a_ref))
    copies = [pltpu.make_async_copy(x, y, sems.at[i]) for i, (x, y) in enumerate(pairs)]
    for copy in copies:
        copy.start()
    for copy in copies:
        copy.wait()
    me = lax.axis_index("modes")
    groups = a_ref.shape[0]
    factor = 0.8 / (6.0 * a_ref[...])
    for g in range(groups):
        w = load_group(v_ref, g, modes, groups)
        w = w + load_group(j_ref, g, modes, groups) * factor[g : g + 1]
        grouped[g * padded : (g + 1) * padded, :] = pad_rows(w, padded)
    emit_slots(me, parts, grouped, outs, padded)


def stencil_groups(x_ref, near_ref, far_ref, modes, groups, padded, emit):
    lane = lane_ids((padded, LANES))
    depth = lane % NZ
    fields = [pad_rows(load_group(x_ref, g, modes, groups), padded) for g in range(groups)]
    for g in range(groups):
        x = fields[g]
        total = 6.0 * x - pad_rows(load_group(near_ref, g, modes, groups), padded)
        total = total - pad_rows(load_group(far_ref, g, modes, groups), padded)
        total = total - jnp.where(depth < NZ - 1, pltpu.roll(x, LANES - 1, 1), 0.0)
        total = total - jnp.where(depth > 0, pltpu.roll(x, 1, 1), 0.0)
        right = fields[g + 1] if g + 1 < groups else jnp.zeros_like(x)
        left = fields[g - 1] if g > 0 else jnp.zeros_like(x)
        total = total - pltpu.roll(jnp.where(lane < NZ, right, x), LANES - NZ, 1)
        total = total - pltpu.roll(jnp.where(lane >= LANES - NZ, left, x), NZ, 1)
        emit(g, x, total)


def rough_kernel(parts, modes, padded, groups, v_ref, near_ref, far_ref, *rest):
    outs, grouped = rest[:-1], rest[-1]
    me = lax.axis_index("modes")

    def emit(g, _, total):
        grouped[g * padded : (g + 1) * padded, :] = total

    stencil_groups(v_ref, near_ref, far_ref, modes, groups, padded, emit)
    emit_slots(me, parts, grouped, outs, padded)


def thermal_kernel(modes, padded, groups, t_ref, near_ref, far_ref, out_ref):
    def emit(g, x, total):
        out_ref[g * padded : (g + 1) * padded, :] = x - 0.15 * total

    stencil_groups(t_ref, near_ref, far_ref, modes, groups, padded, emit)


def tables_kernel(
    parts, modes, padded, table_ref, nodes_ref, share_ref, z_ref, zone_ref,
    ah_ref, al_ref, bh_ref, bl_ref, wh_ref, wl_ref, lift_ref, zones_ref,
    cols, basis_t,
):
    nreg, npar = z_ref.shape
    all_modes = parts * modes
    rows = parts * padded
    points = nodes_ref.shape[1]
    me = lax.axis_index("modes")

    slot = lax.broadcasted_iota(jnp.int32, (rows, all_modes), 0)
    mode = lax.broadcasted_iota(jnp.int32, (rows, all_modes), 1)
    within = slot % padded
    pick = (within < modes) & (mode == slot // padded * modes + within)
    pick = jnp.where(pick, 1.0, 0.0).astype(BF16)
    table = table_ref[...].astype(F32).astype(BF16)
    along = dot_nt(table, pick)
    lane_pad = lane_ids(along.shape) % padded >= modes
    along = jnp.where(lane_pad, -50.0, along)
    down = dot_nt(pick, table)
    row_pad = lax.broadcasted_iota(jnp.int32, down.shape, 0) % padded >= modes
    cols[...] = jnp.where(row_pad, -50.0, down)

    nodes = nodes_ref[...]
    t = jnp.zeros(nodes.shape, F32)
    for which in range(1, len(HERMITE_NODES)):
        t = jnp.where(nodes == which, HERMITE_NODES[which], t)
    h2 = (t * t - 1.0) * (1.0 / 2.0**0.5)
    h3 = (t * t * t - 3.0 * t) * (1.0 / 6.0**0.5)
    share = share_ref[...].astype(F32) * (0.25 / (512.0 * points * all_modes))

    def block(b, carry):
        at = pl.multiple_of(b * TILE16, TILE16)
        mine = cols[pl.ds(at, TILE16), :]
        count = jnp.zeros((TILE16, rows), F32)
        larger = jnp.zeros((TILE16, rows), F32)
        weight = [jnp.zeros((TILE16, rows), F32) for _ in range(nreg)]
        basis = jnp.ones((TILE16, points), F32)
        for m in range(npar):
            own = mine[:, m : m + 1]
            other = along[m : m + 1, :]
            gap = jnp.abs(own - other)
            count = count + jnp.where(gap != 0.0, 1.0, 0.0)
            one = gap == 1.0
            larger = jnp.where(one, jnp.maximum(own, other), larger)
            weight = [jnp.where(one, z_ref[r, m], weight[r]) for r in range(nreg)]
            factor = jnp.where(own == 0.0, 1.0, 0.0) + jnp.where(own == 1.0, t[m : m + 1], 0.0)
            factor = factor + jnp.where(own == 2.0, h2[m : m + 1], 0.0)
            factor = factor + jnp.where(own == 3.0, h3[m : m + 1], 0.0)
            basis = basis * factor
        root = jnp.where(count == 1.0, jnp.sqrt(larger), 0.0)
        for r in range(nreg):
            high, low = split2(jnp.where(count == 0.0, 1.0, root * weight[r]))
            spot = pl.multiple_of(r * rows + at, TILE16)
            ah_ref[pl.ds(spot, TILE16), :] = high
            al_ref[pl.ds(spot, TILE16), :] = low
        basis_t[pl.ds(at, TILE16), :] = basis
        high, low = split2(basis * share)
        wh_ref[pl.ds(at, TILE16), :] = high
        wl_ref[pl.ds(at, TILE16), :] = low
        return carry

    lax.fori_loop(0, rows // TILE16, block, 0)
    high, low = split2(basis_t[...].T)
    bh_ref[...] = high
    bl_ref[...] = low

    terms = []
    for r in range(nreg):
        lift = jnp.ones((1, points), F32)
        for m in range(npar):
            lift = lift + z_ref[r, m] * t[m : m + 1]
        terms.append(lift)
    lift = jnp.concatenate(terms, axis=0)
    high = lift.astype(BF16).astype(F32)
    mid = (lift - high).astype(BF16).astype(F32)
    low = lift - high - mid
    stacked = jnp.concatenate(
        [high, mid, low, jnp.zeros((LANES - 3 * nreg, points), F32)], axis=0
    )
    lift_ref[...] = stacked.T.astype(BF16)

    groups = zone_ref.shape[0]
    per = groups // parts
    zone = zone_ref[...]
    row = lax.broadcasted_iota(jnp.int32, zone.shape, 0)

    def pick_row(g):
        return jnp.sum(jnp.where(row == g, zone, 0), axis=0, keepdims=True)

    for s in range(per):
        zones_ref[:, s * LANES : (s + 1) * LANES] = pick_row(me * per + s)
    low = pltpu.roll(pick_row(jnp.maximum(me * per - 1, 0)), NZ, 1)
    high = pltpu.roll(pick_row(jnp.minimum(me * per + per, groups - 1)), NZ, 1)
    zones_ref[:, per * LANES :] = jnp.where(lane_ids(low.shape) < NZ, low, high)


def couple_kernel(
    parts, padded, per, nreg, *refs
):
    w_refs = refs[:parts]
    r_refs = refs[parts : 2 * parts]
    ah_ref, al_ref, zones_ref = refs[2 * parts : 2 * parts + 3]
    rel_ref, rim_ref = refs[2 * parts + 3 : 2 * parts + 5]
    outs = refs[2 * parts + 5 : -2]
    w_all, r_all = refs[-2:]
    me = lax.axis_index("modes")
    rows = parts * padded
    width = per * LANES
    for k in range(parts):
        source = lax.rem(me + (parts - k), parts)
        at = pl.multiple_of(source * padded, SUB)
        for chunk, dest in ((w_refs[k], w_all), (r_refs[k], r_all)):
            for s in range(per):
                dest[pl.ds(at, padded), s * LANES : (s + 1) * LANES] = chunk[
                    s * padded : (s + 1) * padded, :
                ]
            packed = chunk[per * padded :, :]
            for tile in range(padded // SUB):
                spot = pl.multiple_of(at + tile * SUB, SUB)
                shift = (LANES - 2 * NZ * tile) % LANES
                part = pltpu.roll(packed, shift, 1) if shift else packed
                dest[pl.ds(spot, SUB), width:] = part
    r_high, r_low = split2(r_all[...])
    zones = zones_ref[...]
    applied = jnp.zeros(r_all.shape, F32)
    for r in range(nreg):
        a_high = ah_ref[r * rows : (r + 1) * rows, :]
        a_low = al_ref[r * rows : (r + 1) * rows, :]
        applied = jnp.where(zones == r, dot3(a_high, a_low, r_high, r_low), applied)
    w_all[...] = w_all[...] - (0.8 / 6.0) * applied
    rel_ref[...] = w_all[:, :width]
    rim_ref[...] = w_all[:, width:]
    for k, out in enumerate(outs):
        target = lax.rem(me + k, parts)
        at = pl.multiple_of(target * padded, SUB)
        for s in range(per):
            out[s * padded : (s + 1) * padded, :] = w_all[
                pl.ds(at, padded), s * LANES : (s + 1) * LANES
            ]


def joule_kernel(
    parts, padded, per, nreg, rel_ref, rim_ref, near_ref, far_ref, a_ref, zones_ref,
    bh_ref, bl_ref, wh_ref, wl_ref, lift_ref, *rest,
):
    outs, heat_ref = rest[:-1], rest[-1]
    me = lax.axis_index("modes")
    width = per * LANES
    rel = rel_ref[...]
    rim = rim_ref[...]
    lane = lane_ids(rel.shape)
    depth = lane % NZ
    wide = jnp.concatenate([rim] + [jnp.zeros_like(rim)] * (per - 1), axis=1)
    along_z = jnp.where(depth < NZ - 1, pltpu.roll(rel, width - 1, 1), 0.0)
    along_z = along_z - jnp.where(depth > 0, pltpu.roll(rel, 1, 1), 0.0)
    after = pltpu.roll(wide, width - 2 * NZ, 1)
    along_y = jnp.where(lane >= width - NZ, after, pltpu.roll(rel, width - NZ, 1))
    along_y = along_y - jnp.where(lane < NZ, wide, pltpu.roll(rel, NZ, 1))
    along_x = far_ref[...] - near_ref[...]
    b_high, b_low = bh_ref[...], bl_ref[...]
    total = None
    for grad in (along_y, along_z, along_x):
        g_high, g_low = split2(grad)
        at_point = dot3(b_high, b_low, g_high, g_low)
        total = at_point * at_point if total is None else total + at_point * at_point
    zones = zones_ref[:, :width]
    row = lax.broadcasted_iota(jnp.int32, (LANES, width), 0)
    hot = (row < 3 * nreg) & (row % nreg == zones)
    spread = dot(lift_ref[...], jnp.where(hot, 1.0, 0.0).astype(BF16))
    j_high, j_low = split2(spread * total)
    heat = dot3(wh_ref[...], wl_ref[...], j_high, j_low)
    for s in range(per):
        heat_ref[:, s * LANES : (s + 1) * LANES] = (
            heat[:, s * LANES : (s + 1) * LANES] * a_ref[pl.ds(me * per + s, 1), :]
        )
    for k, out in enumerate(outs):
        target = lax.rem(me + k, parts)
        at = pl.multiple_of(target * padded, SUB)
        for s in range(per):
            out[s * padded : (s + 1) * padded, :] = heat_ref[
                pl.ds(at, padded), s * LANES : (s + 1) * LANES
            ]


def gather_kernel(parts, modes, padded, per, *refs):
    chunks, out = refs[:parts], refs[parts]
    me = lax.axis_index("modes")
    for k in range(parts):
        q = lax.rem(me + (parts - k), parts)
        for s in range(per):
            rows = chunks[k][s * padded : s * padded + modes, :]
            out[pl.ds(q * per + s, modes, stride=parts * per), :] = rows


def final_kernel(parts, modes, padded, per, *refs):
    chunks, base, out = refs[:parts], refs[parts], refs[parts + 1]
    me = lax.axis_index("modes")
    for k in range(parts):
        q = lax.rem(me + (parts - k), parts)
        for s in range(per):
            at = pl.multiple_of((q * per + s) * padded, SUB)
            rows = base[pl.ds(at, padded), :] + 0.1 * chunks[k][s * padded : (s + 1) * padded, :]
            out[pl.ds(q * per + s, modes, stride=parts * per), :] = rows[:modes]


def call(kernel, out_shape, args, scratch=(), smem=(), hbm=(), limit=VMEM_LIMIT):
    specs = [
        pl.BlockSpec(
            memory_space=pltpu.SMEM if i in smem else pltpu.HBM if i in hbm else pltpu.VMEM
        )
        for i in range(len(args))
    ]
    many = isinstance(out_shape, (list, tuple))
    vmem = pl.BlockSpec(memory_space=pltpu.VMEM)
    nbytes = sum(x.size * x.dtype.itemsize for x in args)
    return pl.pallas_call(
        kernel,
        out_shape=out_shape,
        in_specs=specs,
        out_specs=[vmem] * len(out_shape) if many else vmem,
        scratch_shapes=list(scratch),
        compiler_params=pltpu.CompilerParams(vmem_limit_bytes=limit),
        cost_estimate=pl.CostEstimate(flops=0, bytes_accessed=nbytes, transcendentals=0),
    )(*args)


def exchange(chunks):
    parts = lax.axis_size("modes")
    received = [chunks[0]]
    for k in range(1, parts):
        pairs = [(i, (i + k) % parts) for i in range(parts)]
        received.append(lax.ppermute(chunks[k], "modes", pairs))
    return received


def halo(x):
    count = lax.axis_size("space")
    near = [(i, i ^ 1) for i in range(count) if i ^ 1 < count]
    far = [(i, ((i - 1) ^ 1) + 1) for i in range(1, count) if ((i - 1) ^ 1) + 1 < count]
    far = lax.ppermute(x, "space", far)
    return lax.ppermute(x, "space", near), far


def on_device(
    voltage_expansion,
    current_injection,
    thermal_state,
    average_electric_transport,
    material_zone,
    zone_relative_response,
    polynomial_exponent_rows,
    quadrature_abscissa_choice,
    quadrature_integer_share,
):
    parts = lax.axis_size("modes")
    modes, planes, columns = voltage_expansion.shape
    nreg = zone_relative_response.shape[0]
    points = quadrature_integer_share.shape[0]
    groups = columns // LANES
    per = groups // parts
    padded = -(-modes // SUB) * SUB
    rows = parts * padded
    assert planes == 1 and groups * LANES == columns and per * parts == groups
    assert rows % TILE16 == 0 and 2 * NZ * padded <= SUB * LANES and 3 * nreg <= LANES

    def flat(x):
        return x.reshape(modes * groups, LANES)

    def struct(*shape, dtype=F32):
        return jax.ShapeDtypeStruct(shape, dtype)

    v, cur, temp = flat(voltage_expansion), flat(current_injection), flat(thermal_state)
    avg = average_electric_transport.reshape(groups, LANES)
    zone = material_zone.reshape(groups, LANES)
    chunk = struct(per * padded, LANES)
    rimmed = struct(per * padded + SUB, LANES)
    grouped = pltpu.VMEM((groups * padded, LANES), F32)

    fields = pltpu.VMEM((modes * groups, LANES), F32)
    v_near, v_far = halo(v)
    source = call(
        functools.partial(source_kernel, parts, modes, padded),
        [rimmed] * parts,
        [v, cur, avg],
        [grouped, fields, fields, pltpu.VMEM((groups, LANES), F32), pltpu.SemaphoreType.DMA((3,))],
        hbm=(0, 1, 2),
        limit=62 * 1024 * 1024,
    )
    source = exchange(source)
    a_high, a_low, b_high, b_low, w_high, w_low, lift, zones = call(
        functools.partial(tables_kernel, parts, modes, padded),
        [
            struct(nreg * rows, rows, dtype=BF16),
            struct(nreg * rows, rows, dtype=BF16),
            struct(points, rows, dtype=BF16),
            struct(points, rows, dtype=BF16),
            struct(rows, points, dtype=BF16),
            struct(rows, points, dtype=BF16),
            struct(points, LANES, dtype=BF16),
            struct(1, (per + 1) * LANES, dtype=jnp.int32),
        ],
        [
            polynomial_exponent_rows.T,
            quadrature_abscissa_choice.T,
            quadrature_integer_share.reshape(1, points),
            zone_relative_response,
            zone,
        ],
        [pltpu.VMEM((rows, polynomial_exponent_rows.shape[1]), F32), pltpu.VMEM((rows, points), F32)],
        smem=(3,),
    )
    v, zones = lax.optimization_barrier((v, zones))
    rough = call(
        functools.partial(rough_kernel, parts, modes, padded, groups),
        [rimmed] * parts, [v, v_near, v_far], [grouped],
    )
    temp_after, *rough = lax.optimization_barrier((temp, *rough))
    rough = exchange(rough)
    t_near, t_far = halo(temp_after)
    base = call(
        functools.partial(thermal_kernel, modes, padded, groups),
        struct(groups * padded, LANES), [temp, t_near, t_far],
    )
    wide = (per + 1) * LANES
    relaxed, rim, *back = call(
        functools.partial(couple_kernel, parts, padded, per, nreg),
        [struct(rows, per * LANES), struct(rows, LANES)] + [chunk] * parts,
        [*source, *rough, a_high, a_low, zones],
        [pltpu.VMEM((rows, wide), F32), pltpu.VMEM((rows, wide), F32)],
    )
    x_near, x_far = halo(relaxed)
    base, *back = lax.optimization_barrier((base, *back))
    back = exchange(back)
    heat = call(
        functools.partial(joule_kernel, parts, padded, per, nreg),
        [chunk] * parts,
        [relaxed, rim, x_near, x_far, avg, zones, b_high, b_low, w_high, w_low, lift],
        [pltpu.VMEM((rows, per * LANES), F32)],
    )
    heat = exchange(heat)
    relaxed_voltage = call(
        functools.partial(gather_kernel, parts, modes, padded, per),
        struct(modes * groups, LANES), back,
    )
    advanced = call(
        functools.partial(final_kernel, parts, modes, padded, per),
        struct(modes * groups, LANES), [*heat, base],
    )
    shape = voltage_expansion.shape
    return relaxed_voltage.reshape(shape), advanced.reshape(shape)


def solution(mesh):
    in_specs = (
        P("modes", "space", None),
        P("modes", "space", None),
        P("modes", "space", None),
        P("space", None),
        P("space", None),
        P(),
        P(),
        P(),
        P(),
    )
    out_specs = (P("modes", "space", None), P("modes", "space", None))
    return jax.shard_map(
        on_device, mesh=mesh, in_specs=in_specs, out_specs=out_specs, check_vma=False
    )
```

```python
import functools

import jax
import jax.numpy as jnp
from jax import lax
from jax.experimental import pallas as pl
from jax.experimental.pallas import tpu as pltpu
from jax.sharding import PartitionSpec as P

NZ = 8
LANES = 128
SUB = 8
TILE16 = 16
VMEM_LIMIT = 40 * 1024 * 1024

HERMITE_NODES = (
    0.0,
    1.355626179974266,
    -1.355626179974266,
    2.8569700138728056,
    -2.8569700138728056,
)

F32 = jnp.float32
BF16 = jnp.bfloat16


def split2(x):
    high = x.astype(BF16)
    return high, (x - high.astype(F32)).astype(BF16)


def dot(a, b):
    return jnp.dot(a, b, preferred_element_type=F32)


def dot_nt(a, b):
    return lax.dot_general(a, b, (((1,), (1,)), ((), ())), preferred_element_type=F32)


def dot3(a_high, a_low, b_high, b_low):
    return dot(a_high, b_high) + (dot(a_high, b_low) + dot(a_low, b_high))


def lane_ids(shape):
    return lax.broadcasted_iota(jnp.int32, shape, len(shape) - 1)


def load_group(ref, group, modes, groups):
    return ref[pl.ds(group, modes, stride=groups), :]


def pad_rows(x, rows):
    if x.shape[0] == rows:
        return x
    return jnp.concatenate([x, jnp.zeros((rows - x.shape[0], x.shape[1]), x.dtype)], axis=0)


def emit_slots(me, parts, grouped, outs, padded):
    groups = grouped.shape[0] // padded
    per = groups // parts
    lane = lane_ids((padded, LANES))
    for k, out in enumerate(outs):
        q = lax.rem(me + k, parts)
        start = pl.multiple_of(q * (per * padded), SUB)
        out[: per * padded, :] = grouped[pl.ds(start, per * padded), :]
        before = pl.multiple_of(jnp.maximum(q * per - 1, 0) * padded, SUB)
        after = pl.multiple_of(jnp.minimum(q * per + per, groups - 1) * padded, SUB)
        low = pltpu.roll(grouped[pl.ds(before, padded), :], NZ, 1)
        high = pltpu.roll(grouped[pl.ds(after, padded), :], NZ, 1)
        rim = jnp.where((lane < NZ) & (q > 0), low, 0.0)
        rim = jnp.where((lane >= NZ) & (lane < 2 * NZ) & (q < parts - 1), high, rim)
        packed = rim[:SUB]
        for tile in range(1, padded // SUB):
            packed = packed + pltpu.roll(rim[tile * SUB : (tile + 1) * SUB], 2 * NZ * tile, 1)
        out[per * padded :, :] = packed


def source_kernel(parts, modes, padded, v_hbm, j_hbm, a_hbm, *rest):
    outs, (grouped, v_ref, j_ref, a_ref, sems) = rest[:-5], rest[-5:]
    groups = a_ref.shape[0]
    starts = range(0, modes, SUB)
    pairs = [(a_hbm, a_ref)]
    for start in starts:
        rows = pl.ds(start * groups, min(SUB, modes - start) * groups)
        pairs += [(v_hbm.at[rows], v_ref.at[rows]), (j_hbm.at[rows], j_ref.at[rows])]
    copies = [pltpu.make_async_copy(x, y, sems.at[i]) for i, (x, y) in enumerate(pairs)]
    for copy in copies:
        copy.start()
    me = lax.axis_index("modes")
    copies[0].wait()
    factor = 0.8 / (6.0 * a_ref[...])
    for tile, start in enumerate(starts):
        copies[2 * tile + 1].wait()
        copies[2 * tile + 2].wait()
        count = min(SUB, modes - start)
        for g in range(groups):
            rows = pl.ds(start * groups + g, count, stride=groups)
            w = v_ref[rows, :] + j_ref[rows, :] * factor[g : g + 1]
            grouped[g * padded + start : g * padded + start + SUB, :] = pad_rows(w, SUB)
    emit_slots(me, parts, grouped, outs, padded)


def stencil_groups(x_ref, near_ref, far_ref, modes, groups, padded, emit):
    lane = lane_ids((padded, LANES))
    depth = lane % NZ
    fields = [pad_rows(load_group(x_ref, g, modes, groups), padded) for g in range(groups)]
    for g in range(groups):
        x = fields[g]
        total = 6.0 * x - pad_rows(load_group(near_ref, g, modes, groups), padded)
        total = total - pad_rows(load_group(far_ref, g, modes, groups), padded)
        total = total - jnp.where(depth < NZ - 1, pltpu.roll(x, LANES - 1, 1), 0.0)
        total = total - jnp.where(depth > 0, pltpu.roll(x, 1, 1), 0.0)
        right = fields[g + 1] if g + 1 < groups else jnp.zeros_like(x)
        left = fields[g - 1] if g > 0 else jnp.zeros_like(x)
        total = total - pltpu.roll(jnp.where(lane < NZ, right, x), LANES - NZ, 1)
        total = total - pltpu.roll(jnp.where(lane >= LANES - NZ, left, x), NZ, 1)
        emit(g, x, total)


def rough_kernel(parts, modes, padded, groups, v_ref, near_ref, far_ref, *rest):
    outs, grouped = rest[:-1], rest[-1]
    me = lax.axis_index("modes")

    def emit(g, _, total):
        grouped[g * padded : (g + 1) * padded, :] = total

    stencil_groups(v_ref, near_ref, far_ref, modes, groups, padded, emit)
    emit_slots(me, parts, grouped, outs, padded)


def thermal_kernel(modes, padded, groups, t_ref, near_ref, far_ref, out_ref):
    def emit(g, x, total):
        out_ref[g * padded : (g + 1) * padded, :] = x - 0.15 * total

    stencil_groups(t_ref, near_ref, far_ref, modes, groups, padded, emit)


def tables_kernel(
    parts, modes, padded, table_ref, nodes_ref, share_ref, z_ref, zone_ref,
    ah_ref, al_ref, bh_ref, bl_ref, wh_ref, wl_ref, lift_ref, zones_ref,
    cols, basis_t,
):
    nreg, npar = z_ref.shape
    all_modes = parts * modes
    rows = parts * padded
    points = nodes_ref.shape[1]
    me = lax.axis_index("modes")
    kinds = 4 * TILE16

    slot = lax.broadcasted_iota(jnp.int32, (rows, all_modes), 0)
    mode = lax.broadcasted_iota(jnp.int32, (rows, all_modes), 1)
    within = slot % padded
    pick = (within < modes) & (mode == slot // padded * modes + within)
    pick = jnp.where(pick, 1.0, 0.0).astype(BF16)
    table = table_ref[...].astype(F32).astype(BF16)
    spread = lax.broadcasted_iota(jnp.int32, (kinds, npar), 0) % TILE16
    spread = spread == lax.broadcasted_iota(jnp.int32, (kinds, npar), 1)
    table = dot(jnp.where(spread, 1.0, 0.0).astype(BF16), table).astype(BF16)
    along = dot_nt(table, pick)
    down = dot_nt(pick, table)
    cols[...] = down

    def one_hot(values, axis):
        kind = lax.broadcasted_iota(jnp.int32, values.shape, axis)
        row = lax.broadcasted_iota(jnp.int32, values.shape, 1 - axis)
        hit = (values == (kind // TILE16).astype(F32)) & (kind % TILE16 < npar)
        return jnp.where(hit & (row % padded < modes), 1.0, 0.0).astype(BF16)

    hot_down, hot_along = one_hot(down, 1), one_hot(along, 0)
    agree = dot(hot_down, hot_along)
    degree_down = jnp.sum(down[:, :TILE16], axis=1, keepdims=True)
    degree_along = jnp.sum(along[:TILE16], axis=0, keepdims=True)
    linked = (agree == npar - 1.0) & (jnp.abs(degree_down - degree_along) == 1.0)
    same = agree == float(npar)
    left = lax.broadcasted_iota(jnp.int32, (kinds, kinds), 0)
    right = lax.broadcasted_iota(jnp.int32, (kinds, kinds), 1)
    step = (left % TILE16 == right % TILE16) & (jnp.abs(left // TILE16 - right // TILE16) == 1)
    root = jnp.where(step, jnp.sqrt((jnp.maximum(left, right) // TILE16).astype(F32)), 0.0)
    param = lax.broadcasted_iota(jnp.int32, (1, kinds), 1) % TILE16
    hot3 = jnp.concatenate([hot_along] * 3, axis=0)
    for r in range(nreg):
        weight = jnp.zeros((1, kinds), F32)
        for m in range(npar):
            weight = jnp.where(param == m, z_ref[r, m], weight)
        link = root * weight
        high = link.astype(BF16)
        mid = (link - high.astype(F32)).astype(BF16)
        low = (link - high.astype(F32) - mid.astype(F32)).astype(BF16)
        part = dot(hot_down, jnp.concatenate([high, mid, low], axis=1)).astype(BF16)
        matrix = jnp.where(linked, dot(part, hot3), jnp.where(same, 1.0, 0.0))
        high, low = split2(matrix)
        ah_ref[r * rows : (r + 1) * rows, :] = high
        al_ref[r * rows : (r + 1) * rows, :] = low

    nodes = nodes_ref[...]
    t = jnp.zeros(nodes.shape, F32)
    for which in range(1, len(HERMITE_NODES)):
        t = jnp.where(nodes == which, HERMITE_NODES[which], t)
    h2 = (t * t - 1.0) * (1.0 / 2.0**0.5)
    h3 = (t * t * t - 3.0 * t) * (1.0 / 6.0**0.5)
    share = share_ref[...].astype(F32) * (0.25 / (512.0 * points * all_modes))
    tiles = points // LANES

    def block(b, carry):
        at = pl.multiple_of(b * TILE16, TILE16)
        mine = cols[pl.ds(at, TILE16), :]
        row = lax.broadcasted_iota(jnp.int32, (TILE16, LANES), 0) + at
        basis = [jnp.where(row % padded < modes, 1.0, 0.0)] * tiles
        for m in range(npar):
            own = jnp.broadcast_to(mine[:, m : m + 1], (TILE16, LANES))
            is0, is1, is2 = own == 0.0, own == 1.0, own == 2.0
            for i in range(tiles):
                lanes = slice(i * LANES, (i + 1) * LANES)
                factor = jnp.where(is2, h2[m : m + 1, lanes], h3[m : m + 1, lanes])
                factor = jnp.where(is1, t[m : m + 1, lanes], factor)
                basis[i] = basis[i] * jnp.where(is0, 1.0, factor)
        for i in range(tiles):
            lanes = slice(i * LANES, (i + 1) * LANES)
            basis_t[pl.ds(at, TILE16), lanes] = basis[i]
            high, low = split2(basis[i] * share[:, lanes])
            wh_ref[pl.ds(at, TILE16), lanes] = high
            wl_ref[pl.ds(at, TILE16), lanes] = low
        return carry

    lax.fori_loop(0, rows // TILE16, block, 0)
    high, low = split2(basis_t[...].T)
    bh_ref[...] = high
    bl_ref[...] = low

    terms = []
    for r in range(nreg):
        lift = jnp.ones((1, points), F32)
        for m in range(npar):
            lift = lift + z_ref[r, m] * t[m : m + 1]
        terms.append(lift)
    lift = jnp.concatenate(terms, axis=0)
    high = lift.astype(BF16).astype(F32)
    mid = (lift - high).astype(BF16).astype(F32)
    low = lift - high - mid
    stacked = jnp.concatenate(
        [high, mid, low, jnp.zeros((LANES - 3 * nreg, points), F32)], axis=0
    )
    lift_ref[...] = stacked.T.astype(BF16)

    groups = zone_ref.shape[0]
    per = groups // parts
    zone = zone_ref[...]
    row = lax.broadcasted_iota(jnp.int32, zone.shape, 0)

    def pick_row(g):
        return jnp.sum(jnp.where(row == g, zone, 0), axis=0, keepdims=True)

    for s in range(per):
        zones_ref[:, s * LANES : (s + 1) * LANES] = pick_row(me * per + s)
    low = pltpu.roll(pick_row(jnp.maximum(me * per - 1, 0)), NZ, 1)
    high = pltpu.roll(pick_row(jnp.minimum(me * per + per, groups - 1)), NZ, 1)
    zones_ref[:, per * LANES :] = jnp.where(lane_ids(low.shape) < NZ, low, high)


def couple_kernel(parts, padded, per, nreg, halves, *refs):
    w_refs = refs[:parts]
    r_refs = refs[parts : 2 * parts]
    ah_ref, al_ref, zones_ref = refs[2 * parts : 2 * parts + 3]
    rel_refs = refs[2 * parts + 3 : 2 * parts + 3 + halves]
    rim_ref, *outs = refs[2 * parts + 3 + halves : -2]
    w_all, r_all = refs[-2:]
    me = lax.axis_index("modes")
    rows = parts * padded
    width = per * LANES
    for k in range(parts):
        source = lax.rem(me + (parts - k), parts)
        at = pl.multiple_of(source * padded, SUB)
        for chunk, dest in ((w_refs[k], w_all), (r_refs[k], r_all)):
            for s in range(per):
                dest[pl.ds(at, padded), s * LANES : (s + 1) * LANES] = chunk[
                    s * padded : (s + 1) * padded, :
                ]
            packed = chunk[per * padded :, :]
            for tile in range(padded // SUB):
                spot = pl.multiple_of(at + tile * SUB, SUB)
                shift = (LANES - 2 * NZ * tile) % LANES
                part = pltpu.roll(packed, shift, 1) if shift else packed
                dest[pl.ds(spot, SUB), width:] = part
    r_high, r_low = split2(r_all[...])
    zones = zones_ref[...]
    applied = jnp.zeros(r_all.shape, F32)
    for r in range(nreg):
        a_high = ah_ref[r * rows : (r + 1) * rows, :]
        a_low = al_ref[r * rows : (r + 1) * rows, :]
        applied = jnp.where(zones == r, dot3(a_high, a_low, r_high, r_low), applied)
    w_all[...] = w_all[...] - (0.8 / 6.0) * applied
    for h, rel_ref in enumerate(rel_refs):
        rel_ref[...] = w_all[:, h * width // halves : (h + 1) * width // halves]
    rim_ref[...] = w_all[:, width:]
    for k, out in enumerate(outs):
        target = lax.rem(me + k, parts)
        at = pl.multiple_of(target * padded, SUB)
        for s in range(per):
            out[s * padded : (s + 1) * padded, :] = w_all[
                pl.ds(at, padded), s * LANES : (s + 1) * LANES
            ]


def plane_kernel(nreg, halves, *refs):
    rel_refs, (rim_ref, zones_ref, bh_ref, bl_ref, lift_ref, part_ref, spread_ref) = (
        refs[:halves], refs[halves:],
    )
    width = sum(ref.shape[1] for ref in rel_refs)
    rel = jnp.concatenate([ref[...] for ref in rel_refs], axis=1)
    rim = rim_ref[...]
    lane = lane_ids(rel.shape)
    depth = lane % NZ
    wide = jnp.concatenate([rim, jnp.zeros((rim.shape[0], width - LANES), F32)], axis=1)
    along_z = jnp.where(depth < NZ - 1, pltpu.roll(rel, width - 1, 1), 0.0)
    along_z = along_z - jnp.where(depth > 0, pltpu.roll(rel, 1, 1), 0.0)
    after = pltpu.roll(wide, width - 2 * NZ, 1)
    along_y = jnp.where(lane >= width - NZ, after, pltpu.roll(rel, width - NZ, 1))
    along_y = along_y - jnp.where(lane < NZ, wide, pltpu.roll(rel, NZ, 1))
    b_high, b_low = bh_ref[...], bl_ref[...]
    total = None
    for grad in (along_y, along_z):
        g_high, g_low = split2(grad)
        at_point = dot3(b_high, b_low, g_high, g_low)
        total = at_point * at_point if total is None else total + at_point * at_point
    row = lax.broadcasted_iota(jnp.int32, (LANES, width), 0)
    hot = (row < 3 * nreg) & (row % nreg == zones_ref[:, :width])
    spread = dot(lift_ref[...], jnp.where(hot, 1.0, 0.0).astype(BF16))
    spread_ref[...] = spread
    part_ref[...] = spread * total


def joule_kernel(
    parts, padded, per, halves, half, near_ref, far_ref, part_ref, spread_ref, a_ref,
    bh_ref, bl_ref, wh_ref, wl_ref, *rest,
):
    outs, heat_ref = rest[:-1], rest[-1]
    me = lax.axis_index("modes")
    own = per // halves
    lanes = slice(half * own * LANES, (half + 1) * own * LANES)
    g_high, g_low = split2(far_ref[...] - near_ref[...])
    at_point = dot3(bh_ref[...], bl_ref[...], g_high, g_low)
    joule = part_ref[:, lanes] + spread_ref[:, lanes] * (at_point * at_point)
    j_high, j_low = split2(joule)
    heat = dot3(wh_ref[...], wl_ref[...], j_high, j_low)
    for s in range(own):
        heat_ref[:, s * LANES : (s + 1) * LANES] = (
            heat[:, s * LANES : (s + 1) * LANES] * a_ref[pl.ds(me * per + half * own + s, 1), :]
        )
    for k, out in enumerate(outs):
        target = lax.rem(me + k, parts)
        at = pl.multiple_of(target * padded, SUB)
        for s in range(own):
            out[s * padded : (s + 1) * padded, :] = heat_ref[
                pl.ds(at, padded), s * LANES : (s + 1) * LANES
            ]


def gather_kernel(parts, modes, padded, per, *refs):
    chunks, out = refs[:parts], refs[parts]
    me = lax.axis_index("modes")
    for k in range(parts):
        q = lax.rem(me + (parts - k), parts)
        for s in range(per):
            rows = chunks[k][s * padded : s * padded + modes, :]
            out[pl.ds(q * per + s, modes, stride=parts * per), :] = rows


def final_kernel(parts, modes, padded, per, halves, *refs):
    chunks, base, out = refs[: parts * halves], refs[-2], refs[-1]
    me = lax.axis_index("modes")
    own = per // halves
    for k in range(parts):
        q = lax.rem(me + (parts - k), parts)
        for s in range(per):
            chunk = chunks[s // own * parts + k]
            at = pl.multiple_of((q * per + s) * padded, SUB)
            within = s % own * padded
            rows = base[pl.ds(at, padded), :] + 0.1 * chunk[within : within + padded, :]
            out[pl.ds(q * per + s, modes, stride=parts * per), :] = rows[:modes]


def call(kernel, out_shape, args, scratch=(), smem=(), hbm=(), limit=VMEM_LIMIT):
    specs = [
        pl.BlockSpec(
            memory_space=pltpu.SMEM if i in smem else pltpu.HBM if i in hbm else pltpu.VMEM
        )
        for i in range(len(args))
    ]
    many = isinstance(out_shape, (list, tuple))
    vmem = pl.BlockSpec(memory_space=pltpu.VMEM)
    nbytes = sum(x.size * x.dtype.itemsize for x in args)
    return pl.pallas_call(
        kernel,
        out_shape=out_shape,
        in_specs=specs,
        out_specs=[vmem] * len(out_shape) if many else vmem,
        scratch_shapes=list(scratch),
        compiler_params=pltpu.CompilerParams(vmem_limit_bytes=limit),
        cost_estimate=pl.CostEstimate(flops=0, bytes_accessed=nbytes, transcendentals=0),
    )(*args)


def exchange(chunks):
    parts = lax.axis_size("modes")
    received = [chunks[0]]
    for k in range(1, parts):
        pairs = [(i, (i + k) % parts) for i in range(parts)]
        received.append(lax.ppermute(chunks[k], "modes", pairs))
    return received


def halo(x):
    count = lax.axis_size("space")
    near = [(i, i ^ 1) for i in range(count) if i ^ 1 < count]
    far = [(i, ((i - 1) ^ 1) + 1) for i in range(1, count) if ((i - 1) ^ 1) + 1 < count]
    far = lax.ppermute(x, "space", far)
    return lax.ppermute(x, "space", near), far


def on_device(
    voltage_expansion,
    current_injection,
    thermal_state,
    average_electric_transport,
    material_zone,
    zone_relative_response,
    polynomial_exponent_rows,
    quadrature_abscissa_choice,
    quadrature_integer_share,
):
    parts = lax.axis_size("modes")
    modes, planes, columns = voltage_expansion.shape
    nreg = zone_relative_response.shape[0]
    points = quadrature_integer_share.shape[0]
    groups = columns // LANES
    per = groups // parts
    padded = -(-modes // SUB) * SUB
    halves = 1
    rows = parts * padded
    assert planes == 1 and groups * LANES == columns and per * parts == groups
    assert polynomial_exponent_rows.shape[1] <= TILE16 and points % LANES == 0
    assert rows % TILE16 == 0 and 2 * NZ * padded <= SUB * LANES and 3 * nreg <= LANES

    def flat(x):
        return x.reshape(modes * groups, LANES)

    def struct(*shape, dtype=F32):
        return jax.ShapeDtypeStruct(shape, dtype)

    v, cur, temp = flat(voltage_expansion), flat(current_injection), flat(thermal_state)
    avg = average_electric_transport.reshape(groups, LANES)
    zone = material_zone.reshape(groups, LANES)
    chunk = struct(per * padded, LANES)
    rimmed = struct(per * padded + SUB, LANES)
    grouped = pltpu.VMEM((groups * padded, LANES), F32)

    fields = pltpu.VMEM((modes * groups, LANES), F32)
    v_near, v_far = halo(v)
    source = call(
        functools.partial(source_kernel, parts, modes, padded),
        [rimmed] * parts,
        [v, cur, avg],
        [grouped, fields, fields, pltpu.VMEM((groups, LANES), F32), pltpu.SemaphoreType.DMA((1 + 2 * (padded // SUB),))],
        hbm=(0, 1, 2),
        limit=62 * 1024 * 1024,
    )
    source = exchange(source)
    temp, source[1] = lax.optimization_barrier((temp, source[1]))
    a_high, a_low, b_high, b_low, w_high, w_low, lift, zones = call(
        functools.partial(tables_kernel, parts, modes, padded),
        [
            struct(nreg * rows, rows, dtype=BF16),
            struct(nreg * rows, rows, dtype=BF16),
            struct(points, rows, dtype=BF16),
            struct(points, rows, dtype=BF16),
            struct(rows, points, dtype=BF16),
            struct(rows, points, dtype=BF16),
            struct(points, LANES, dtype=BF16),
            struct(1, (per + 1) * LANES, dtype=jnp.int32),
        ],
        [
            polynomial_exponent_rows.T,
            quadrature_abscissa_choice.T,
            quadrature_integer_share.reshape(1, points),
            zone_relative_response,
            zone,
        ],
        [pltpu.VMEM((rows, 4 * TILE16), F32), pltpu.VMEM((rows, points), F32)],
        smem=(3,),
    )
    v, zones = lax.optimization_barrier((v, zones))
    rough = call(
        functools.partial(rough_kernel, parts, modes, padded, groups),
        [rimmed] * parts, [v, v_near, v_far], [grouped],
    )
    rough = exchange(rough)
    t_near, t_far = halo(temp)
    base = call(
        functools.partial(thermal_kernel, modes, padded, groups),
        struct(groups * padded, LANES), [temp, t_near, t_far],
    )
    wide = (per + 1) * LANES
    half_width = per * LANES // halves
    results = call(
        functools.partial(couple_kernel, parts, padded, per, nreg, halves),
        [struct(rows, half_width)] * halves + [struct(rows, LANES)] + [chunk] * parts,
        [*source, *rough, a_high, a_low, zones],
        [pltpu.VMEM((rows, wide), F32), pltpu.VMEM((rows, wide), F32)],
    )
    relaxed, rim, back = results[:halves], results[halves], results[halves + 1 :]
    beside = [halo(x) for x in relaxed]
    base, *back = lax.optimization_barrier((base, *back))
    back = exchange(back)
    part, spread = call(
        functools.partial(plane_kernel, nreg, halves),
        [struct(points, per * LANES)] * 2,
        [*relaxed, rim, zones, b_high, b_low, lift],
    )
    heat = []
    for half in range(halves):
        pieces = call(
            functools.partial(joule_kernel, parts, padded, per, halves, half),
            [struct(per // halves * padded, LANES)] * parts,
            [*beside[half], part, spread, avg, b_high, b_low, w_high, w_low],
            [pltpu.VMEM((rows, half_width), F32)],
        )
        heat += exchange(pieces)
    relaxed_voltage = call(
        functools.partial(gather_kernel, parts, modes, padded, per),
        struct(modes * groups, LANES), back,
    )
    advanced = call(
        functools.partial(final_kernel, parts, modes, padded, per, halves),
        struct(modes * groups, LANES), [*heat, base],
    )
    shape = voltage_expansion.shape
    return relaxed_voltage.reshape(shape), advanced.reshape(shape)


def solution(mesh):
    in_specs = (
        P("modes", "space", None),
        P("modes", "space", None),
        P("modes", "space", None),
        P("space", None),
        P("space", None),
        P(),
        P(),
        P(),
        P(),
    )
    out_specs = (P("modes", "space", None), P("modes", "space", None))
    return jax.shard_map(
        on_device, mesh=mesh, in_specs=in_specs, out_specs=out_specs, check_vma=False
    )
```

```python
import functools

import jax
import jax.numpy as jnp
from jax import lax
from jax.experimental import pallas as pl
from jax.experimental.pallas import tpu as pltpu
from jax.sharding import PartitionSpec as P

NZ = 8
LANES = 128
SUB = 8
TILE16 = 16
VMEM_LIMIT = 40 * 1024 * 1024

HERMITE_NODES = (
    0.0,
    1.355626179974266,
    -1.355626179974266,
    2.8569700138728056,
    -2.8569700138728056,
)

F32 = jnp.float32
BF16 = jnp.bfloat16


def split2(x):
    high = x.astype(BF16)
    return high, (x - high.astype(F32)).astype(BF16)


def dot(a, b):
    return jnp.dot(a, b, preferred_element_type=F32)


def dot_nt(a, b):
    return lax.dot_general(a, b, (((1,), (1,)), ((), ())), preferred_element_type=F32)


def dot3(a_high, a_low, b_high, b_low):
    return dot(a_high, b_high) + (dot(a_high, b_low) + dot(a_low, b_high))


def lane_ids(shape):
    return lax.broadcasted_iota(jnp.int32, shape, len(shape) - 1)


def load_group(ref, group, modes, groups):
    return ref[pl.ds(group, modes, stride=groups), :]


def pad_rows(x, rows):
    if x.shape[0] == rows:
        return x
    return jnp.concatenate([x, jnp.zeros((rows - x.shape[0], x.shape[1]), x.dtype)], axis=0)


def emit_slots(me, parts, grouped, outs, padded):
    groups = grouped.shape[0] // padded
    per = groups // parts
    lane = lane_ids((padded, LANES))
    for k, out in enumerate(outs):
        q = lax.rem(me + k, parts)
        start = pl.multiple_of(q * (per * padded), SUB)
        out[: per * padded, :] = grouped[pl.ds(start, per * padded), :]
        before = pl.multiple_of(jnp.maximum(q * per - 1, 0) * padded, SUB)
        after = pl.multiple_of(jnp.minimum(q * per + per, groups - 1) * padded, SUB)
        low = pltpu.roll(grouped[pl.ds(before, padded), :], NZ, 1)
        high = pltpu.roll(grouped[pl.ds(after, padded), :], NZ, 1)
        rim = jnp.where((lane < NZ) & (q > 0), low, 0.0)
        rim = jnp.where((lane >= NZ) & (lane < 2 * NZ) & (q < parts - 1), high, rim)
        packed = rim[:SUB]
        for tile in range(1, padded // SUB):
            packed = packed + pltpu.roll(rim[tile * SUB : (tile + 1) * SUB], 2 * NZ * tile, 1)
        out[per * padded :, :] = packed


def source_kernel(parts, modes, padded, v_hbm, j_hbm, a_hbm, *rest):
    outs, (grouped, v_ref, j_ref, a_ref, sems) = rest[:-5], rest[-5:]
    groups = a_ref.shape[0]
    starts = range(0, modes, SUB)
    pairs = [(a_hbm, a_ref)]
    for start in starts:
        rows = pl.ds(start * groups, min(SUB, modes - start) * groups)
        pairs += [(v_hbm.at[rows], v_ref.at[rows]), (j_hbm.at[rows], j_ref.at[rows])]
    copies = [pltpu.make_async_copy(x, y, sems.at[i]) for i, (x, y) in enumerate(pairs)]
    for copy in copies:
        copy.start()
    me = lax.axis_index("modes")
    copies[0].wait()
    factor = 0.8 / (6.0 * a_ref[...])
    for tile, start in enumerate(starts):
        copies[2 * tile + 1].wait()
        copies[2 * tile + 2].wait()
        count = min(SUB, modes - start)
        for g in range(groups):
            rows = pl.ds(start * groups + g, count, stride=groups)
            w = v_ref[rows, :] + j_ref[rows, :] * factor[g : g + 1]
            grouped[g * padded + start : g * padded + start + SUB, :] = pad_rows(w, SUB)
    emit_slots(me, parts, grouped, outs, padded)


def stencil_groups(x_ref, near_ref, far_ref, modes, groups, padded, emit):
    lane = lane_ids((padded, LANES))
    depth = lane % NZ
    fields = [pad_rows(load_group(x_ref, g, modes, groups), padded) for g in range(groups)]
    for g in range(groups):
        x = fields[g]
        total = 6.0 * x - pad_rows(load_group(near_ref, g, modes, groups), padded)
        total = total - pad_rows(load_group(far_ref, g, modes, groups), padded)
        total = total - jnp.where(depth < NZ - 1, pltpu.roll(x, LANES - 1, 1), 0.0)
        total = total - jnp.where(depth > 0, pltpu.roll(x, 1, 1), 0.0)
        right = fields[g + 1] if g + 1 < groups else jnp.zeros_like(x)
        left = fields[g - 1] if g > 0 else jnp.zeros_like(x)
        total = total - pltpu.roll(jnp.where(lane < NZ, right, x), LANES - NZ, 1)
        total = total - pltpu.roll(jnp.where(lane >= LANES - NZ, left, x), NZ, 1)
        emit(g, x, total)


def rough_kernel(parts, modes, padded, groups, v_ref, near_ref, far_ref, *rest):
    outs, grouped = rest[:-1], rest[-1]
    me = lax.axis_index("modes")

    def emit(g, _, total):
        grouped[g * padded : (g + 1) * padded, :] = total

    stencil_groups(v_ref, near_ref, far_ref, modes, groups, padded, emit)
    emit_slots(me, parts, grouped, outs, padded)


def thermal_kernel(modes, padded, groups, t_ref, near_ref, far_ref, out_ref):
    def emit(g, x, total):
        out_ref[g * padded : (g + 1) * padded, :] = x - 0.15 * total

    stencil_groups(t_ref, near_ref, far_ref, modes, groups, padded, emit)


def tables_kernel(
    parts, modes, padded, table_ref, nodes_ref, share_ref, z_ref, zone_ref,
    ah_ref, al_ref, bh_ref, bl_ref, wh_ref, wl_ref, lift_ref, zones_ref,
    cols, basis_t,
):
    nreg, npar = z_ref.shape
    all_modes = parts * modes
    rows = parts * padded
    points = nodes_ref.shape[1]
    me = lax.axis_index("modes")
    kinds = 4 * TILE16

    slot = lax.broadcasted_iota(jnp.int32, (rows, all_modes), 0)
    mode = lax.broadcasted_iota(jnp.int32, (rows, all_modes), 1)
    within = slot % padded
    pick = (within < modes) & (mode == slot // padded * modes + within)
    pick = jnp.where(pick, 1.0, 0.0).astype(BF16)
    table = table_ref[...].astype(F32).astype(BF16)
    spread = lax.broadcasted_iota(jnp.int32, (kinds, npar), 0) % TILE16
    spread = spread == lax.broadcasted_iota(jnp.int32, (kinds, npar), 1)
    table = dot(jnp.where(spread, 1.0, 0.0).astype(BF16), table).astype(BF16)
    along = dot_nt(table, pick)
    down = dot_nt(pick, table)
    cols[...] = down

    def one_hot(values, axis):
        kind = lax.broadcasted_iota(jnp.int32, values.shape, axis)
        row = lax.broadcasted_iota(jnp.int32, values.shape, 1 - axis)
        hit = (values == (kind // TILE16).astype(F32)) & (kind % TILE16 < npar)
        return jnp.where(hit & (row % padded < modes), 1.0, 0.0).astype(BF16)

    hot_down, hot_along = one_hot(down, 1), one_hot(along, 0)
    agree = dot(hot_down, hot_along)
    degree_down = jnp.sum(down[:, :TILE16], axis=1, keepdims=True)
    degree_along = jnp.sum(along[:TILE16], axis=0, keepdims=True)
    linked = (agree == npar - 1.0) & (jnp.abs(degree_down - degree_along) == 1.0)
    same = agree == float(npar)
    left = lax.broadcasted_iota(jnp.int32, (kinds, kinds), 0)
    right = lax.broadcasted_iota(jnp.int32, (kinds, kinds), 1)
    step = (left % TILE16 == right % TILE16) & (jnp.abs(left // TILE16 - right // TILE16) == 1)
    root = jnp.where(step, jnp.sqrt((jnp.maximum(left, right) // TILE16).astype(F32)), 0.0)
    param = lax.broadcasted_iota(jnp.int32, (1, kinds), 1) % TILE16
    hot3 = jnp.concatenate([hot_along] * 3, axis=0)
    for r in range(nreg):
        weight = jnp.zeros((1, kinds), F32)
        for m in range(npar):
            weight = jnp.where(param == m, z_ref[r, m], weight)
        link = root * weight
        high = link.astype(BF16)
        mid = (link - high.astype(F32)).astype(BF16)
        low = (link - high.astype(F32) - mid.astype(F32)).astype(BF16)
        part = dot(hot_down, jnp.concatenate([high, mid, low], axis=1)).astype(BF16)
        matrix = jnp.where(linked, dot(part, hot3), jnp.where(same, 1.0, 0.0))
        high, low = split2(matrix)
        ah_ref[r * rows : (r + 1) * rows, :] = high
        al_ref[r * rows : (r + 1) * rows, :] = low

    nodes = nodes_ref[...]
    t = jnp.zeros(nodes.shape, F32)
    for which in range(1, len(HERMITE_NODES)):
        t = jnp.where(nodes == which, HERMITE_NODES[which], t)
    h2 = (t * t - 1.0) * (1.0 / 2.0**0.5)
    h3 = (t * t * t - 3.0 * t) * (1.0 / 6.0**0.5)
    share = share_ref[...].astype(F32) * (0.25 / (512.0 * points * all_modes))
    tiles = points // LANES

    def block(b, carry):
        at = pl.multiple_of(b * TILE16, TILE16)
        mine = cols[pl.ds(at, TILE16), :]
        row = lax.broadcasted_iota(jnp.int32, (TILE16, LANES), 0) + at
        basis = [jnp.where(row % padded < modes, 1.0, 0.0)] * tiles
        for m in range(npar):
            own = jnp.broadcast_to(mine[:, m : m + 1], (TILE16, LANES))
            is0, is1, is2 = own == 0.0, own == 1.0, own == 2.0
            for i in range(tiles):
                lanes = slice(i * LANES, (i + 1) * LANES)
                factor = jnp.where(is2, h2[m : m + 1, lanes], h3[m : m + 1, lanes])
                factor = jnp.where(is1, t[m : m + 1, lanes], factor)
                basis[i] = basis[i] * jnp.where(is0, 1.0, factor)
        for i in range(tiles):
            lanes = slice(i * LANES, (i + 1) * LANES)
            basis_t[pl.ds(at, TILE16), lanes] = basis[i]
            high, low = split2(basis[i] * share[:, lanes])
            wh_ref[pl.ds(at, TILE16), lanes] = high
            wl_ref[pl.ds(at, TILE16), lanes] = low
        return carry

    lax.fori_loop(0, rows // TILE16, block, 0)
    high, low = split2(basis_t[...].T)
    bh_ref[...] = high
    bl_ref[...] = low

    terms = []
    for r in range(nreg):
        lift = jnp.ones((1, points), F32)
        for m in range(npar):
            lift = lift + z_ref[r, m] * t[m : m + 1]
        terms.append(lift)
    lift = jnp.concatenate(terms, axis=0)
    high = lift.astype(BF16).astype(F32)
    mid = (lift - high).astype(BF16).astype(F32)
    low = lift - high - mid
    stacked = jnp.concatenate(
        [high, mid, low, jnp.zeros((LANES - 3 * nreg, points), F32)], axis=0
    )
    lift_ref[...] = stacked.T.astype(BF16)

    groups = zone_ref.shape[0]
    per = groups // parts
    zone = zone_ref[...]
    row = lax.broadcasted_iota(jnp.int32, zone.shape, 0)

    def pick_row(g):
        return jnp.sum(jnp.where(row == g, zone, 0), axis=0, keepdims=True)

    for s in range(per):
        zones_ref[:, s * LANES : (s + 1) * LANES] = pick_row(me * per + s)
    low = pltpu.roll(pick_row(jnp.maximum(me * per - 1, 0)), NZ, 1)
    high = pltpu.roll(pick_row(jnp.minimum(me * per + per, groups - 1)), NZ, 1)
    zones_ref[:, per * LANES :] = jnp.where(lane_ids(low.shape) < NZ, low, high)


def couple_kernel(parts, padded, per, nreg, halves, *refs):
    w_refs = refs[:parts]
    r_refs = refs[parts : 2 * parts]
    ah_ref, al_ref, zones_ref = refs[2 * parts : 2 * parts + 3]
    rel_refs = refs[2 * parts + 3 : 2 * parts + 3 + halves]
    rim_ref, *outs = refs[2 * parts + 3 + halves : -2]
    w_all, r_all = refs[-2:]
    me = lax.axis_index("modes")
    rows = parts * padded
    width = per * LANES
    for k in range(parts):
        source = lax.rem(me + (parts - k), parts)
        at = pl.multiple_of(source * padded, SUB)
        for chunk, dest in ((w_refs[k], w_all), (r_refs[k], r_all)):
            for s in range(per):
                dest[pl.ds(at, padded), s * LANES : (s + 1) * LANES] = chunk[
                    s * padded : (s + 1) * padded, :
                ]
            packed = chunk[per * padded :, :]
            for tile in range(padded // SUB):
                spot = pl.multiple_of(at + tile * SUB, SUB)
                shift = (LANES - 2 * NZ * tile) % LANES
                part = pltpu.roll(packed, shift, 1) if shift else packed
                dest[pl.ds(spot, SUB), width:] = part
    r_high, r_low = split2(r_all[...])
    zones = zones_ref[...]
    applied = jnp.zeros(r_all.shape, F32)
    for r in range(nreg):
        a_high = ah_ref[r * rows : (r + 1) * rows, :]
        a_low = al_ref[r * rows : (r + 1) * rows, :]
        applied = jnp.where(zones == r, dot3(a_high, a_low, r_high, r_low), applied)
    w_all[...] = w_all[...] - (0.8 / 6.0) * applied
    for h, rel_ref in enumerate(rel_refs):
        rel_ref[...] = w_all[:, h * width // halves : (h + 1) * width // halves]
    rim_ref[...] = w_all[:, width:]
    for k, out in enumerate(outs):
        target = lax.rem(me + k, parts)
        at = pl.multiple_of(target * padded, SUB)
        for s in range(per):
            out[s * padded : (s + 1) * padded, :] = w_all[
                pl.ds(at, padded), s * LANES : (s + 1) * LANES
            ]


def plane_kernel(nreg, halves, *refs):
    rel_refs, (rim_ref, zones_ref, bh_ref, bl_ref, lift_ref, part_ref, spread_ref) = (
        refs[:halves], refs[halves:],
    )
    width = sum(ref.shape[1] for ref in rel_refs)
    rel = jnp.concatenate([ref[...] for ref in rel_refs], axis=1)
    rim = rim_ref[...]
    lane = lane_ids(rel.shape)
    depth = lane % NZ
    wide = jnp.concatenate([rim, jnp.zeros((rim.shape[0], width - LANES), F32)], axis=1)
    along_z = jnp.where(depth < NZ - 1, pltpu.roll(rel, width - 1, 1), 0.0)
    along_z = along_z - jnp.where(depth > 0, pltpu.roll(rel, 1, 1), 0.0)
    after = pltpu.roll(wide, width - 2 * NZ, 1)
    along_y = jnp.where(lane >= width - NZ, after, pltpu.roll(rel, width - NZ, 1))
    along_y = along_y - jnp.where(lane < NZ, wide, pltpu.roll(rel, NZ, 1))
    b_high, b_low = bh_ref[...], bl_ref[...]
    total = None
    for grad in (along_y, along_z):
        g_high, g_low = split2(grad)
        at_point = dot3(b_high, b_low, g_high, g_low)
        total = at_point * at_point if total is None else total + at_point * at_point
    row = lax.broadcasted_iota(jnp.int32, (LANES, width), 0)
    hot = (row < 3 * nreg) & (row % nreg == zones_ref[:, :width])
    spread = dot(lift_ref[...], jnp.where(hot, 1.0, 0.0).astype(BF16))
    spread_ref[...] = spread
    part_ref[...] = spread * total


def joule_kernel(
    parts, padded, per, halves, half, near_ref, far_ref, part_ref, spread_ref, a_ref,
    bh_ref, bl_ref, wh_ref, wl_ref, *rest,
):
    outs, heat_ref = rest[:-1], rest[-1]
    me = lax.axis_index("modes")
    own = per // halves
    lanes = slice(half * own * LANES, (half + 1) * own * LANES)
    g_high, g_low = split2(far_ref[...] - near_ref[...])
    at_point = dot3(bh_ref[...], bl_ref[...], g_high, g_low)
    joule = part_ref[:, lanes] + spread_ref[:, lanes] * (at_point * at_point)
    j_high, j_low = split2(joule)
    heat = dot3(wh_ref[...], wl_ref[...], j_high, j_low)
    for s in range(own):
        heat_ref[:, s * LANES : (s + 1) * LANES] = (
            heat[:, s * LANES : (s + 1) * LANES] * a_ref[pl.ds(me * per + half * own + s, 1), :]
        )
    for k, out in enumerate(outs):
        target = lax.rem(me + k, parts)
        at = pl.multiple_of(target * padded, SUB)
        for s in range(own):
            out[s * padded : (s + 1) * padded, :] = heat_ref[
                pl.ds(at, padded), s * LANES : (s + 1) * LANES
            ]


def gather_kernel(parts, modes, padded, per, *refs):
    chunks, out = refs[:parts], refs[parts]
    me = lax.axis_index("modes")
    for k in range(parts):
        q = lax.rem(me + (parts - k), parts)
        for s in range(per):
            rows = chunks[k][s * padded : s * padded + modes, :]
            out[pl.ds(q * per + s, modes, stride=parts * per), :] = rows


def final_kernel(parts, modes, padded, per, halves, *refs):
    chunks, base, out = refs[: parts * halves], refs[-2], refs[-1]
    me = lax.axis_index("modes")
    own = per // halves
    for k in range(parts):
        q = lax.rem(me + (parts - k), parts)
        for s in range(per):
            chunk = chunks[s // own * parts + k]
            at = pl.multiple_of((q * per + s) * padded, SUB)
            within = s % own * padded
            rows = base[pl.ds(at, padded), :] + 0.1 * chunk[within : within + padded, :]
            out[pl.ds(q * per + s, modes, stride=parts * per), :] = rows[:modes]


def call(kernel, out_shape, args, scratch=(), smem=(), hbm=(), limit=VMEM_LIMIT):
    specs = [
        pl.BlockSpec(
            memory_space=pltpu.SMEM if i in smem else pltpu.HBM if i in hbm else pltpu.VMEM
        )
        for i in range(len(args))
    ]
    many = isinstance(out_shape, (list, tuple))
    vmem = pl.BlockSpec(memory_space=pltpu.VMEM)
    nbytes = sum(x.size * x.dtype.itemsize for x in args)
    return pl.pallas_call(
        kernel,
        out_shape=out_shape,
        in_specs=specs,
        out_specs=[vmem] * len(out_shape) if many else vmem,
        scratch_shapes=list(scratch),
        compiler_params=pltpu.CompilerParams(vmem_limit_bytes=limit),
        cost_estimate=pl.CostEstimate(flops=0, bytes_accessed=nbytes, transcendentals=0),
    )(*args)


def exchange(chunks):
    parts = lax.axis_size("modes")
    received = [chunks[0]]
    for k in range(1, parts):
        pairs = [(i, (i + k) % parts) for i in range(parts)]
        received.append(lax.ppermute(chunks[k], "modes", pairs))
    return received


def halo(x):
    count = lax.axis_size("space")
    near = [(i, i ^ 1) for i in range(count) if i ^ 1 < count]
    far = [(i, ((i - 1) ^ 1) + 1) for i in range(1, count) if ((i - 1) ^ 1) + 1 < count]
    far = lax.ppermute(x, "space", far)
    return lax.ppermute(x, "space", near), far


def on_device(
    voltage_expansion,
    current_injection,
    thermal_state,
    average_electric_transport,
    material_zone,
    zone_relative_response,
    polynomial_exponent_rows,
    quadrature_abscissa_choice,
    quadrature_integer_share,
):
    parts = lax.axis_size("modes")
    modes, planes, columns = voltage_expansion.shape
    nreg = zone_relative_response.shape[0]
    points = quadrature_integer_share.shape[0]
    groups = columns // LANES
    per = groups // parts
    padded = -(-modes // SUB) * SUB
    halves = 1
    rows = parts * padded
    assert planes == 1 and groups * LANES == columns and per * parts == groups
    assert polynomial_exponent_rows.shape[1] <= TILE16 and points % LANES == 0
    assert rows % TILE16 == 0 and 2 * NZ * padded <= SUB * LANES and 3 * nreg <= LANES

    def flat(x):
        return x.reshape(modes * groups, LANES)

    def struct(*shape, dtype=F32):
        return jax.ShapeDtypeStruct(shape, dtype)

    v, cur, temp = flat(voltage_expansion), flat(current_injection), flat(thermal_state)
    avg = average_electric_transport.reshape(groups, LANES)
    zone = material_zone.reshape(groups, LANES)
    chunk = struct(per * padded, LANES)
    rimmed = struct(per * padded + SUB, LANES)
    grouped = pltpu.VMEM((groups * padded, LANES), F32)

    fields = pltpu.VMEM((modes * groups, LANES), F32)
    v_near, v_far = halo(v)
    source = call(
        functools.partial(source_kernel, parts, modes, padded),
        [rimmed] * parts,
        [v, cur, avg],
        [grouped, fields, fields, pltpu.VMEM((groups, LANES), F32), pltpu.SemaphoreType.DMA((1 + 2 * (padded // SUB),))],
        hbm=(0, 1, 2),
        limit=62 * 1024 * 1024,
    )
    source = exchange(source)
    temp, source[1] = lax.optimization_barrier((temp, source[1]))
    a_high, a_low, b_high, b_low, w_high, w_low, lift, zones = call(
        functools.partial(tables_kernel, parts, modes, padded),
        [
            struct(nreg * rows, rows, dtype=BF16),
            struct(nreg * rows, rows, dtype=BF16),
            struct(points, rows, dtype=BF16),
            struct(points, rows, dtype=BF16),
            struct(rows, points, dtype=BF16),
            struct(rows, points, dtype=BF16),
            struct(points, LANES, dtype=BF16),
            struct(1, (per + 1) * LANES, dtype=jnp.int32),
        ],
        [
            polynomial_exponent_rows.T,
            quadrature_abscissa_choice.T,
            quadrature_integer_share.reshape(1, points),
            zone_relative_response,
            zone,
        ],
        [pltpu.VMEM((rows, 4 * TILE16), F32), pltpu.VMEM((rows, points), F32)],
        smem=(3,),
    )
    v, zones = lax.optimization_barrier((v, zones))
    rough = call(
        functools.partial(rough_kernel, parts, modes, padded, groups),
        [rimmed] * parts, [v, v_near, v_far], [grouped],
    )
    rough = exchange(rough)
    t_near, t_far = halo(temp)
    base = call(
        functools.partial(thermal_kernel, modes, padded, groups),
        struct(groups * padded, LANES), [temp, t_near, t_far],
    )
    wide = (per + 1) * LANES
    half_width = per * LANES // halves
    results = call(
        functools.partial(couple_kernel, parts, padded, per, nreg, halves),
        [struct(rows, half_width)] * halves + [struct(rows, LANES)] + [chunk] * parts,
        [*source, *rough, a_high, a_low, zones],
        [pltpu.VMEM((rows, wide), F32), pltpu.VMEM((rows, wide), F32)],
    )
    relaxed, rim, back = results[:halves], results[halves], list(results[halves + 1 :])
    beside = [halo(x) for x in relaxed]
    base, rim, back[2] = lax.optimization_barrier((base, rim, back[2]))
    back = exchange(back)
    part, spread = call(
        functools.partial(plane_kernel, nreg, halves),
        [struct(points, per * LANES)] * 2,
        [*relaxed, rim, zones, b_high, b_low, lift],
    )
    heat = []
    for half in range(halves):
        pieces = call(
            functools.partial(joule_kernel, parts, padded, per, halves, half),
            [struct(per // halves * padded, LANES)] * parts,
            [*beside[half], part, spread, avg, b_high, b_low, w_high, w_low],
            [pltpu.VMEM((rows, half_width), F32)],
        )
        heat += exchange(pieces)
    relaxed_voltage = call(
        functools.partial(gather_kernel, parts, modes, padded, per),
        struct(modes * groups, LANES), back,
    )
    advanced = call(
        functools.partial(final_kernel, parts, modes, padded, per, halves),
        struct(modes * groups, LANES), [*heat, base],
    )
    shape = voltage_expansion.shape
    return relaxed_voltage.reshape(shape), advanced.reshape(shape)


def solution(mesh):
    in_specs = (
        P("modes", "space", None),
        P("modes", "space", None),
        P("modes", "space", None),
        P("space", None),
        P("space", None),
        P(),
        P(),
        P(),
        P(),
    )
    out_specs = (P("modes", "space", None), P("modes", "space", None))
    return jax.shard_map(
        on_device, mesh=mesh, in_specs=in_specs, out_specs=out_specs, check_vma=False
    )
```

```python
import functools

import jax
import jax.numpy as jnp
from jax import lax
from jax.experimental import pallas as pl
from jax.experimental.pallas import tpu as pltpu
from jax.sharding import PartitionSpec as P

NZ = 8
LANES = 128
SUB = 8
TILE16 = 16
VMEM_LIMIT = 40 * 1024 * 1024

HERMITE_NODES = (
    0.0,
    1.355626179974266,
    -1.355626179974266,
    2.8569700138728056,
    -2.8569700138728056,
)

F32 = jnp.float32
BF16 = jnp.bfloat16


def split2(x):
    high = x.astype(BF16)
    return high, (x - high.astype(F32)).astype(BF16)


def dot(a, b):
    return jnp.dot(a, b, preferred_element_type=F32)


def dot_nt(a, b):
    return lax.dot_general(a, b, (((1,), (1,)), ((), ())), preferred_element_type=F32)


def dot3(a_high, a_low, b_high, b_low):
    return dot(a_high, b_high) + (dot(a_high, b_low) + dot(a_low, b_high))


def lane_ids(shape):
    return lax.broadcasted_iota(jnp.int32, shape, len(shape) - 1)


def target_of(swap, me, k, parts):
    if swap and parts & (parts - 1) == 0:
        return me ^ (swap(k, parts) if k else 0)
    return (me + k) % parts if isinstance(me, int) else lax.rem(me + k, parts)


def origin_of(swap, me, k, parts):
    if swap and parts & (parts - 1) == 0:
        return me ^ (swap(k, parts) if k else 0)
    return lax.rem(me + (parts - k), parts)


def upward(k, parts):
    return k


def downward(k, parts):
    return parts - k


W_SWAP, R_SWAP, B_SWAP, H_SWAP = None, upward, None, None


def load_group(ref, group, modes, groups):
    return ref[pl.ds(group, modes, stride=groups), :]


def pad_rows(x, rows):
    if x.shape[0] == rows:
        return x
    return jnp.concatenate([x, jnp.zeros((rows - x.shape[0], x.shape[1]), x.dtype)], axis=0)


def emit_slots(swap, me, parts, grouped, outs, padded):
    groups = grouped.shape[0] // padded
    per = groups // parts
    lane = lane_ids((padded, LANES))
    for k, out in enumerate(outs):
        q = target_of(swap, me, k, parts)
        start = pl.multiple_of(q * (per * padded), SUB)
        out[: per * padded, :] = grouped[pl.ds(start, per * padded), :]
        before = pl.multiple_of(jnp.maximum(q * per - 1, 0) * padded, SUB)
        after = pl.multiple_of(jnp.minimum(q * per + per, groups - 1) * padded, SUB)
        low = pltpu.roll(grouped[pl.ds(before, padded), :], NZ, 1)
        high = pltpu.roll(grouped[pl.ds(after, padded), :], NZ, 1)
        rim = jnp.where((lane < NZ) & (q > 0), low, 0.0)
        rim = jnp.where((lane >= NZ) & (lane < 2 * NZ) & (q < parts - 1), high, rim)
        packed = rim[:SUB]
        for tile in range(1, padded // SUB):
            packed = packed + pltpu.roll(rim[tile * SUB : (tile + 1) * SUB], 2 * NZ * tile, 1)
        out[per * padded :, :] = packed


def source_kernel(parts, modes, padded, v_hbm, j_hbm, a_hbm, *rest):
    outs, (grouped, v_ref, j_ref, a_ref, sems) = rest[:-5], rest[-5:]
    groups = a_ref.shape[0]
    starts = range(0, modes, SUB)
    pairs = [(a_hbm, a_ref)]
    for start in starts:
        rows = pl.ds(start * groups, min(SUB, modes - start) * groups)
        pairs += [(v_hbm.at[rows], v_ref.at[rows]), (j_hbm.at[rows], j_ref.at[rows])]
    copies = [pltpu.make_async_copy(x, y, sems.at[i]) for i, (x, y) in enumerate(pairs)]
    for copy in copies:
        copy.start()
    me = lax.axis_index("modes")
    copies[0].wait()
    factor = 0.8 / (6.0 * a_ref[...])
    for tile, start in enumerate(starts):
        copies[2 * tile + 1].wait()
        copies[2 * tile + 2].wait()
        count = min(SUB, modes - start)
        for g in range(groups):
            rows = pl.ds(start * groups + g, count, stride=groups)
            w = v_ref[rows, :] + j_ref[rows, :] * factor[g : g + 1]
            grouped[g * padded + start : g * padded + start + SUB, :] = pad_rows(w, SUB)
    emit_slots(W_SWAP, me, parts, grouped, outs, padded)


def stencil_groups(x_ref, near_ref, far_ref, modes, groups, padded, emit):
    lane = lane_ids((padded, LANES))
    depth = lane % NZ
    fields = [pad_rows(load_group(x_ref, g, modes, groups), padded) for g in range(groups)]
    for g in range(groups):
        x = fields[g]
        total = 6.0 * x - pad_rows(load_group(near_ref, g, modes, groups), padded)
        total = total - pad_rows(load_group(far_ref, g, modes, groups), padded)
        total = total - jnp.where(depth < NZ - 1, pltpu.roll(x, LANES - 1, 1), 0.0)
        total = total - jnp.where(depth > 0, pltpu.roll(x, 1, 1), 0.0)
        right = fields[g + 1] if g + 1 < groups else jnp.zeros_like(x)
        left = fields[g - 1] if g > 0 else jnp.zeros_like(x)
        total = total - pltpu.roll(jnp.where(lane < NZ, right, x), LANES - NZ, 1)
        total = total - pltpu.roll(jnp.where(lane >= LANES - NZ, left, x), NZ, 1)
        emit(g, x, total)


def rough_kernel(parts, modes, padded, groups, v_ref, near_ref, far_ref, *rest):
    outs, grouped = rest[:-1], rest[-1]
    me = lax.axis_index("modes")

    def emit(g, _, total):
        grouped[g * padded : (g + 1) * padded, :] = total

    stencil_groups(v_ref, near_ref, far_ref, modes, groups, padded, emit)
    emit_slots(R_SWAP, me, parts, grouped, outs, padded)


def thermal_kernel(modes, padded, groups, t_ref, near_ref, far_ref, out_ref):
    def emit(g, x, total):
        out_ref[g * padded : (g + 1) * padded, :] = x - 0.15 * total

    stencil_groups(t_ref, near_ref, far_ref, modes, groups, padded, emit)


def tables_kernel(
    parts, modes, padded, table_ref, nodes_ref, share_ref, z_ref, zone_ref,
    ah_ref, al_ref, bh_ref, bl_ref, wh_ref, wl_ref, lift_ref, zones_ref,
    cols, basis_t,
):
    nreg, npar = z_ref.shape
    all_modes = parts * modes
    rows = parts * padded
    points = nodes_ref.shape[1]
    me = lax.axis_index("modes")
    kinds = 4 * TILE16

    slot = lax.broadcasted_iota(jnp.int32, (rows, all_modes), 0)
    mode = lax.broadcasted_iota(jnp.int32, (rows, all_modes), 1)
    within = slot % padded
    pick = (within < modes) & (mode == slot // padded * modes + within)
    pick = jnp.where(pick, 1.0, 0.0).astype(BF16)
    table = table_ref[...].astype(F32).astype(BF16)
    spread = lax.broadcasted_iota(jnp.int32, (kinds, npar), 0) % TILE16
    spread = spread == lax.broadcasted_iota(jnp.int32, (kinds, npar), 1)
    table = dot(jnp.where(spread, 1.0, 0.0).astype(BF16), table).astype(BF16)
    along = dot_nt(table, pick)
    down = dot_nt(pick, table)
    cols[...] = down

    def one_hot(values, axis):
        kind = lax.broadcasted_iota(jnp.int32, values.shape, axis)
        row = lax.broadcasted_iota(jnp.int32, values.shape, 1 - axis)
        hit = (values == (kind // TILE16).astype(F32)) & (kind % TILE16 < npar)
        return jnp.where(hit & (row % padded < modes), 1.0, 0.0).astype(BF16)

    hot_down, hot_along = one_hot(down, 1), one_hot(along, 0)
    agree = dot(hot_down, hot_along)
    degree_down = jnp.sum(down[:, :TILE16], axis=1, keepdims=True)
    degree_along = jnp.sum(along[:TILE16], axis=0, keepdims=True)
    linked = (agree == npar - 1.0) & (jnp.abs(degree_down - degree_along) == 1.0)
    same = agree == float(npar)
    left = lax.broadcasted_iota(jnp.int32, (kinds, kinds), 0)
    right = lax.broadcasted_iota(jnp.int32, (kinds, kinds), 1)
    step = (left % TILE16 == right % TILE16) & (jnp.abs(left // TILE16 - right // TILE16) == 1)
    root = jnp.where(step, jnp.sqrt((jnp.maximum(left, right) // TILE16).astype(F32)), 0.0)
    param = lax.broadcasted_iota(jnp.int32, (1, kinds), 1) % TILE16
    hot3 = jnp.concatenate([hot_along] * 3, axis=0)
    matrices = []
    for r in range(nreg):
        weight = jnp.zeros((1, kinds), F32)
        for m in range(npar):
            weight = jnp.where(param == m, z_ref[r, m], weight)
        link = root * weight
        high = link.astype(BF16)
        mid = (link - high.astype(F32)).astype(BF16)
        low = (link - high.astype(F32) - mid.astype(F32)).astype(BF16)
        part = dot(hot_down, jnp.concatenate([high, mid, low], axis=1)).astype(BF16)
        matrices.append(jnp.where(linked, dot(part, hot3), jnp.where(same, 1.0, 0.0)))
    for source in range(parts):
        columns = slice(source * padded, (source + 1) * padded)
        high, low = split2(jnp.concatenate([x[:, columns] for x in matrices], axis=1))
        ah_ref[source] = high
        al_ref[source] = low

    nodes = nodes_ref[...]
    t = jnp.zeros(nodes.shape, F32)
    for which in range(1, len(HERMITE_NODES)):
        t = jnp.where(nodes == which, HERMITE_NODES[which], t)
    h2 = (t * t - 1.0) * (1.0 / 2.0**0.5)
    h3 = (t * t * t - 3.0 * t) * (1.0 / 6.0**0.5)
    share = share_ref[...].astype(F32) * (0.25 / (512.0 * points * all_modes))
    tiles = points // LANES

    def block(b, carry):
        at = pl.multiple_of(b * TILE16, TILE16)
        mine = cols[pl.ds(at, TILE16), :]
        row = lax.broadcasted_iota(jnp.int32, (TILE16, LANES), 0) + at
        basis = [jnp.where(row % padded < modes, 1.0, 0.0)] * tiles
        for m in range(npar):
            own = jnp.broadcast_to(mine[:, m : m + 1], (TILE16, LANES))
            is0, is1, is2 = own == 0.0, own == 1.0, own == 2.0
            for i in range(tiles):
                lanes = slice(i * LANES, (i + 1) * LANES)
                factor = jnp.where(is2, h2[m : m + 1, lanes], h3[m : m + 1, lanes])
                factor = jnp.where(is1, t[m : m + 1, lanes], factor)
                basis[i] = basis[i] * jnp.where(is0, 1.0, factor)
        for i in range(tiles):
            lanes = slice(i * LANES, (i + 1) * LANES)
            basis_t[pl.ds(at, TILE16), lanes] = basis[i]
            high, low = split2(basis[i] * share[:, lanes])
            wh_ref[pl.ds(at, TILE16), lanes] = high
            wl_ref[pl.ds(at, TILE16), lanes] = low
        return carry

    lax.fori_loop(0, rows // TILE16, block, 0)
    high, low = split2(basis_t[...].T)
    bh_ref[...] = high
    bl_ref[...] = low

    terms = []
    for r in range(nreg):
        lift = jnp.ones((1, points), F32)
        for m in range(npar):
            lift = lift + z_ref[r, m] * t[m : m + 1]
        terms.append(lift)
    lift = jnp.concatenate(terms, axis=0)
    high = lift.astype(BF16).astype(F32)
    mid = (lift - high).astype(BF16).astype(F32)
    low = lift - high - mid
    stacked = jnp.concatenate(
        [high, mid, low, jnp.zeros((LANES - 3 * nreg, points), F32)], axis=0
    )
    lift_ref[...] = stacked.T.astype(BF16)

    groups = zone_ref.shape[0]
    per = groups // parts
    zone = zone_ref[...]
    row = lax.broadcasted_iota(jnp.int32, zone.shape, 0)

    def pick_row(g):
        return jnp.sum(jnp.where(row == g, zone, 0), axis=0, keepdims=True)

    for s in range(per):
        zones_ref[:, s * LANES : (s + 1) * LANES] = pick_row(me * per + s)
    low = pltpu.roll(pick_row(jnp.maximum(me * per - 1, 0)), NZ, 1)
    high = pltpu.roll(pick_row(jnp.minimum(me * per + per, groups - 1)), NZ, 1)
    zones_ref[:, per * LANES :] = jnp.where(lane_ids(low.shape) < NZ, low, high)


def unpack(chunk, padded, per):
    packed = chunk[per * padded :, :]
    rims = [packed]
    for tile in range(1, padded // SUB):
        rims.append(pltpu.roll(packed, LANES - 2 * NZ * tile, 1))
    columns = [chunk[s * padded : (s + 1) * padded, :] for s in range(per)]
    return jnp.concatenate(columns + [jnp.concatenate(rims, axis=0)], axis=1)


def coupled(chunk, source, ah_ref, al_ref, zones, nreg, padded, per):
    field = unpack(chunk, padded, per)
    stacked = jnp.concatenate([jnp.where(zones == r, field, 0.0) for r in range(nreg)], axis=0)
    high, low = split2(stacked)
    return dot3(ah_ref[source], al_ref[source], high, low)


def couple_kernel(parts, padded, per, nreg, count, *refs):
    w_refs, r_refs = refs[:parts], refs[parts : parts + count]
    ah_ref, al_ref, zones_ref, out_ref = refs[parts + count :]
    me = lax.axis_index("modes")
    zones = zones_ref[...]
    applied = None
    for k in range(count):
        source = origin_of(R_SWAP, me, k, parts)
        part = coupled(r_refs[k], source, ah_ref, al_ref, zones, nreg, padded, per)
        applied = part if applied is None else applied + part
    for k in range(parts):
        at = pl.multiple_of(origin_of(W_SWAP, me, k, parts) * padded, SUB)
        out_ref[pl.ds(at, padded), :] = unpack(w_refs[k], padded, per)
    out_ref[...] = out_ref[...] - (0.8 / 6.0) * applied


def relax_kernel(parts, padded, per, nreg, count, *refs):
    r_refs = refs[: parts - count]
    most_ref, ah_ref, al_ref, zones_ref, rel_ref, rim_ref, *outs, all_ref = refs[parts - count :]
    me = lax.axis_index("modes")
    width = per * LANES
    zones = zones_ref[...]
    applied = None
    for k in range(count, parts):
        source = origin_of(R_SWAP, me, k, parts)
        part = coupled(r_refs[k - count], source, ah_ref, al_ref, zones, nreg, padded, per)
        applied = part if applied is None else applied + part
    relaxed = most_ref[...] - (0.8 / 6.0) * applied
    rel_ref[...] = relaxed[:, :width]
    rim_ref[...] = relaxed[:, width:]
    all_ref[...] = relaxed[:, :width]
    for k, out in enumerate(outs):
        at = pl.multiple_of(target_of(B_SWAP, me, k, parts) * padded, SUB)
        for s in range(per):
            out[s * padded : (s + 1) * padded, :] = all_ref[
                pl.ds(at, padded), s * LANES : (s + 1) * LANES
            ]


def plane_kernel(nreg, halves, *refs):
    rel_refs, (rim_ref, zones_ref, bh_ref, bl_ref, lift_ref, part_ref, spread_ref) = (
        refs[:halves], refs[halves:],
    )
    width = sum(ref.shape[1] for ref in rel_refs)
    rel = jnp.concatenate([ref[...] for ref in rel_refs], axis=1)
    rim = rim_ref[...]
    lane = lane_ids(rel.shape)
    depth = lane % NZ
    wide = jnp.concatenate([rim, jnp.zeros((rim.shape[0], width - LANES), F32)], axis=1)
    along_z = jnp.where(depth < NZ - 1, pltpu.roll(rel, width - 1, 1), 0.0)
    along_z = along_z - jnp.where(depth > 0, pltpu.roll(rel, 1, 1), 0.0)
    after = pltpu.roll(wide, width - 2 * NZ, 1)
    along_y = jnp.where(lane >= width - NZ, after, pltpu.roll(rel, width - NZ, 1))
    along_y = along_y - jnp.where(lane < NZ, wide, pltpu.roll(rel, NZ, 1))
    b_high, b_low = bh_ref[...], bl_ref[...]
    total = None
    for grad in (along_y, along_z):
        g_high, g_low = split2(grad)
        at_point = dot3(b_high, b_low, g_high, g_low)
        total = at_point * at_point if total is None else total + at_point * at_point
    row = lax.broadcasted_iota(jnp.int32, (LANES, width), 0)
    hot = (row < 3 * nreg) & (row % nreg == zones_ref[:, :width])
    spread = dot(lift_ref[...], jnp.where(hot, 1.0, 0.0).astype(BF16))
    spread_ref[...] = spread
    part_ref[...] = spread * total


def joule_kernel(
    parts, padded, per, halves, half, near_ref, far_ref, part_ref, spread_ref, a_ref,
    bh_ref, bl_ref, wh_ref, wl_ref, *rest,
):
    outs, heat_ref = rest[:-1], rest[-1]
    me = lax.axis_index("modes")
    own = per // halves
    lanes = slice(half * own * LANES, (half + 1) * own * LANES)
    g_high, g_low = split2(far_ref[...] - near_ref[...])
    at_point = dot3(bh_ref[...], bl_ref[...], g_high, g_low)
    joule = part_ref[:, lanes] + spread_ref[:, lanes] * (at_point * at_point)
    j_high, j_low = split2(joule)
    heat = dot3(wh_ref[...], wl_ref[...], j_high, j_low)
    for s in range(own):
        heat_ref[:, s * LANES : (s + 1) * LANES] = (
            heat[:, s * LANES : (s + 1) * LANES] * a_ref[pl.ds(me * per + half * own + s, 1), :]
        )
    for k, out in enumerate(outs):
        target = target_of(H_SWAP, me, k, parts)
        at = pl.multiple_of(target * padded, SUB)
        for s in range(own):
            out[s * padded : (s + 1) * padded, :] = heat_ref[
                pl.ds(at, padded), s * LANES : (s + 1) * LANES
            ]


def flat_tiles(modes, groups, write, out_hbm, buffer, sems):
    copies = []
    for tile, start in enumerate(range(0, modes, SUB)):
        count = min(SUB, modes - start)
        write(start, count)
        rows = pl.ds(start * groups, count * groups)
        copy = pltpu.make_async_copy(buffer.at[rows], out_hbm.at[rows], sems.at[tile])
        copy.start()
        copies.append(copy)
    for copy in copies:
        copy.wait()


def gather_kernel(parts, modes, padded, per, *refs):
    chunks, (out_hbm, buffer, sems) = refs[:parts], refs[parts:]
    me = lax.axis_index("modes")
    groups = parts * per

    def write(start, count):
        for k in range(parts):
            q = origin_of(B_SWAP, me, k, parts)
            for s in range(per):
                at = pl.ds(start * groups + q * per + s, count, stride=groups)
                buffer[at, :] = chunks[k][s * padded + start : s * padded + start + count, :]

    flat_tiles(modes, groups, write, out_hbm, buffer, sems)


def final_kernel(parts, modes, padded, per, *refs):
    chunks, (base, out_hbm, buffer, sems) = refs[:parts], refs[parts:]
    me = lax.axis_index("modes")
    groups = parts * per

    def write(start, count):
        for k in range(parts):
            q = origin_of(H_SWAP, me, k, parts)
            for s in range(per):
                at = pl.multiple_of((q * per + s) * padded + start, SUB)
                within = s * padded + start
                rows = base[pl.ds(at, SUB), :] + 0.1 * chunks[k][within : within + SUB, :]
                buffer[pl.ds(start * groups + q * per + s, count, stride=groups), :] = rows[:count]

    flat_tiles(modes, groups, write, out_hbm, buffer, sems)


def call(kernel, out_shape, args, scratch=(), smem=(), hbm=(), limit=VMEM_LIMIT, out_hbm=False):
    specs = [
        pl.BlockSpec(
            memory_space=pltpu.SMEM if i in smem else pltpu.HBM if i in hbm else pltpu.VMEM
        )
        for i in range(len(args))
    ]
    many = isinstance(out_shape, (list, tuple))
    where = pl.BlockSpec(memory_space=pltpu.HBM if out_hbm else pltpu.VMEM)
    nbytes = sum(x.size * x.dtype.itemsize for x in args)
    return pl.pallas_call(
        kernel,
        out_shape=out_shape,
        in_specs=specs,
        out_specs=[where] * len(out_shape) if many else where,
        scratch_shapes=list(scratch),
        compiler_params=pltpu.CompilerParams(vmem_limit_bytes=limit),
        cost_estimate=pl.CostEstimate(flops=0, bytes_accessed=nbytes, transcendentals=0),
    )(*args)


def exchange(chunks, swap):
    parts = lax.axis_size("modes")
    received = list(chunks)
    for k in range(1, parts):
        pairs = [(i, target_of(swap, i, k, parts)) for i in range(parts)]
        received[k] = lax.ppermute(chunks[k], "modes", pairs)
    return received


def halo(x):
    count = lax.axis_size("space")
    near = [(i, i ^ 1) for i in range(count) if i ^ 1 < count]
    far = [(i, ((i - 1) ^ 1) + 1) for i in range(1, count) if ((i - 1) ^ 1) + 1 < count]
    far = lax.ppermute(x, "space", far)
    return lax.ppermute(x, "space", near), far


def on_device(
    voltage_expansion,
    current_injection,
    thermal_state,
    average_electric_transport,
    material_zone,
    zone_relative_response,
    polynomial_exponent_rows,
    quadrature_abscissa_choice,
    quadrature_integer_share,
):
    parts = lax.axis_size("modes")
    modes, planes, columns = voltage_expansion.shape
    nreg = zone_relative_response.shape[0]
    points = quadrature_integer_share.shape[0]
    groups = columns // LANES
    per = groups // parts
    padded = -(-modes // SUB) * SUB
    halves = 1
    rows = parts * padded
    assert planes == 1 and groups * LANES == columns and per * parts == groups
    assert polynomial_exponent_rows.shape[1] <= TILE16 and points % LANES == 0
    assert rows % TILE16 == 0 and 2 * NZ * padded <= SUB * LANES and 3 * nreg <= LANES

    def flat(x):
        return x.reshape(modes * groups, LANES)

    def struct(*shape, dtype=F32):
        return jax.ShapeDtypeStruct(shape, dtype)

    v, cur, temp = flat(voltage_expansion), flat(current_injection), flat(thermal_state)
    avg = average_electric_transport.reshape(groups, LANES)
    zone = material_zone.reshape(groups, LANES)
    rimmed = struct(per * padded + SUB, LANES)
    grouped = pltpu.VMEM((groups * padded, LANES), F32)

    fields = pltpu.VMEM((modes * groups, LANES), F32)
    v_near, v_far = halo(v)
    source = call(
        functools.partial(source_kernel, parts, modes, padded),
        [rimmed] * parts,
        [v, cur, avg],
        [grouped, fields, fields, pltpu.VMEM((groups, LANES), F32), pltpu.SemaphoreType.DMA((1 + 2 * (padded // SUB),))],
        hbm=(0, 1, 2),
        limit=62 * 1024 * 1024,
    )
    source = exchange(source, W_SWAP)
    temp, source[1] = lax.optimization_barrier((temp, source[1]))
    a_high, a_low, b_high, b_low, w_high, w_low, lift, zones = call(
        functools.partial(tables_kernel, parts, modes, padded),
        [
            struct(parts, rows, nreg * padded, dtype=BF16),
            struct(parts, rows, nreg * padded, dtype=BF16),
            struct(points, rows, dtype=BF16),
            struct(points, rows, dtype=BF16),
            struct(rows, points, dtype=BF16),
            struct(rows, points, dtype=BF16),
            struct(points, LANES, dtype=BF16),
            struct(1, (per + 1) * LANES, dtype=jnp.int32),
        ],
        [
            polynomial_exponent_rows.T,
            quadrature_abscissa_choice.T,
            quadrature_integer_share.reshape(1, points),
            zone_relative_response,
            zone,
        ],
        [pltpu.VMEM((rows, 4 * TILE16), F32), pltpu.VMEM((rows, points), F32)],
        smem=(3,),
    )
    v, zones = lax.optimization_barrier((v, zones))
    rough = call(
        functools.partial(rough_kernel, parts, modes, padded, groups),
        [rimmed] * parts, [v, v_near, v_far], [grouped],
    )
    rough = exchange(rough, R_SWAP)
    t_near, t_far = halo(temp)
    base = call(
        functools.partial(thermal_kernel, modes, padded, groups),
        struct(groups * padded, LANES), [temp, t_near, t_far],
    )
    wide = (per + 1) * LANES
    count = parts - 1
    most = call(
        functools.partial(couple_kernel, parts, padded, per, nreg, count),
        struct(rows, wide), [*source, *rough[:count], a_high, a_low, zones],
    )
    relaxed, rim, *back = call(
        functools.partial(relax_kernel, parts, padded, per, nreg, count),
        [struct(rows, per * LANES), struct(rows, LANES)]
        + [struct(per * padded, LANES)] * parts,
        [*rough[count:], most, a_high, a_low, zones],
        [pltpu.VMEM((rows, per * LANES), F32)],
    )
    relaxed = [relaxed]
    beside = [halo(x) for x in relaxed]
    base, back[2] = lax.optimization_barrier((base, back[2]))
    back = exchange(back, B_SWAP)
    part, spread = call(
        functools.partial(plane_kernel, nreg, halves),
        [struct(points, per * LANES)] * 2,
        [*relaxed, rim, zones, b_high, b_low, lift],
    )
    heat = []
    for half in range(halves):
        pieces = call(
            functools.partial(joule_kernel, parts, padded, per, halves, half),
            [struct(per // halves * padded, LANES)] * parts,
            [*beside[half], part, spread, avg, b_high, b_low, w_high, w_low],
            [pltpu.VMEM((rows, per * LANES // halves), F32)],
        )
        heat += exchange(pieces, H_SWAP)
    tiled = [fields, pltpu.SemaphoreType.DMA((padded // SUB,))]
    relaxed_voltage = call(
        functools.partial(gather_kernel, parts, modes, padded, per),
        struct(modes * groups, LANES), back, tiled, out_hbm=True,
    )
    advanced = call(
        functools.partial(final_kernel, parts, modes, padded, per),
        struct(modes * groups, LANES), [*heat, base], tiled, out_hbm=True,
    )
    shape = voltage_expansion.shape
    return relaxed_voltage.reshape(shape), advanced.reshape(shape)


def solution(mesh):
    in_specs = (
        P("modes", "space", None),
        P("modes", "space", None),
        P("modes", "space", None),
        P("space", None),
        P("space", None),
        P(),
        P(),
        P(),
        P(),
    )
    out_specs = (P("modes", "space", None), P("modes", "space", None))
    return jax.shard_map(
        on_device, mesh=mesh, in_specs=in_specs, out_specs=out_specs, check_vma=False
    )
```

```python
import functools

import jax
import jax.numpy as jnp
from jax import lax
from jax.experimental import pallas as pl
from jax.experimental.pallas import tpu as pltpu
from jax.sharding import PartitionSpec as P

NZ = 8
LANES = 128
SUB = 8
TILE16 = 16
VMEM_LIMIT = 40 * 1024 * 1024

HERMITE_NODES = (
    0.0,
    1.355626179974266,
    -1.355626179974266,
    2.8569700138728056,
    -2.8569700138728056,
)

F32 = jnp.float32
BF16 = jnp.bfloat16


def split2(x):
    high = x.astype(BF16)
    return high, (x - high.astype(F32)).astype(BF16)


def dot(a, b):
    return jnp.dot(a, b, preferred_element_type=F32)


def dot_nt(a, b):
    return lax.dot_general(a, b, (((1,), (1,)), ((), ())), preferred_element_type=F32)


def dot3(a_high, a_low, b_high, b_low):
    return dot(a_high, b_high) + (dot(a_high, b_low) + dot(a_low, b_high))


def lane_ids(shape):
    return lax.broadcasted_iota(jnp.int32, shape, len(shape) - 1)


def target_of(swap, me, k, parts):
    if swap and parts & (parts - 1) == 0:
        return me ^ (swap(k, parts) if k else 0)
    return (me + k) % parts if isinstance(me, int) else lax.rem(me + k, parts)


def origin_of(swap, me, k, parts):
    if swap and parts & (parts - 1) == 0:
        return me ^ (swap(k, parts) if k else 0)
    return lax.rem(me + (parts - k), parts)


def upward(k, parts):
    return k


def downward(k, parts):
    return parts - k


W_SWAP, R_SWAP, B_SWAP, H_SWAP = None, upward, None, None


def load_group(ref, group, modes, groups):
    spare = modes % SUB
    main = modes - spare
    if not spare:
        return ref[pl.ds(group, modes, stride=groups), :]
    last = ref[pl.ds((modes - SUB) * groups + group, SUB, stride=groups), :]
    row = lax.broadcasted_iota(jnp.int32, last.shape, 0)
    last = jnp.where(row < spare, pltpu.roll(last, spare, 0), 0.0)
    return jnp.concatenate([ref[pl.ds(group, main, stride=groups), :], last], axis=0)


def emit_slots(swap, me, parts, grouped, outs, padded):
    groups = grouped.shape[0] // padded
    per = groups // parts
    lane = lane_ids((padded, LANES))
    for k, out in enumerate(outs):
        q = target_of(swap, me, k, parts)
        start = pl.multiple_of(q * (per * padded), SUB)
        out[: per * padded, :] = grouped[pl.ds(start, per * padded), :]
        before = pl.multiple_of(jnp.maximum(q * per - 1, 0) * padded, SUB)
        after = pl.multiple_of(jnp.minimum(q * per + per, groups - 1) * padded, SUB)
        low = pltpu.roll(grouped[pl.ds(before, padded), :], NZ, 1)
        high = pltpu.roll(grouped[pl.ds(after, padded), :], NZ, 1)
        rim = jnp.where((lane < NZ) & (q > 0), low, 0.0)
        rim = jnp.where((lane >= NZ) & (lane < 2 * NZ) & (q < parts - 1), high, rim)
        packed = rim[:SUB]
        for tile in range(1, padded // SUB):
            packed = packed + pltpu.roll(rim[tile * SUB : (tile + 1) * SUB], 2 * NZ * tile, 1)
        out[per * padded :, :] = packed


def source_kernel(parts, modes, padded, v_hbm, j_hbm, a_hbm, *rest):
    outs, (grouped, v_ref, j_ref, a_ref, sems) = rest[:-5], rest[-5:]
    groups = a_ref.shape[0]
    starts = range(0, modes, SUB)
    pairs = [(a_hbm, a_ref)]
    for start in starts:
        rows = pl.ds(start * groups, min(SUB, modes - start) * groups)
        pairs += [(v_hbm.at[rows], v_ref.at[rows]), (j_hbm.at[rows], j_ref.at[rows])]
    copies = [pltpu.make_async_copy(x, y, sems.at[i]) for i, (x, y) in enumerate(pairs)]
    for copy in copies:
        copy.start()
    me = lax.axis_index("modes")
    row = lax.broadcasted_iota(jnp.int32, (SUB, LANES), 0)
    copies[0].wait()
    factor = 0.8 / (6.0 * a_ref[...])
    for tile, start in enumerate(starts):
        copies[2 * tile + 1].wait()
        copies[2 * tile + 2].wait()
        count = min(SUB, modes - start)
        for g in range(groups):
            rows = pl.ds(start * groups + g, SUB, stride=groups)
            w = v_ref[rows, :] + j_ref[rows, :] * factor[g : g + 1]
            if count < SUB:
                w = jnp.where(row < count, w, 0.0)
            grouped[g * padded + start : g * padded + start + SUB, :] = w
    emit_slots(W_SWAP, me, parts, grouped, outs, padded)


def stencil_groups(x_ref, near_ref, far_ref, modes, groups, padded, emit):
    lane = lane_ids((padded, LANES))
    depth = lane % NZ
    fields = [load_group(x_ref, g, modes, groups) for g in range(groups)]
    for g in range(groups):
        x = fields[g]
        total = 6.0 * x - load_group(near_ref, g, modes, groups)
        total = total - load_group(far_ref, g, modes, groups)
        total = total - jnp.where(depth < NZ - 1, pltpu.roll(x, LANES - 1, 1), 0.0)
        total = total - jnp.where(depth > 0, pltpu.roll(x, 1, 1), 0.0)
        right = fields[g + 1] if g + 1 < groups else jnp.zeros_like(x)
        left = fields[g - 1] if g > 0 else jnp.zeros_like(x)
        total = total - pltpu.roll(jnp.where(lane < NZ, right, x), LANES - NZ, 1)
        total = total - pltpu.roll(jnp.where(lane >= LANES - NZ, left, x), NZ, 1)
        emit(g, x, total)


def rough_kernel(parts, modes, padded, groups, v_ref, near_ref, far_ref, *rest):
    outs, grouped = rest[:-1], rest[-1]
    me = lax.axis_index("modes")

    def emit(g, _, total):
        grouped[g * padded : (g + 1) * padded, :] = total

    stencil_groups(v_ref, near_ref, far_ref, modes, groups, padded, emit)
    emit_slots(R_SWAP, me, parts, grouped, outs, padded)


def thermal_kernel(modes, padded, groups, t_ref, near_ref, far_ref, out_ref):
    def emit(g, x, total):
        out_ref[g * padded : (g + 1) * padded, :] = x - 0.15 * total

    stencil_groups(t_ref, near_ref, far_ref, modes, groups, padded, emit)


def tables_kernel(
    parts, modes, padded, table_ref, nodes_ref, share_ref, z_ref, zone_ref,
    ah_ref, al_ref, bh_ref, bl_ref, wh_ref, wl_ref, lift_ref, zones_ref,
    cols, basis_t,
):
    nreg, npar = z_ref.shape
    all_modes = parts * modes
    rows = parts * padded
    points = nodes_ref.shape[1]
    me = lax.axis_index("modes")
    kinds = 4 * TILE16

    slot = lax.broadcasted_iota(jnp.int32, (rows, all_modes), 0)
    mode = lax.broadcasted_iota(jnp.int32, (rows, all_modes), 1)
    within = slot % padded
    pick = (within < modes) & (mode == slot // padded * modes + within)
    pick = jnp.where(pick, 1.0, 0.0).astype(BF16)
    table = table_ref[...].astype(F32).astype(BF16)
    spread = lax.broadcasted_iota(jnp.int32, (kinds, npar), 0) % TILE16
    spread = spread == lax.broadcasted_iota(jnp.int32, (kinds, npar), 1)
    table = dot(jnp.where(spread, 1.0, 0.0).astype(BF16), table).astype(BF16)
    along = dot_nt(table, pick)
    down = dot_nt(pick, table)
    cols[...] = down

    def one_hot(values, axis):
        kind = lax.broadcasted_iota(jnp.int32, values.shape, axis)
        row = lax.broadcasted_iota(jnp.int32, values.shape, 1 - axis)
        hit = (values == (kind // TILE16).astype(F32)) & (kind % TILE16 < npar)
        return jnp.where(hit & (row % padded < modes), 1.0, 0.0).astype(BF16)

    hot_down, hot_along = one_hot(down, 1), one_hot(along, 0)
    agree = dot(hot_down, hot_along)
    degree_down = jnp.sum(down[:, :TILE16], axis=1, keepdims=True)
    degree_along = jnp.sum(along[:TILE16], axis=0, keepdims=True)
    linked = (agree == npar - 1.0) & (jnp.abs(degree_down - degree_along) == 1.0)
    same = agree == float(npar)
    left = lax.broadcasted_iota(jnp.int32, (kinds, kinds), 0)
    right = lax.broadcasted_iota(jnp.int32, (kinds, kinds), 1)
    step = (left % TILE16 == right % TILE16) & (jnp.abs(left // TILE16 - right // TILE16) == 1)
    root = jnp.where(step, jnp.sqrt((jnp.maximum(left, right) // TILE16).astype(F32)), 0.0)
    param = lax.broadcasted_iota(jnp.int32, (1, kinds), 1) % TILE16
    hot3 = jnp.concatenate([hot_along] * 3, axis=0)
    matrices = []
    for r in range(nreg):
        weight = jnp.zeros((1, kinds), F32)
        for m in range(npar):
            weight = jnp.where(param == m, z_ref[r, m], weight)
        link = root * weight
        high = link.astype(BF16)
        mid = (link - high.astype(F32)).astype(BF16)
        low = (link - high.astype(F32) - mid.astype(F32)).astype(BF16)
        part = dot(hot_down, jnp.concatenate([high, mid, low], axis=1)).astype(BF16)
        matrices.append(jnp.where(linked, dot(part, hot3), jnp.where(same, 1.0, 0.0)))
    for source in range(parts):
        columns = slice(source * padded, (source + 1) * padded)
        high, low = split2(jnp.concatenate([x[:, columns] for x in matrices], axis=1))
        ah_ref[source] = high
        al_ref[source] = low

    nodes = nodes_ref[...]
    t = jnp.zeros(nodes.shape, F32)
    for which in range(1, len(HERMITE_NODES)):
        t = jnp.where(nodes == which, HERMITE_NODES[which], t)
    h2 = (t * t - 1.0) * (1.0 / 2.0**0.5)
    h3 = (t * t * t - 3.0 * t) * (1.0 / 6.0**0.5)
    share = share_ref[...].astype(F32) * (0.25 / (512.0 * points * all_modes))
    tiles = points // LANES

    def block(b, carry):
        at = pl.multiple_of(b * TILE16, TILE16)
        mine = cols[pl.ds(at, TILE16), :]
        row = lax.broadcasted_iota(jnp.int32, (TILE16, LANES), 0) + at
        basis = [jnp.where(row % padded < modes, 1.0, 0.0)] * tiles
        for m in range(npar):
            own = jnp.broadcast_to(mine[:, m : m + 1], (TILE16, LANES))
            is0, is1, is2 = own == 0.0, own == 1.0, own == 2.0
            for i in range(tiles):
                lanes = slice(i * LANES, (i + 1) * LANES)
                factor = jnp.where(is2, h2[m : m + 1, lanes], h3[m : m + 1, lanes])
                factor = jnp.where(is1, t[m : m + 1, lanes], factor)
                basis[i] = basis[i] * jnp.where(is0, 1.0, factor)
        for i in range(tiles):
            lanes = slice(i * LANES, (i + 1) * LANES)
            basis_t[pl.ds(at, TILE16), lanes] = basis[i]
            high, low = split2(basis[i] * share[:, lanes])
            wh_ref[pl.ds(at, TILE16), lanes] = high
            wl_ref[pl.ds(at, TILE16), lanes] = low
        return carry

    lax.fori_loop(0, rows // TILE16, block, 0)
    high, low = split2(basis_t[...].T)
    bh_ref[...] = high
    bl_ref[...] = low

    terms = []
    for r in range(nreg):
        lift = jnp.ones((1, points), F32)
        for m in range(npar):
            lift = lift + z_ref[r, m] * t[m : m + 1]
        terms.append(lift)
    lift = jnp.concatenate(terms, axis=0)
    high = lift.astype(BF16).astype(F32)
    mid = (lift - high).astype(BF16).astype(F32)
    low = lift - high - mid
    stacked = jnp.concatenate(
        [high, mid, low, jnp.zeros((LANES - 3 * nreg, points), F32)], axis=0
    )
    lift_ref[...] = stacked.T.astype(BF16)

    groups = zone_ref.shape[0]
    per = groups // parts
    zone = zone_ref[...]
    row = lax.broadcasted_iota(jnp.int32, zone.shape, 0)

    def pick_row(g):
        return jnp.sum(jnp.where(row == g, zone, 0), axis=0, keepdims=True)

    for s in range(per):
        zones_ref[:, s * LANES : (s + 1) * LANES] = pick_row(me * per + s)
    low = pltpu.roll(pick_row(jnp.maximum(me * per - 1, 0)), NZ, 1)
    high = pltpu.roll(pick_row(jnp.minimum(me * per + per, groups - 1)), NZ, 1)
    zones_ref[:, per * LANES :] = jnp.where(lane_ids(low.shape) < NZ, low, high)


def unpack(chunk, padded, per):
    packed = chunk[per * padded :, :]
    rims = [packed]
    for tile in range(1, padded // SUB):
        rims.append(pltpu.roll(packed, LANES - 2 * NZ * tile, 1))
    columns = [chunk[s * padded : (s + 1) * padded, :] for s in range(per)]
    return jnp.concatenate(columns + [jnp.concatenate(rims, axis=0)], axis=1)


def coupled(chunk, source, ah_ref, al_ref, zones, nreg, padded, per):
    field = unpack(chunk, padded, per)
    stacked = jnp.concatenate([jnp.where(zones == r, field, 0.0) for r in range(nreg)], axis=0)
    high, low = split2(stacked)
    return dot3(ah_ref[source], al_ref[source], high, low)


def couple_kernel(parts, padded, per, nreg, count, *refs):
    w_refs, r_refs = refs[:parts], refs[parts : parts + count]
    ah_ref, al_ref, zones_ref, out_ref = refs[parts + count :]
    me = lax.axis_index("modes")
    zones = zones_ref[...]
    applied = None
    for k in range(count):
        source = origin_of(R_SWAP, me, k, parts)
        part = coupled(r_refs[k], source, ah_ref, al_ref, zones, nreg, padded, per)
        applied = part if applied is None else applied + part
    for k in range(parts):
        at = pl.multiple_of(origin_of(W_SWAP, me, k, parts) * padded, SUB)
        out_ref[pl.ds(at, padded), :] = unpack(w_refs[k], padded, per)
    out_ref[...] = out_ref[...] - (0.8 / 6.0) * applied


def relax_kernel(parts, padded, per, nreg, count, *refs):
    r_refs = refs[: parts - count]
    most_ref, ah_ref, al_ref, zones_ref, rel_ref, rim_ref, *outs, all_ref = refs[parts - count :]
    me = lax.axis_index("modes")
    width = per * LANES
    zones = zones_ref[...]
    applied = None
    for k in range(count, parts):
        source = origin_of(R_SWAP, me, k, parts)
        part = coupled(r_refs[k - count], source, ah_ref, al_ref, zones, nreg, padded, per)
        applied = part if applied is None else applied + part
    relaxed = most_ref[...] - (0.8 / 6.0) * applied
    rel_ref[...] = relaxed[:, :width]
    rim_ref[...] = relaxed[:, width:]
    all_ref[...] = relaxed[:, :width]
    for k, out in enumerate(outs):
        at = pl.multiple_of(target_of(B_SWAP, me, k, parts) * padded, SUB)
        for s in range(per):
            out[s * padded : (s + 1) * padded, :] = all_ref[
                pl.ds(at, padded), s * LANES : (s + 1) * LANES
            ]


def plane_kernel(nreg, halves, *refs):
    rel_refs, (rim_ref, zones_ref, bh_ref, bl_ref, lift_ref, part_ref, spread_ref) = (
        refs[:halves], refs[halves:],
    )
    width = sum(ref.shape[1] for ref in rel_refs)
    rel = jnp.concatenate([ref[...] for ref in rel_refs], axis=1)
    rim = rim_ref[...]
    lane = lane_ids(rel.shape)
    depth = lane % NZ
    wide = jnp.concatenate([rim, jnp.zeros((rim.shape[0], width - LANES), F32)], axis=1)
    along_z = jnp.where(depth < NZ - 1, pltpu.roll(rel, width - 1, 1), 0.0)
    along_z = along_z - jnp.where(depth > 0, pltpu.roll(rel, 1, 1), 0.0)
    after = pltpu.roll(wide, width - 2 * NZ, 1)
    along_y = jnp.where(lane >= width - NZ, after, pltpu.roll(rel, width - NZ, 1))
    along_y = along_y - jnp.where(lane < NZ, wide, pltpu.roll(rel, NZ, 1))
    b_high, b_low = bh_ref[...], bl_ref[...]
    total = None
    for grad in (along_y, along_z):
        g_high, g_low = split2(grad)
        at_point = dot3(b_high, b_low, g_high, g_low)
        total = at_point * at_point if total is None else total + at_point * at_point
    row = lax.broadcasted_iota(jnp.int32, (LANES, width), 0)
    hot = (row < 3 * nreg) & (row % nreg == zones_ref[:, :width])
    spread = dot(lift_ref[...], jnp.where(hot, 1.0, 0.0).astype(BF16))
    spread_ref[...] = spread
    part_ref[...] = spread * total


def joule_kernel(
    parts, padded, per, halves, half, near_ref, far_ref, part_ref, spread_ref, a_ref,
    bh_ref, bl_ref, wh_ref, wl_ref, *rest,
):
    outs, heat_ref = rest[:-1], rest[-1]
    me = lax.axis_index("modes")
    own = per // halves
    lanes = slice(half * own * LANES, (half + 1) * own * LANES)
    g_high, g_low = split2(far_ref[...] - near_ref[...])
    at_point = dot3(bh_ref[...], bl_ref[...], g_high, g_low)
    joule = part_ref[:, lanes] + spread_ref[:, lanes] * (at_point * at_point)
    j_high, j_low = split2(joule)
    heat = dot3(wh_ref[...], wl_ref[...], j_high, j_low)
    for s in range(own):
        heat_ref[:, s * LANES : (s + 1) * LANES] = (
            heat[:, s * LANES : (s + 1) * LANES] * a_ref[pl.ds(me * per + half * own + s, 1), :]
        )
    for k, out in enumerate(outs):
        target = target_of(H_SWAP, me, k, parts)
        at = pl.multiple_of(target * padded, SUB)
        for s in range(own):
            out[s * padded : (s + 1) * padded, :] = heat_ref[
                pl.ds(at, padded), s * LANES : (s + 1) * LANES
            ]


def flat_tiles(modes, groups, write, out_hbm, buffer, sems):
    copies = []
    for tile, start in enumerate(range(0, modes, SUB)):
        count = min(SUB, modes - start)
        write(start)
        rows = pl.ds(start * groups, count * groups)
        copy = pltpu.make_async_copy(buffer.at[rows], out_hbm.at[rows], sems.at[tile])
        copy.start()
        copies.append(copy)
    for copy in copies:
        copy.wait()


def gather_kernel(parts, modes, padded, per, *refs):
    chunks, (out_hbm, buffer, sems) = refs[:parts], refs[parts:]
    me = lax.axis_index("modes")
    groups = parts * per

    def write(start):
        for k in range(parts):
            q = origin_of(B_SWAP, me, k, parts)
            for s in range(per):
                at = pl.ds(start * groups + q * per + s, SUB, stride=groups)
                buffer[at, :] = chunks[k][s * padded + start : s * padded + start + SUB, :]

    flat_tiles(modes, groups, write, out_hbm, buffer, sems)


def final_kernel(parts, modes, padded, per, *refs):
    chunks, (base, out_hbm, buffer, sems) = refs[:parts], refs[parts:]
    me = lax.axis_index("modes")
    groups = parts * per

    def write(start):
        for k in range(parts):
            q = origin_of(H_SWAP, me, k, parts)
            for s in range(per):
                at = pl.multiple_of((q * per + s) * padded + start, SUB)
                within = s * padded + start
                rows = base[pl.ds(at, SUB), :] + 0.1 * chunks[k][within : within + SUB, :]
                buffer[pl.ds(start * groups + q * per + s, SUB, stride=groups), :] = rows

    flat_tiles(modes, groups, write, out_hbm, buffer, sems)


def call(kernel, out_shape, args, scratch=(), smem=(), hbm=(), limit=VMEM_LIMIT, out_hbm=False):
    specs = [
        pl.BlockSpec(
            memory_space=pltpu.SMEM if i in smem else pltpu.HBM if i in hbm else pltpu.VMEM
        )
        for i in range(len(args))
    ]
    many = isinstance(out_shape, (list, tuple))
    where = pl.BlockSpec(memory_space=pltpu.HBM if out_hbm else pltpu.VMEM)
    nbytes = sum(x.size * x.dtype.itemsize for x in args)
    return pl.pallas_call(
        kernel,
        out_shape=out_shape,
        in_specs=specs,
        out_specs=[where] * len(out_shape) if many else where,
        scratch_shapes=list(scratch),
        compiler_params=pltpu.CompilerParams(vmem_limit_bytes=limit),
        cost_estimate=pl.CostEstimate(flops=0, bytes_accessed=nbytes, transcendentals=0),
    )(*args)


def exchange(chunks, swap):
    parts = lax.axis_size("modes")
    received = list(chunks)
    for k in range(1, parts):
        pairs = [(i, target_of(swap, i, k, parts)) for i in range(parts)]
        received[k] = lax.ppermute(chunks[k], "modes", pairs)
    return received


def halo(x):
    count = lax.axis_size("space")
    near = [(i, i ^ 1) for i in range(count) if i ^ 1 < count]
    far = [(i, ((i - 1) ^ 1) + 1) for i in range(1, count) if ((i - 1) ^ 1) + 1 < count]
    far = lax.ppermute(x, "space", far)
    return lax.ppermute(x, "space", near), far


def on_device(
    voltage_expansion,
    current_injection,
    thermal_state,
    average_electric_transport,
    material_zone,
    zone_relative_response,
    polynomial_exponent_rows,
    quadrature_abscissa_choice,
    quadrature_integer_share,
):
    parts = lax.axis_size("modes")
    modes, planes, columns = voltage_expansion.shape
    nreg = zone_relative_response.shape[0]
    points = quadrature_integer_share.shape[0]
    groups = columns // LANES
    per = groups // parts
    padded = -(-modes // SUB) * SUB
    halves = 1
    rows = parts * padded
    assert modes > SUB and planes == 1 and groups * LANES == columns and per * parts == groups
    assert polynomial_exponent_rows.shape[1] <= TILE16 and points % LANES == 0
    assert rows % TILE16 == 0 and 2 * NZ * padded <= SUB * LANES and 3 * nreg <= LANES

    def flat(x):
        return x.reshape(modes * groups, LANES)

    def struct(*shape, dtype=F32):
        return jax.ShapeDtypeStruct(shape, dtype)

    v, cur, temp = flat(voltage_expansion), flat(current_injection), flat(thermal_state)
    avg = average_electric_transport.reshape(groups, LANES)
    zone = material_zone.reshape(groups, LANES)
    rimmed = struct(per * padded + SUB, LANES)
    grouped = pltpu.VMEM((groups * padded, LANES), F32)

    fields = pltpu.VMEM((padded * groups, LANES), F32)
    v_near, v_far = halo(v)
    source = call(
        functools.partial(source_kernel, parts, modes, padded),
        [rimmed] * parts,
        [v, cur, avg],
        [grouped, fields, fields, pltpu.VMEM((groups, LANES), F32), pltpu.SemaphoreType.DMA((1 + 2 * (padded // SUB),))],
        hbm=(0, 1, 2),
        limit=62 * 1024 * 1024,
    )
    source = exchange(source, W_SWAP)
    temp, source[1] = lax.optimization_barrier((temp, source[1]))
    a_high, a_low, b_high, b_low, w_high, w_low, lift, zones = call(
        functools.partial(tables_kernel, parts, modes, padded),
        [
            struct(parts, rows, nreg * padded, dtype=BF16),
            struct(parts, rows, nreg * padded, dtype=BF16),
            struct(points, rows, dtype=BF16),
            struct(points, rows, dtype=BF16),
            struct(rows, points, dtype=BF16),
            struct(rows, points, dtype=BF16),
            struct(points, LANES, dtype=BF16),
            struct(1, (per + 1) * LANES, dtype=jnp.int32),
        ],
        [
            polynomial_exponent_rows.T,
            quadrature_abscissa_choice.T,
            quadrature_integer_share.reshape(1, points),
            zone_relative_response,
            zone,
        ],
        [pltpu.VMEM((rows, 4 * TILE16), F32), pltpu.VMEM((rows, points), F32)],
        smem=(3,),
    )
    v, zones = lax.optimization_barrier((v, zones))
    rough = call(
        functools.partial(rough_kernel, parts, modes, padded, groups),
        [rimmed] * parts, [v, v_near, v_far], [grouped],
    )
    rough = exchange(rough, R_SWAP)
    t_near, t_far = halo(temp)
    base = call(
        functools.partial(thermal_kernel, modes, padded, groups),
        struct(groups * padded, LANES), [temp, t_near, t_far],
    )
    wide = (per + 1) * LANES
    count = parts - 1
    most = call(
        functools.partial(couple_kernel, parts, padded, per, nreg, count),
        struct(rows, wide), [*source, *rough[:count], a_high, a_low, zones],
    )
    relaxed, rim, *back = call(
        functools.partial(relax_kernel, parts, padded, per, nreg, count),
        [struct(rows, per * LANES), struct(rows, LANES)]
        + [struct(per * padded, LANES)] * parts,
        [*rough[count:], most, a_high, a_low, zones],
        [pltpu.VMEM((rows, per * LANES), F32)],
    )
    relaxed = [relaxed]
    beside = [halo(x) for x in relaxed]
    base, back[2] = lax.optimization_barrier((base, back[2]))
    back = exchange(back, B_SWAP)
    part, spread = call(
        functools.partial(plane_kernel, nreg, halves),
        [struct(points, per * LANES)] * 2,
        [*relaxed, rim, zones, b_high, b_low, lift],
    )
    heat = []
    for half in range(halves):
        pieces = call(
            functools.partial(joule_kernel, parts, padded, per, halves, half),
            [struct(per // halves * padded, LANES)] * parts,
            [*beside[half], part, spread, avg, b_high, b_low, w_high, w_low],
            [pltpu.VMEM((rows, per * LANES // halves), F32)],
        )
        heat += exchange(pieces, H_SWAP)
    tiled = [fields, pltpu.SemaphoreType.DMA((padded // SUB,))]
    relaxed_voltage = call(
        functools.partial(gather_kernel, parts, modes, padded, per),
        struct(modes * groups, LANES), back, tiled, out_hbm=True,
    )
    advanced = call(
        functools.partial(final_kernel, parts, modes, padded, per),
        struct(modes * groups, LANES), [*heat, base], tiled, out_hbm=True,
    )
    shape = voltage_expansion.shape
    return relaxed_voltage.reshape(shape), advanced.reshape(shape)


def solution(mesh):
    in_specs = (
        P("modes", "space", None),
        P("modes", "space", None),
        P("modes", "space", None),
        P("space", None),
        P("space", None),
        P(),
        P(),
        P(),
        P(),
    )
    out_specs = (P("modes", "space", None), P("modes", "space", None))
    return jax.shard_map(
        on_device, mesh=mesh, in_specs=in_specs, out_specs=out_specs, check_vma=False
    )
```

```python
import functools

import jax
import jax.numpy as jnp
from jax import lax
from jax.experimental import pallas as pl
from jax.experimental.pallas import tpu as pltpu
from jax.sharding import PartitionSpec as P

NZ = 8
LANES = 128
SUB = 8
TILE16 = 16
VMEM_LIMIT = 40 * 1024 * 1024

HERMITE_NODES = (
    0.0,
    1.355626179974266,
    -1.355626179974266,
    2.8569700138728056,
    -2.8569700138728056,
)

F32 = jnp.float32
BF16 = jnp.bfloat16


def split2(x):
    high = x.astype(BF16)
    return high, (x - high.astype(F32)).astype(BF16)


def dot(a, b):
    return jnp.dot(a, b, preferred_element_type=F32)


def dot_nt(a, b):
    return lax.dot_general(a, b, (((1,), (1,)), ((), ())), preferred_element_type=F32)


def dot3(a_high, a_low, b_high, b_low):
    return dot(a_high, b_high) + (dot(a_high, b_low) + dot(a_low, b_high))


def lane_ids(shape):
    return lax.broadcasted_iota(jnp.int32, shape, len(shape) - 1)


def target_of(route, me, k, parts):
    swap, order = route
    step = order(k, parts) if k else 0
    if swap and parts & (parts - 1) == 0:
        return me ^ step
    return (me + step) % parts if isinstance(me, int) else lax.rem(me + step, parts)


def origin_of(route, me, k, parts):
    swap, order = route
    step = order(k, parts) if k else 0
    if swap and parts & (parts - 1) == 0:
        return me ^ step
    return lax.rem(me + (parts - step), parts)


def upward(k, parts):
    return k


def downward(k, parts):
    return parts - k


def turned(k, parts):
    return 1 + k % (parts - 1)


W_ROUTE, R_ROUTE, B_ROUTE, H_ROUTE = (
    (True, downward),
    (True, upward),
    (False, upward),
    (False, turned),
)


def load_group(ref, group, modes, groups):
    spare = modes % SUB
    main = modes - spare
    if not spare:
        return ref[pl.ds(group, modes, stride=groups), :]
    last = ref[pl.ds((modes - SUB) * groups + group, SUB, stride=groups), :]
    row = lax.broadcasted_iota(jnp.int32, last.shape, 0)
    last = jnp.where(row < spare, pltpu.roll(last, spare, 0), 0.0)
    return jnp.concatenate([ref[pl.ds(group, main, stride=groups), :], last], axis=0)


def emit_slots(route, me, parts, grouped, outs, padded):
    groups = grouped.shape[0] // padded
    per = groups // parts
    lane = lane_ids((padded, LANES))
    for k, out in enumerate(outs):
        q = target_of(route, me, k, parts)
        start = pl.multiple_of(q * (per * padded), SUB)
        out[: per * padded, :] = grouped[pl.ds(start, per * padded), :]
        before = pl.multiple_of(jnp.maximum(q * per - 1, 0) * padded, SUB)
        after = pl.multiple_of(jnp.minimum(q * per + per, groups - 1) * padded, SUB)
        low = pltpu.roll(grouped[pl.ds(before, padded), :], NZ, 1)
        high = pltpu.roll(grouped[pl.ds(after, padded), :], NZ, 1)
        rim = jnp.where((lane < NZ) & (q > 0), low, 0.0)
        rim = jnp.where((lane >= NZ) & (lane < 2 * NZ) & (q < parts - 1), high, rim)
        packed = rim[:SUB]
        for tile in range(1, padded // SUB):
            packed = packed + pltpu.roll(rim[tile * SUB : (tile + 1) * SUB], 2 * NZ * tile, 1)
        out[per * padded :, :] = packed


def source_kernel(parts, modes, padded, v_hbm, j_hbm, a_hbm, *rest):
    outs, (grouped, v_ref, j_ref, a_ref, sems) = rest[:-5], rest[-5:]
    groups = a_ref.shape[0]
    starts = range(0, modes, SUB)
    pairs = [(a_hbm, a_ref)]
    for start in starts:
        rows = pl.ds(start * groups, min(SUB, modes - start) * groups)
        pairs += [(v_hbm.at[rows], v_ref.at[rows]), (j_hbm.at[rows], j_ref.at[rows])]
    copies = [pltpu.make_async_copy(x, y, sems.at[i]) for i, (x, y) in enumerate(pairs)]
    for copy in copies:
        copy.start()
    me = lax.axis_index("modes")
    row = lax.broadcasted_iota(jnp.int32, (SUB, LANES), 0)
    copies[0].wait()
    factor = 0.8 / (6.0 * a_ref[...])
    for tile, start in enumerate(starts):
        copies[2 * tile + 1].wait()
        copies[2 * tile + 2].wait()
        count = min(SUB, modes - start)
        for g in range(groups):
            rows = pl.ds(start * groups + g, SUB, stride=groups)
            w = v_ref[rows, :] + j_ref[rows, :] * factor[g : g + 1]
            if count < SUB:
                w = jnp.where(row < count, w, 0.0)
            grouped[g * padded + start : g * padded + start + SUB, :] = w
    emit_slots(W_ROUTE, me, parts, grouped, outs, padded)


def stencil_groups(x_ref, near_ref, far_ref, modes, groups, padded, emit):
    lane = lane_ids((padded, LANES))
    depth = lane % NZ
    fields = [load_group(x_ref, g, modes, groups) for g in range(groups)]
    for g in range(groups):
        x = fields[g]
        total = 6.0 * x - load_group(near_ref, g, modes, groups)
        total = total - load_group(far_ref, g, modes, groups)
        total = total - jnp.where(depth < NZ - 1, pltpu.roll(x, LANES - 1, 1), 0.0)
        total = total - jnp.where(depth > 0, pltpu.roll(x, 1, 1), 0.0)
        right = fields[g + 1] if g + 1 < groups else jnp.zeros_like(x)
        left = fields[g - 1] if g > 0 else jnp.zeros_like(x)
        total = total - pltpu.roll(jnp.where(lane < NZ, right, x), LANES - NZ, 1)
        total = total - pltpu.roll(jnp.where(lane >= LANES - NZ, left, x), NZ, 1)
        emit(g, x, total)


def rough_kernel(parts, modes, padded, groups, v_ref, near_ref, far_ref, *rest):
    outs, grouped = rest[:-1], rest[-1]
    me = lax.axis_index("modes")

    def emit(g, _, total):
        grouped[g * padded : (g + 1) * padded, :] = total

    stencil_groups(v_ref, near_ref, far_ref, modes, groups, padded, emit)
    emit_slots(R_ROUTE, me, parts, grouped, outs, padded)


def thermal_kernel(modes, padded, groups, t_ref, near_ref, far_ref, out_ref):
    def emit(g, x, total):
        out_ref[g * padded : (g + 1) * padded, :] = x - 0.15 * total

    stencil_groups(t_ref, near_ref, far_ref, modes, groups, padded, emit)


def tables_kernel(
    parts, modes, padded, table_ref, nodes_ref, share_ref, z_ref, zone_ref,
    ah_ref, al_ref, bh_ref, bl_ref, wh_ref, wl_ref, lift_ref, zones_ref,
    cols, basis_t,
):
    nreg, npar = z_ref.shape
    all_modes = parts * modes
    rows = parts * padded
    points = nodes_ref.shape[1]
    me = lax.axis_index("modes")
    kinds = 4 * TILE16

    slot = lax.broadcasted_iota(jnp.int32, (rows, all_modes), 0)
    mode = lax.broadcasted_iota(jnp.int32, (rows, all_modes), 1)
    within = slot % padded
    pick = (within < modes) & (mode == slot // padded * modes + within)
    pick = jnp.where(pick, 1.0, 0.0).astype(BF16)
    table = table_ref[...].astype(F32).astype(BF16)
    spread = lax.broadcasted_iota(jnp.int32, (kinds, npar), 0) % TILE16
    spread = spread == lax.broadcasted_iota(jnp.int32, (kinds, npar), 1)
    table = dot(jnp.where(spread, 1.0, 0.0).astype(BF16), table).astype(BF16)
    along = dot_nt(table, pick)
    down = dot_nt(pick, table)
    cols[...] = down

    def one_hot(values, axis):
        kind = lax.broadcasted_iota(jnp.int32, values.shape, axis)
        row = lax.broadcasted_iota(jnp.int32, values.shape, 1 - axis)
        hit = (values == (kind // TILE16).astype(F32)) & (kind % TILE16 < npar)
        return jnp.where(hit & (row % padded < modes), 1.0, 0.0).astype(BF16)

    hot_down, hot_along = one_hot(down, 1), one_hot(along, 0)
    agree = dot(hot_down, hot_along)
    degree_down = jnp.sum(down[:, :TILE16], axis=1, keepdims=True)
    degree_along = jnp.sum(along[:TILE16], axis=0, keepdims=True)
    linked = (agree == npar - 1.0) & (jnp.abs(degree_down - degree_along) == 1.0)
    same = agree == float(npar)
    left = lax.broadcasted_iota(jnp.int32, (kinds, kinds), 0)
    right = lax.broadcasted_iota(jnp.int32, (kinds, kinds), 1)
    step = (left % TILE16 == right % TILE16) & (jnp.abs(left // TILE16 - right // TILE16) == 1)
    root = jnp.where(step, jnp.sqrt((jnp.maximum(left, right) // TILE16).astype(F32)), 0.0)
    param = lax.broadcasted_iota(jnp.int32, (1, kinds), 1) % TILE16
    hot3 = jnp.concatenate([hot_along] * 3, axis=0)
    matrices = []
    for r in range(nreg):
        weight = jnp.zeros((1, kinds), F32)
        for m in range(npar):
            weight = jnp.where(param == m, z_ref[r, m], weight)
        link = root * weight
        high = link.astype(BF16)
        mid = (link - high.astype(F32)).astype(BF16)
        low = (link - high.astype(F32) - mid.astype(F32)).astype(BF16)
        part = dot(hot_down, jnp.concatenate([high, mid, low], axis=1)).astype(BF16)
        matrices.append(jnp.where(linked, dot(part, hot3), jnp.where(same, 1.0, 0.0)))
    for source in range(parts):
        columns = slice(source * padded, (source + 1) * padded)
        high, low = split2(jnp.concatenate([x[:, columns] for x in matrices], axis=1))
        ah_ref[source] = high
        al_ref[source] = low

    nodes = nodes_ref[...]
    t = jnp.zeros(nodes.shape, F32)
    for which in range(1, len(HERMITE_NODES)):
        t = jnp.where(nodes == which, HERMITE_NODES[which], t)
    h2 = (t * t - 1.0) * (1.0 / 2.0**0.5)
    h3 = (t * t * t - 3.0 * t) * (1.0 / 6.0**0.5)
    share = share_ref[...].astype(F32) * (0.25 / (512.0 * points * all_modes))
    tiles = points // LANES

    def block(b, carry):
        at = pl.multiple_of(b * TILE16, TILE16)
        mine = cols[pl.ds(at, TILE16), :]
        row = lax.broadcasted_iota(jnp.int32, (TILE16, LANES), 0) + at
        basis = [jnp.where(row % padded < modes, 1.0, 0.0)] * tiles
        for m in range(npar):
            own = jnp.broadcast_to(mine[:, m : m + 1], (TILE16, LANES))
            is0, is1, is2 = own == 0.0, own == 1.0, own == 2.0
            for i in range(tiles):
                lanes = slice(i * LANES, (i + 1) * LANES)
                factor = jnp.where(is2, h2[m : m + 1, lanes], h3[m : m + 1, lanes])
                factor = jnp.where(is1, t[m : m + 1, lanes], factor)
                basis[i] = basis[i] * jnp.where(is0, 1.0, factor)
        for i in range(tiles):
            lanes = slice(i * LANES, (i + 1) * LANES)
            basis_t[pl.ds(at, TILE16), lanes] = basis[i]
            high, low = split2(basis[i] * share[:, lanes])
            wh_ref[pl.ds(at, TILE16), lanes] = high
            wl_ref[pl.ds(at, TILE16), lanes] = low
        return carry

    lax.fori_loop(0, rows // TILE16, block, 0)
    high, low = split2(basis_t[...].T)
    bh_ref[...] = high
    bl_ref[...] = low

    terms = []
    for r in range(nreg):
        lift = jnp.ones((1, points), F32)
        for m in range(npar):
            lift = lift + z_ref[r, m] * t[m : m + 1]
        terms.append(lift)
    lift = jnp.concatenate(terms, axis=0)
    high = lift.astype(BF16).astype(F32)
    mid = (lift - high).astype(BF16).astype(F32)
    low = lift - high - mid
    stacked = jnp.concatenate(
        [high, mid, low, jnp.zeros((LANES - 3 * nreg, points), F32)], axis=0
    )
    lift_ref[...] = stacked.T.astype(BF16)

    groups = zone_ref.shape[0]
    per = groups // parts
    zone = zone_ref[...]
    row = lax.broadcasted_iota(jnp.int32, zone.shape, 0)

    def pick_row(g):
        return jnp.sum(jnp.where(row == g, zone, 0), axis=0, keepdims=True)

    for s in range(per):
        zones_ref[:, s * LANES : (s + 1) * LANES] = pick_row(me * per + s)
    low = pltpu.roll(pick_row(jnp.maximum(me * per - 1, 0)), NZ, 1)
    high = pltpu.roll(pick_row(jnp.minimum(me * per + per, groups - 1)), NZ, 1)
    zones_ref[:, per * LANES :] = jnp.where(lane_ids(low.shape) < NZ, low, high)


def unpack(chunk, padded, per):
    packed = chunk[per * padded :, :]
    rims = [packed]
    for tile in range(1, padded // SUB):
        rims.append(pltpu.roll(packed, LANES - 2 * NZ * tile, 1))
    columns = [chunk[s * padded : (s + 1) * padded, :] for s in range(per)]
    return jnp.concatenate(columns + [jnp.concatenate(rims, axis=0)], axis=1)


def coupled(chunk, source, ah_ref, al_ref, zones, nreg, padded, per):
    field = unpack(chunk, padded, per)
    stacked = jnp.concatenate([jnp.where(zones == r, field, 0.0) for r in range(nreg)], axis=0)
    high, low = split2(stacked)
    return dot3(ah_ref[source], al_ref[source], high, low)


def couple_kernel(parts, padded, per, nreg, count, *refs):
    w_refs, r_refs = refs[:parts], refs[parts : parts + count]
    ah_ref, al_ref, zones_ref, out_ref = refs[parts + count :]
    me = lax.axis_index("modes")
    zones = zones_ref[...]
    applied = None
    for k in range(count):
        source = origin_of(R_ROUTE, me, k, parts)
        part = coupled(r_refs[k], source, ah_ref, al_ref, zones, nreg, padded, per)
        applied = part if applied is None else applied + part
    for k in range(parts):
        at = pl.multiple_of(origin_of(W_ROUTE, me, k, parts) * padded, SUB)
        out_ref[pl.ds(at, padded), :] = unpack(w_refs[k], padded, per)
    out_ref[...] = out_ref[...] - (0.8 / 6.0) * applied


def relax_kernel(parts, padded, per, nreg, count, *refs):
    r_refs = refs[: parts - count]
    most_ref, ah_ref, al_ref, zones_ref, rel_ref, rim_ref, *outs, all_ref = refs[parts - count :]
    me = lax.axis_index("modes")
    width = per * LANES
    zones = zones_ref[...]
    applied = None
    for k in range(count, parts):
        source = origin_of(R_ROUTE, me, k, parts)
        part = coupled(r_refs[k - count], source, ah_ref, al_ref, zones, nreg, padded, per)
        applied = part if applied is None else applied + part
    relaxed = most_ref[...] - (0.8 / 6.0) * applied
    rel_ref[...] = relaxed[:, :width]
    rim_ref[...] = relaxed[:, width:]
    all_ref[...] = relaxed[:, :width]
    for k, out in enumerate(outs):
        at = pl.multiple_of(target_of(B_ROUTE, me, k, parts) * padded, SUB)
        for s in range(per):
            out[s * padded : (s + 1) * padded, :] = all_ref[
                pl.ds(at, padded), s * LANES : (s + 1) * LANES
            ]


def plane_kernel(nreg, halves, *refs):
    rel_refs, (rim_ref, zones_ref, bh_ref, bl_ref, lift_ref, part_ref, spread_ref) = (
        refs[:halves], refs[halves:],
    )
    width = sum(ref.shape[1] for ref in rel_refs)
    rel = jnp.concatenate([ref[...] for ref in rel_refs], axis=1)
    rim = rim_ref[...]
    lane = lane_ids(rel.shape)
    depth = lane % NZ
    wide = jnp.concatenate([rim, jnp.zeros((rim.shape[0], width - LANES), F32)], axis=1)
    along_z = jnp.where(depth < NZ - 1, pltpu.roll(rel, width - 1, 1), 0.0)
    along_z = along_z - jnp.where(depth > 0, pltpu.roll(rel, 1, 1), 0.0)
    after = pltpu.roll(wide, width - 2 * NZ, 1)
    along_y = jnp.where(lane >= width - NZ, after, pltpu.roll(rel, width - NZ, 1))
    along_y = along_y - jnp.where(lane < NZ, wide, pltpu.roll(rel, NZ, 1))
    b_high, b_low = bh_ref[...], bl_ref[...]
    total = None
    for grad in (along_y, along_z):
        g_high, g_low = split2(grad)
        at_point = dot3(b_high, b_low, g_high, g_low)
        total = at_point * at_point if total is None else total + at_point * at_point
    row = lax.broadcasted_iota(jnp.int32, (LANES, width), 0)
    hot = (row < 3 * nreg) & (row % nreg == zones_ref[:, :width])
    spread = dot(lift_ref[...], jnp.where(hot, 1.0, 0.0).astype(BF16))
    spread_ref[...] = spread
    part_ref[...] = spread * total


def joule_kernel(
    parts, padded, per, halves, half, near_ref, far_ref, part_ref, spread_ref, a_ref,
    bh_ref, bl_ref, wh_ref, wl_ref, *rest,
):
    outs, heat_ref = rest[:-1], rest[-1]
    me = lax.axis_index("modes")
    own = per // halves
    lanes = slice(half * own * LANES, (half + 1) * own * LANES)
    g_high, g_low = split2(far_ref[...] - near_ref[...])
    at_point = dot3(bh_ref[...], bl_ref[...], g_high, g_low)
    joule = part_ref[:, lanes] + spread_ref[:, lanes] * (at_point * at_point)
    j_high, j_low = split2(joule)
    heat = dot3(wh_ref[...], wl_ref[...], j_high, j_low)
    for s in range(own):
        heat_ref[:, s * LANES : (s + 1) * LANES] = (
            heat[:, s * LANES : (s + 1) * LANES] * a_ref[pl.ds(me * per + half * own + s, 1), :]
        )
    for k, out in enumerate(outs):
        target = target_of(H_ROUTE, me, k, parts)
        at = pl.multiple_of(target * padded, SUB)
        for s in range(own):
            out[s * padded : (s + 1) * padded, :] = heat_ref[
                pl.ds(at, padded), s * LANES : (s + 1) * LANES
            ]


def flat_tiles(modes, groups, write, out_hbm, buffer, sems):
    copies = []
    for tile, start in enumerate(range(0, modes, SUB)):
        count = min(SUB, modes - start)
        write(start)
        rows = pl.ds(start * groups, count * groups)
        copy = pltpu.make_async_copy(buffer.at[rows], out_hbm.at[rows], sems.at[tile])
        copy.start()
        copies.append(copy)
    for copy in copies:
        copy.wait()


def gather_kernel(parts, modes, padded, per, *refs):
    chunks, (out_hbm, buffer, sems) = refs[:parts], refs[parts:]
    me = lax.axis_index("modes")
    groups = parts * per

    def write(start):
        for k in range(parts):
            q = origin_of(B_ROUTE, me, k, parts)
            for s in range(per):
                at = pl.ds(start * groups + q * per + s, SUB, stride=groups)
                buffer[at, :] = chunks[k][s * padded + start : s * padded + start + SUB, :]

    flat_tiles(modes, groups, write, out_hbm, buffer, sems)


def final_kernel(parts, modes, padded, per, *refs):
    chunks, (base, out_hbm, buffer, sems) = refs[:parts], refs[parts:]
    me = lax.axis_index("modes")
    groups = parts * per

    def write(start):
        for k in range(parts):
            q = origin_of(H_ROUTE, me, k, parts)
            for s in range(per):
                at = pl.multiple_of((q * per + s) * padded + start, SUB)
                within = s * padded + start
                rows = base[pl.ds(at, SUB), :] + 0.1 * chunks[k][within : within + SUB, :]
                buffer[pl.ds(start * groups + q * per + s, SUB, stride=groups), :] = rows

    flat_tiles(modes, groups, write, out_hbm, buffer, sems)


def call(kernel, out_shape, args, scratch=(), smem=(), hbm=(), limit=VMEM_LIMIT, out_hbm=False):
    specs = [
        pl.BlockSpec(
            memory_space=pltpu.SMEM if i in smem else pltpu.HBM if i in hbm else pltpu.VMEM
        )
        for i in range(len(args))
    ]
    many = isinstance(out_shape, (list, tuple))
    where = pl.BlockSpec(memory_space=pltpu.HBM if out_hbm else pltpu.VMEM)
    nbytes = sum(x.size * x.dtype.itemsize for x in args)
    return pl.pallas_call(
        kernel,
        out_shape=out_shape,
        in_specs=specs,
        out_specs=[where] * len(out_shape) if many else where,
        scratch_shapes=list(scratch),
        compiler_params=pltpu.CompilerParams(vmem_limit_bytes=limit),
        cost_estimate=pl.CostEstimate(flops=0, bytes_accessed=nbytes, transcendentals=0),
    )(*args)


def exchange(chunks, route):
    parts = lax.axis_size("modes")
    received = list(chunks)
    for k in range(1, parts):
        pairs = [(i, target_of(route, i, k, parts)) for i in range(parts)]
        received[k] = lax.ppermute(chunks[k], "modes", pairs)
    return received


def halo(x):
    count = lax.axis_size("space")
    near = [(i, i ^ 1) for i in range(count) if i ^ 1 < count]
    far = [(i, ((i - 1) ^ 1) + 1) for i in range(1, count) if ((i - 1) ^ 1) + 1 < count]
    far = lax.ppermute(x, "space", far)
    return lax.ppermute(x, "space", near), far


def on_device(
    voltage_expansion,
    current_injection,
    thermal_state,
    average_electric_transport,
    material_zone,
    zone_relative_response,
    polynomial_exponent_rows,
    quadrature_abscissa_choice,
    quadrature_integer_share,
):
    parts = lax.axis_size("modes")
    modes, planes, columns = voltage_expansion.shape
    nreg = zone_relative_response.shape[0]
    points = quadrature_integer_share.shape[0]
    groups = columns // LANES
    per = groups // parts
    padded = -(-modes // SUB) * SUB
    halves = 1
    rows = parts * padded
    assert modes > SUB and planes == 1 and groups * LANES == columns and per * parts == groups
    assert polynomial_exponent_rows.shape[1] <= TILE16 and points % LANES == 0
    assert rows % TILE16 == 0 and 2 * NZ * padded <= SUB * LANES and 3 * nreg <= LANES

    def flat(x):
        return x.reshape(modes * groups, LANES)

    def struct(*shape, dtype=F32):
        return jax.ShapeDtypeStruct(shape, dtype)

    v, cur, temp = flat(voltage_expansion), flat(current_injection), flat(thermal_state)
    avg = average_electric_transport.reshape(groups, LANES)
    zone = material_zone.reshape(groups, LANES)
    rimmed = struct(per * padded + SUB, LANES)
    grouped = pltpu.VMEM((groups * padded, LANES), F32)

    fields = pltpu.VMEM((padded * groups, LANES), F32)
    v_near, v_far = halo(v)
    source = call(
        functools.partial(source_kernel, parts, modes, padded),
        [rimmed] * parts,
        [v, cur, avg],
        [grouped, fields, fields, pltpu.VMEM((groups, LANES), F32), pltpu.SemaphoreType.DMA((1 + 2 * (padded // SUB),))],
        hbm=(0, 1, 2),
        limit=62 * 1024 * 1024,
    )
    source = exchange(source, W_ROUTE)
    temp, source[1] = lax.optimization_barrier((temp, source[1]))
    a_high, a_low, b_high, b_low, w_high, w_low, lift, zones = call(
        functools.partial(tables_kernel, parts, modes, padded),
        [
            struct(parts, rows, nreg * padded, dtype=BF16),
            struct(parts, rows, nreg * padded, dtype=BF16),
            struct(points, rows, dtype=BF16),
            struct(points, rows, dtype=BF16),
            struct(rows, points, dtype=BF16),
            struct(rows, points, dtype=BF16),
            struct(points, LANES, dtype=BF16),
            struct(1, (per + 1) * LANES, dtype=jnp.int32),
        ],
        [
            polynomial_exponent_rows.T,
            quadrature_abscissa_choice.T,
            quadrature_integer_share.reshape(1, points),
            zone_relative_response,
            zone,
        ],
        [pltpu.VMEM((rows, 4 * TILE16), F32), pltpu.VMEM((rows, points), F32)],
        smem=(3,),
    )
    v, zones = lax.optimization_barrier((v, zones))
    rough = call(
        functools.partial(rough_kernel, parts, modes, padded, groups),
        [rimmed] * parts, [v, v_near, v_far], [grouped],
    )
    rough = exchange(rough, R_ROUTE)
    t_near, t_far = halo(temp)
    base = call(
        functools.partial(thermal_kernel, modes, padded, groups),
        struct(groups * padded, LANES), [temp, t_near, t_far],
    )
    wide = (per + 1) * LANES
    count = parts - 1
    most = call(
        functools.partial(couple_kernel, parts, padded, per, nreg, count),
        struct(rows, wide), [*source, *rough[:count], a_high, a_low, zones],
    )
    relaxed, rim, *back = call(
        functools.partial(relax_kernel, parts, padded, per, nreg, count),
        [struct(rows, per * LANES), struct(rows, LANES)]
        + [struct(per * padded, LANES)] * parts,
        [*rough[count:], most, a_high, a_low, zones],
        [pltpu.VMEM((rows, per * LANES), F32)],
    )
    relaxed = [relaxed]
    beside = [halo(x) for x in relaxed]
    base, back[2] = lax.optimization_barrier((base, back[2]))
    back = exchange(back, B_ROUTE)
    part, spread = call(
        functools.partial(plane_kernel, nreg, halves),
        [struct(points, per * LANES)] * 2,
        [*relaxed, rim, zones, b_high, b_low, lift],
    )
    heat = []
    for half in range(halves):
        pieces = call(
            functools.partial(joule_kernel, parts, padded, per, halves, half),
            [struct(per // halves * padded, LANES)] * parts,
            [*beside[half], part, spread, avg, b_high, b_low, w_high, w_low],
            [pltpu.VMEM((rows, per * LANES // halves), F32)],
        )
        heat += exchange(pieces, H_ROUTE)
    tiled = [fields, pltpu.SemaphoreType.DMA((padded // SUB,))]
    relaxed_voltage = call(
        functools.partial(gather_kernel, parts, modes, padded, per),
        struct(modes * groups, LANES), back, tiled, out_hbm=True,
    )
    advanced = call(
        functools.partial(final_kernel, parts, modes, padded, per),
        struct(modes * groups, LANES), [*heat, base], tiled, out_hbm=True,
    )
    shape = voltage_expansion.shape
    return relaxed_voltage.reshape(shape), advanced.reshape(shape)


def solution(mesh):
    in_specs = (
        P("modes", "space", None),
        P("modes", "space", None),
        P("modes", "space", None),
        P("space", None),
        P("space", None),
        P(),
        P(),
        P(),
        P(),
    )
    out_specs = (P("modes", "space", None), P("modes", "space", None))
    return jax.shard_map(
        on_device, mesh=mesh, in_specs=in_specs, out_specs=out_specs, check_vma=False
    )
```

```python
import functools

import jax
import jax.numpy as jnp
from jax import lax
from jax.experimental import pallas as pl
from jax.experimental.pallas import tpu as pltpu
from jax.sharding import PartitionSpec as P

NZ = 8
LANES = 128
SUB = 8
TILE16 = 16
VMEM_LIMIT = 40 * 1024 * 1024

HERMITE_NODES = (
    0.0,
    1.355626179974266,
    -1.355626179974266,
    2.8569700138728056,
    -2.8569700138728056,
)

F32 = jnp.float32
BF16 = jnp.bfloat16


def split2(x):
    high = x.astype(BF16)
    return high, (x - high.astype(F32)).astype(BF16)


def dot(a, b):
    return jnp.dot(a, b, preferred_element_type=F32)


def dot_nt(a, b):
    return lax.dot_general(a, b, (((1,), (1,)), ((), ())), preferred_element_type=F32)


def dot3(a_high, a_low, b_high, b_low):
    return dot(a_high, b_high) + (dot(a_high, b_low) + dot(a_low, b_high))


def lane_ids(shape):
    return lax.broadcasted_iota(jnp.int32, shape, len(shape) - 1)


def target_of(route, me, k, parts):
    swap, order = route
    step = order(k, parts) if k else 0
    if swap and parts & (parts - 1) == 0:
        return me ^ step
    return (me + step) % parts if isinstance(me, int) else lax.rem(me + step, parts)


def origin_of(route, me, k, parts):
    swap, order = route
    step = order(k, parts) if k else 0
    if swap and parts & (parts - 1) == 0:
        return me ^ step
    return lax.rem(me + (parts - step), parts)


def upward(k, parts):
    return k


def longest_first(k, parts):
    return (k - 2) % (parts - 1) + 1


def longest_last(k, parts):
    return parts - 1 - k if k < parts - 1 else k


W_ROUTE = (True, longest_first)
R_ROUTE = (True, longest_last)
B_ROUTE = (False, upward)
H_ROUTE = (False, longest_last)


def load_group(ref, group, modes, groups):
    spare = modes % SUB
    main = modes - spare
    if not spare:
        return ref[pl.ds(group, modes, stride=groups), :]
    last = ref[pl.ds((modes - SUB) * groups + group, SUB, stride=groups), :]
    row = lax.broadcasted_iota(jnp.int32, last.shape, 0)
    last = jnp.where(row < spare, pltpu.roll(last, spare, 0), 0.0)
    return jnp.concatenate([ref[pl.ds(group, main, stride=groups), :], last], axis=0)


def emit_slots(route, me, parts, grouped, outs, padded):
    groups = grouped.shape[0] // padded
    per = groups // parts
    lane = lane_ids((padded, LANES))
    for k, out in enumerate(outs):
        q = target_of(route, me, k, parts)
        start = pl.multiple_of(q * (per * padded), SUB)
        out[: per * padded, :] = grouped[pl.ds(start, per * padded), :]
        before = pl.multiple_of(jnp.maximum(q * per - 1, 0) * padded, SUB)
        after = pl.multiple_of(jnp.minimum(q * per + per, groups - 1) * padded, SUB)
        low = pltpu.roll(grouped[pl.ds(before, padded), :], NZ, 1)
        high = pltpu.roll(grouped[pl.ds(after, padded), :], NZ, 1)
        rim = jnp.where((lane < NZ) & (q > 0), low, 0.0)
        rim = jnp.where((lane >= NZ) & (lane < 2 * NZ) & (q < parts - 1), high, rim)
        packed = rim[:SUB]
        for tile in range(1, padded // SUB):
            packed = packed + pltpu.roll(rim[tile * SUB : (tile + 1) * SUB], 2 * NZ * tile, 1)
        out[per * padded :, :] = packed


def source_kernel(parts, modes, padded, v_hbm, j_hbm, a_hbm, *rest):
    outs, (grouped, v_ref, j_ref, a_ref, sems) = rest[:-5], rest[-5:]
    groups = a_ref.shape[0]
    starts = range(0, modes, SUB)
    pairs = [(a_hbm, a_ref)]
    for start in starts:
        rows = pl.ds(start * groups, min(SUB, modes - start) * groups)
        pairs += [(v_hbm.at[rows], v_ref.at[rows]), (j_hbm.at[rows], j_ref.at[rows])]
    copies = [pltpu.make_async_copy(x, y, sems.at[i]) for i, (x, y) in enumerate(pairs)]
    for copy in copies:
        copy.start()
    me = lax.axis_index("modes")
    row = lax.broadcasted_iota(jnp.int32, (SUB, LANES), 0)
    copies[0].wait()
    factor = 0.8 / (6.0 * a_ref[...])
    for tile, start in enumerate(starts):
        copies[2 * tile + 1].wait()
        copies[2 * tile + 2].wait()
        count = min(SUB, modes - start)
        for g in range(groups):
            rows = pl.ds(start * groups + g, SUB, stride=groups)
            w = v_ref[rows, :] + j_ref[rows, :] * factor[g : g + 1]
            if count < SUB:
                w = jnp.where(row < count, w, 0.0)
            grouped[g * padded + start : g * padded + start + SUB, :] = w
    emit_slots(W_ROUTE, me, parts, grouped, outs, padded)


def stencil_groups(x_ref, near_ref, far_ref, modes, groups, padded, emit):
    lane = lane_ids((padded, LANES))
    depth = lane % NZ
    fields = [load_group(x_ref, g, modes, groups) for g in range(groups)]
    for g in range(groups):
        x = fields[g]
        total = 6.0 * x - load_group(near_ref, g, modes, groups)
        total = total - load_group(far_ref, g, modes, groups)
        total = total - jnp.where(depth < NZ - 1, pltpu.roll(x, LANES - 1, 1), 0.0)
        total = total - jnp.where(depth > 0, pltpu.roll(x, 1, 1), 0.0)
        right = fields[g + 1] if g + 1 < groups else jnp.zeros_like(x)
        left = fields[g - 1] if g > 0 else jnp.zeros_like(x)
        total = total - pltpu.roll(jnp.where(lane < NZ, right, x), LANES - NZ, 1)
        total = total - pltpu.roll(jnp.where(lane >= LANES - NZ, left, x), NZ, 1)
        emit(g, x, total)


def rough_kernel(parts, modes, padded, groups, v_ref, near_ref, far_ref, *rest):
    outs, grouped = rest[:-1], rest[-1]
    me = lax.axis_index("modes")

    def emit(g, _, total):
        grouped[g * padded : (g + 1) * padded, :] = total

    stencil_groups(v_ref, near_ref, far_ref, modes, groups, padded, emit)
    emit_slots(R_ROUTE, me, parts, grouped, outs, padded)


def thermal_kernel(modes, padded, groups, t_ref, near_ref, far_ref, out_ref):
    def emit(g, x, total):
        out_ref[g * padded : (g + 1) * padded, :] = x - 0.15 * total

    stencil_groups(t_ref, near_ref, far_ref, modes, groups, padded, emit)


def tables_kernel(
    parts, modes, padded, table_ref, nodes_ref, share_ref, z_ref, zone_ref,
    ah_ref, al_ref, bh_ref, bl_ref, wh_ref, wl_ref, lift_ref, zones_ref,
    cols, basis_t,
):
    nreg, npar = z_ref.shape
    all_modes = parts * modes
    rows = parts * padded
    points = nodes_ref.shape[1]
    me = lax.axis_index("modes")
    kinds = 4 * TILE16

    slot = lax.broadcasted_iota(jnp.int32, (rows, all_modes), 0)
    mode = lax.broadcasted_iota(jnp.int32, (rows, all_modes), 1)
    within = slot % padded
    pick = (within < modes) & (mode == slot // padded * modes + within)
    pick = jnp.where(pick, 1.0, 0.0).astype(BF16)
    table = table_ref[...].astype(F32).astype(BF16)
    spread = lax.broadcasted_iota(jnp.int32, (kinds, npar), 0) % TILE16
    spread = spread == lax.broadcasted_iota(jnp.int32, (kinds, npar), 1)
    table = dot(jnp.where(spread, 1.0, 0.0).astype(BF16), table).astype(BF16)
    along = dot_nt(table, pick)
    down = dot_nt(pick, table)
    cols[...] = down

    def one_hot(values, axis):
        kind = lax.broadcasted_iota(jnp.int32, values.shape, axis)
        row = lax.broadcasted_iota(jnp.int32, values.shape, 1 - axis)
        hit = (values == (kind // TILE16).astype(F32)) & (kind % TILE16 < npar)
        return jnp.where(hit & (row % padded < modes), 1.0, 0.0).astype(BF16)

    hot_down, hot_along = one_hot(down, 1), one_hot(along, 0)
    agree = dot(hot_down, hot_along)
    degree_down = jnp.sum(down[:, :TILE16], axis=1, keepdims=True)
    degree_along = jnp.sum(along[:TILE16], axis=0, keepdims=True)
    linked = (agree == npar - 1.0) & (jnp.abs(degree_down - degree_along) == 1.0)
    same = agree == float(npar)
    left = lax.broadcasted_iota(jnp.int32, (kinds, kinds), 0)
    right = lax.broadcasted_iota(jnp.int32, (kinds, kinds), 1)
    step = (left % TILE16 == right % TILE16) & (jnp.abs(left // TILE16 - right // TILE16) == 1)
    root = jnp.where(step, jnp.sqrt((jnp.maximum(left, right) // TILE16).astype(F32)), 0.0)
    param = lax.broadcasted_iota(jnp.int32, (1, kinds), 1) % TILE16
    hot3 = jnp.concatenate([hot_along] * 3, axis=0)
    matrices = []
    for r in range(nreg):
        weight = jnp.zeros((1, kinds), F32)
        for m in range(npar):
            weight = jnp.where(param == m, z_ref[r, m], weight)
        link = root * weight
        high = link.astype(BF16)
        mid = (link - high.astype(F32)).astype(BF16)
        low = (link - high.astype(F32) - mid.astype(F32)).astype(BF16)
        part = dot(hot_down, jnp.concatenate([high, mid, low], axis=1)).astype(BF16)
        matrices.append(jnp.where(linked, dot(part, hot3), jnp.where(same, 1.0, 0.0)))
    for source in range(parts):
        columns = slice(source * padded, (source + 1) * padded)
        high, low = split2(jnp.concatenate([x[:, columns] for x in matrices], axis=1))
        ah_ref[source] = high
        al_ref[source] = low

    nodes = nodes_ref[...]
    t = jnp.zeros(nodes.shape, F32)
    for which in range(1, len(HERMITE_NODES)):
        t = jnp.where(nodes == which, HERMITE_NODES[which], t)
    h2 = (t * t - 1.0) * (1.0 / 2.0**0.5)
    h3 = (t * t * t - 3.0 * t) * (1.0 / 6.0**0.5)
    share = share_ref[...].astype(F32) * (0.25 / (512.0 * points * all_modes))
    tiles = points // LANES

    def block(b, carry):
        at = pl.multiple_of(b * TILE16, TILE16)
        mine = cols[pl.ds(at, TILE16), :]
        row = lax.broadcasted_iota(jnp.int32, (TILE16, LANES), 0) + at
        basis = [jnp.where(row % padded < modes, 1.0, 0.0)] * tiles
        for m in range(npar):
            own = jnp.broadcast_to(mine[:, m : m + 1], (TILE16, LANES))
            is0, is1, is2 = own == 0.0, own == 1.0, own == 2.0
            for i in range(tiles):
                lanes = slice(i * LANES, (i + 1) * LANES)
                factor = jnp.where(is2, h2[m : m + 1, lanes], h3[m : m + 1, lanes])
                factor = jnp.where(is1, t[m : m + 1, lanes], factor)
                basis[i] = basis[i] * jnp.where(is0, 1.0, factor)
        for i in range(tiles):
            lanes = slice(i * LANES, (i + 1) * LANES)
            basis_t[pl.ds(at, TILE16), lanes] = basis[i]
            high, low = split2(basis[i] * share[:, lanes])
            wh_ref[pl.ds(at, TILE16), lanes] = high
            wl_ref[pl.ds(at, TILE16), lanes] = low
        return carry

    lax.fori_loop(0, rows // TILE16, block, 0)
    high, low = split2(basis_t[...].T)
    bh_ref[...] = high
    bl_ref[...] = low

    terms = []
    for r in range(nreg):
        lift = jnp.ones((1, points), F32)
        for m in range(npar):
            lift = lift + z_ref[r, m] * t[m : m + 1]
        terms.append(lift)
    lift = jnp.concatenate(terms, axis=0)
    high = lift.astype(BF16).astype(F32)
    mid = (lift - high).astype(BF16).astype(F32)
    low = lift - high - mid
    stacked = jnp.concatenate(
        [high, mid, low, jnp.zeros((LANES - 3 * nreg, points), F32)], axis=0
    )
    lift_ref[...] = stacked.T.astype(BF16)

    groups = zone_ref.shape[0]
    per = groups // parts
    zone = zone_ref[...]
    row = lax.broadcasted_iota(jnp.int32, zone.shape, 0)

    def pick_row(g):
        return jnp.sum(jnp.where(row == g, zone, 0), axis=0, keepdims=True)

    for s in range(per):
        zones_ref[:, s * LANES : (s + 1) * LANES] = pick_row(me * per + s)
    low = pltpu.roll(pick_row(jnp.maximum(me * per - 1, 0)), NZ, 1)
    high = pltpu.roll(pick_row(jnp.minimum(me * per + per, groups - 1)), NZ, 1)
    zones_ref[:, per * LANES :] = jnp.where(lane_ids(low.shape) < NZ, low, high)


def unpack(chunk, padded, per):
    packed = chunk[per * padded :, :]
    rims = [packed]
    for tile in range(1, padded // SUB):
        rims.append(pltpu.roll(packed, LANES - 2 * NZ * tile, 1))
    columns = [chunk[s * padded : (s + 1) * padded, :] for s in range(per)]
    return jnp.concatenate(columns + [jnp.concatenate(rims, axis=0)], axis=1)


def coupled(chunk, source, ah_ref, al_ref, zones, nreg, padded, per):
    field = unpack(chunk, padded, per)
    stacked = jnp.concatenate([jnp.where(zones == r, field, 0.0) for r in range(nreg)], axis=0)
    high, low = split2(stacked)
    return dot3(ah_ref[source], al_ref[source], high, low)


def couple_kernel(parts, padded, per, nreg, count, *refs):
    w_refs, r_refs = refs[:parts], refs[parts : parts + count]
    ah_ref, al_ref, zones_ref, out_ref = refs[parts + count :]
    me = lax.axis_index("modes")
    zones = zones_ref[...]
    applied = None
    for k in range(count):
        source = origin_of(R_ROUTE, me, k, parts)
        part = coupled(r_refs[k], source, ah_ref, al_ref, zones, nreg, padded, per)
        applied = part if applied is None else applied + part
    for k in range(parts):
        at = pl.multiple_of(origin_of(W_ROUTE, me, k, parts) * padded, SUB)
        out_ref[pl.ds(at, padded), :] = unpack(w_refs[k], padded, per)
    out_ref[...] = out_ref[...] - (0.8 / 6.0) * applied


def relax_kernel(parts, padded, per, nreg, count, *refs):
    r_refs = refs[: parts - count]
    most_ref, ah_ref, al_ref, zones_ref, rel_ref, rim_ref, *outs, all_ref = refs[parts - count :]
    me = lax.axis_index("modes")
    width = per * LANES
    zones = zones_ref[...]
    applied = None
    for k in range(count, parts):
        source = origin_of(R_ROUTE, me, k, parts)
        part = coupled(r_refs[k - count], source, ah_ref, al_ref, zones, nreg, padded, per)
        applied = part if applied is None else applied + part
    relaxed = most_ref[...] - (0.8 / 6.0) * applied
    rel_ref[...] = relaxed[:, :width]
    rim_ref[...] = relaxed[:, width:]
    all_ref[...] = relaxed[:, :width]
    for k, out in enumerate(outs):
        at = pl.multiple_of(target_of(B_ROUTE, me, k, parts) * padded, SUB)
        for s in range(per):
            out[s * padded : (s + 1) * padded, :] = all_ref[
                pl.ds(at, padded), s * LANES : (s + 1) * LANES
            ]


def plane_kernel(nreg, halves, *refs):
    rel_refs, (rim_ref, zones_ref, bh_ref, bl_ref, lift_ref, part_ref, spread_ref) = (
        refs[:halves], refs[halves:],
    )
    width = sum(ref.shape[1] for ref in rel_refs)
    rel = jnp.concatenate([ref[...] for ref in rel_refs], axis=1)
    rim = rim_ref[...]
    lane = lane_ids(rel.shape)
    depth = lane % NZ
    wide = jnp.concatenate([rim, jnp.zeros((rim.shape[0], width - LANES), F32)], axis=1)
    along_z = jnp.where(depth < NZ - 1, pltpu.roll(rel, width - 1, 1), 0.0)
    along_z = along_z - jnp.where(depth > 0, pltpu.roll(rel, 1, 1), 0.0)
    after = pltpu.roll(wide, width - 2 * NZ, 1)
    along_y = jnp.where(lane >= width - NZ, after, pltpu.roll(rel, width - NZ, 1))
    along_y = along_y - jnp.where(lane < NZ, wide, pltpu.roll(rel, NZ, 1))
    b_high, b_low = bh_ref[...], bl_ref[...]
    total = None
    for grad in (along_y, along_z):
        g_high, g_low = split2(grad)
        at_point = dot3(b_high, b_low, g_high, g_low)
        total = at_point * at_point if total is None else total + at_point * at_point
    row = lax.broadcasted_iota(jnp.int32, (LANES, width), 0)
    hot = (row < 3 * nreg) & (row % nreg == zones_ref[:, :width])
    spread = dot(lift_ref[...], jnp.where(hot, 1.0, 0.0).astype(BF16))
    spread_ref[...] = spread
    part_ref[...] = spread * total


def joule_kernel(
    parts, padded, per, halves, half, near_ref, far_ref, part_ref, spread_ref, a_ref,
    bh_ref, bl_ref, wh_ref, wl_ref, *rest,
):
    outs, heat_ref = rest[:-1], rest[-1]
    me = lax.axis_index("modes")
    own = per // halves
    lanes = slice(half * own * LANES, (half + 1) * own * LANES)
    g_high, g_low = split2(far_ref[...] - near_ref[...])
    at_point = dot3(bh_ref[...], bl_ref[...], g_high, g_low)
    joule = part_ref[:, lanes] + spread_ref[:, lanes] * (at_point * at_point)
    j_high, j_low = split2(joule)
    heat = dot3(wh_ref[...], wl_ref[...], j_high, j_low)
    for s in range(own):
        heat_ref[:, s * LANES : (s + 1) * LANES] = (
            heat[:, s * LANES : (s + 1) * LANES] * a_ref[pl.ds(me * per + half * own + s, 1), :]
        )
    for k, out in enumerate(outs):
        target = target_of(H_ROUTE, me, k, parts)
        at = pl.multiple_of(target * padded, SUB)
        for s in range(own):
            out[s * padded : (s + 1) * padded, :] = heat_ref[
                pl.ds(at, padded), s * LANES : (s + 1) * LANES
            ]


def flat_tiles(modes, groups, write, out_hbm, buffer, sems):
    copies = []
    for tile, start in enumerate(range(0, modes, SUB)):
        count = min(SUB, modes - start)
        write(start)
        rows = pl.ds(start * groups, count * groups)
        copy = pltpu.make_async_copy(buffer.at[rows], out_hbm.at[rows], sems.at[tile])
        copy.start()
        copies.append(copy)
    for copy in copies:
        copy.wait()


def gather_kernel(parts, modes, padded, per, *refs):
    chunks, (out_hbm, buffer, sems) = refs[:parts], refs[parts:]
    me = lax.axis_index("modes")
    groups = parts * per

    def write(start):
        for k in range(parts):
            q = origin_of(B_ROUTE, me, k, parts)
            for s in range(per):
                at = pl.ds(start * groups + q * per + s, SUB, stride=groups)
                buffer[at, :] = chunks[k][s * padded + start : s * padded + start + SUB, :]

    flat_tiles(modes, groups, write, out_hbm, buffer, sems)


def final_kernel(parts, modes, padded, per, *refs):
    chunks, (base, out_hbm, buffer, sems) = refs[:parts], refs[parts:]
    me = lax.axis_index("modes")
    groups = parts * per

    def write(start):
        for k in range(parts):
            q = origin_of(H_ROUTE, me, k, parts)
            for s in range(per):
                at = pl.multiple_of((q * per + s) * padded + start, SUB)
                within = s * padded + start
                rows = base[pl.ds(at, SUB), :] + 0.1 * chunks[k][within : within + SUB, :]
                buffer[pl.ds(start * groups + q * per + s, SUB, stride=groups), :] = rows

    flat_tiles(modes, groups, write, out_hbm, buffer, sems)


def call(kernel, out_shape, args, scratch=(), smem=(), hbm=(), limit=VMEM_LIMIT, out_hbm=False):
    specs = [
        pl.BlockSpec(
            memory_space=pltpu.SMEM if i in smem else pltpu.HBM if i in hbm else pltpu.VMEM
        )
        for i in range(len(args))
    ]
    many = isinstance(out_shape, (list, tuple))
    where = pl.BlockSpec(memory_space=pltpu.HBM if out_hbm else pltpu.VMEM)
    nbytes = sum(x.size * x.dtype.itemsize for x in args)
    return pl.pallas_call(
        kernel,
        out_shape=out_shape,
        in_specs=specs,
        out_specs=[where] * len(out_shape) if many else where,
        scratch_shapes=list(scratch),
        compiler_params=pltpu.CompilerParams(vmem_limit_bytes=limit),
        cost_estimate=pl.CostEstimate(flops=0, bytes_accessed=nbytes, transcendentals=0),
    )(*args)


def exchange(chunks, route):
    parts = lax.axis_size("modes")
    received = list(chunks)
    for k in range(1, parts):
        pairs = [(i, target_of(route, i, k, parts)) for i in range(parts)]
        received[k] = lax.ppermute(chunks[k], "modes", pairs)
    return received


def halo(x):
    count = lax.axis_size("space")
    near = [(i, i ^ 1) for i in range(count) if i ^ 1 < count]
    far = [(i, ((i - 1) ^ 1) + 1) for i in range(1, count) if ((i - 1) ^ 1) + 1 < count]
    far = lax.ppermute(x, "space", far)
    return lax.ppermute(x, "space", near), far


def on_device(
    voltage_expansion,
    current_injection,
    thermal_state,
    average_electric_transport,
    material_zone,
    zone_relative_response,
    polynomial_exponent_rows,
    quadrature_abscissa_choice,
    quadrature_integer_share,
):
    parts = lax.axis_size("modes")
    modes, planes, columns = voltage_expansion.shape
    nreg = zone_relative_response.shape[0]
    points = quadrature_integer_share.shape[0]
    groups = columns // LANES
    per = groups // parts
    padded = -(-modes // SUB) * SUB
    halves = 1
    rows = parts * padded
    assert modes > SUB and planes == 1 and groups * LANES == columns and per * parts == groups
    assert polynomial_exponent_rows.shape[1] <= TILE16 and points % LANES == 0
    assert rows % TILE16 == 0 and 2 * NZ * padded <= SUB * LANES and 3 * nreg <= LANES

    def flat(x):
        return x.reshape(modes * groups, LANES)

    def struct(*shape, dtype=F32):
        return jax.ShapeDtypeStruct(shape, dtype)

    v, cur, temp = flat(voltage_expansion), flat(current_injection), flat(thermal_state)
    avg = average_electric_transport.reshape(groups, LANES)
    zone = material_zone.reshape(groups, LANES)
    rimmed = struct(per * padded + SUB, LANES)
    grouped = pltpu.VMEM((groups * padded, LANES), F32)

    fields = pltpu.VMEM((padded * groups, LANES), F32)
    v_near, v_far = halo(v)
    source = call(
        functools.partial(source_kernel, parts, modes, padded),
        [rimmed] * parts,
        [v, cur, avg],
        [grouped, fields, fields, pltpu.VMEM((groups, LANES), F32), pltpu.SemaphoreType.DMA((1 + 2 * (padded // SUB),))],
        hbm=(0, 1, 2),
        limit=62 * 1024 * 1024,
    )
    source = exchange(source, W_ROUTE)
    temp, source[1] = lax.optimization_barrier((temp, source[1]))
    a_high, a_low, b_high, b_low, w_high, w_low, lift, zones = call(
        functools.partial(tables_kernel, parts, modes, padded),
        [
            struct(parts, rows, nreg * padded, dtype=BF16),
            struct(parts, rows, nreg * padded, dtype=BF16),
            struct(points, rows, dtype=BF16),
            struct(points, rows, dtype=BF16),
            struct(rows, points, dtype=BF16),
            struct(rows, points, dtype=BF16),
            struct(points, LANES, dtype=BF16),
            struct(1, (per + 1) * LANES, dtype=jnp.int32),
        ],
        [
            polynomial_exponent_rows.T,
            quadrature_abscissa_choice.T,
            quadrature_integer_share.reshape(1, points),
            zone_relative_response,
            zone,
        ],
        [pltpu.VMEM((rows, 4 * TILE16), F32), pltpu.VMEM((rows, points), F32)],
        smem=(3,),
    )
    v, zones = lax.optimization_barrier((v, zones))
    rough = call(
        functools.partial(rough_kernel, parts, modes, padded, groups),
        [rimmed] * parts, [v, v_near, v_far], [grouped],
    )
    rough = exchange(rough, R_ROUTE)
    t_near, t_far = halo(temp)
    base = call(
        functools.partial(thermal_kernel, modes, padded, groups),
        struct(groups * padded, LANES), [temp, t_near, t_far],
    )
    wide = (per + 1) * LANES
    count = parts - 1
    most = call(
        functools.partial(couple_kernel, parts, padded, per, nreg, count),
        struct(rows, wide), [*source, *rough[:count], a_high, a_low, zones],
    )
    relaxed, rim, *back = call(
        functools.partial(relax_kernel, parts, padded, per, nreg, count),
        [struct(rows, per * LANES), struct(rows, LANES)]
        + [struct(per * padded, LANES)] * parts,
        [*rough[count:], most, a_high, a_low, zones],
        [pltpu.VMEM((rows, per * LANES), F32)],
    )
    relaxed = [relaxed]
    beside = [halo(x) for x in relaxed]
    base, back[2] = lax.optimization_barrier((base, back[2]))
    back = exchange(back, B_ROUTE)
    part, spread = call(
        functools.partial(plane_kernel, nreg, halves),
        [struct(points, per * LANES)] * 2,
        [*relaxed, rim, zones, b_high, b_low, lift],
    )
    heat = []
    for half in range(halves):
        pieces = call(
            functools.partial(joule_kernel, parts, padded, per, halves, half),
            [struct(per // halves * padded, LANES)] * parts,
            [*beside[half], part, spread, avg, b_high, b_low, w_high, w_low],
            [pltpu.VMEM((rows, per * LANES // halves), F32)],
        )
        heat += exchange(pieces, H_ROUTE)
    tiled = [fields, pltpu.SemaphoreType.DMA((padded // SUB,))]
    relaxed_voltage = call(
        functools.partial(gather_kernel, parts, modes, padded, per),
        struct(modes * groups, LANES), back, tiled, out_hbm=True,
    )
    advanced = call(
        functools.partial(final_kernel, parts, modes, padded, per),
        struct(modes * groups, LANES), [*heat, base], tiled, out_hbm=True,
    )
    shape = voltage_expansion.shape
    return relaxed_voltage.reshape(shape), advanced.reshape(shape)


def solution(mesh):
    in_specs = (
        P("modes", "space", None),
        P("modes", "space", None),
        P("modes", "space", None),
        P("space", None),
        P("space", None),
        P(),
        P(),
        P(),
        P(),
    )
    out_specs = (P("modes", "space", None), P("modes", "space", None))
    return jax.shard_map(
        on_device, mesh=mesh, in_specs=in_specs, out_specs=out_specs, check_vma=False
    )
```

```python
import functools

import jax
import jax.numpy as jnp
from jax import lax
from jax.experimental import pallas as pl
from jax.experimental.pallas import tpu as pltpu
from jax.sharding import PartitionSpec as P

NZ = 8
LANES = 128
SUB = 8
TILE16 = 16
VMEM_LIMIT = 40 * 1024 * 1024

HERMITE_NODES = (
    0.0,
    1.355626179974266,
    -1.355626179974266,
    2.8569700138728056,
    -2.8569700138728056,
)

F32 = jnp.float32
BF16 = jnp.bfloat16


def split2(x):
    high = x.astype(BF16)
    return high, (x - high.astype(F32)).astype(BF16)


def dot(a, b):
    return jnp.dot(a, b, preferred_element_type=F32)


def dot_nt(a, b):
    return lax.dot_general(a, b, (((1,), (1,)), ((), ())), preferred_element_type=F32)


def dot3(a_high, a_low, b_high, b_low):
    return dot(a_high, b_high) + (dot(a_high, b_low) + dot(a_low, b_high))


def lane_ids(shape):
    return lax.broadcasted_iota(jnp.int32, shape, len(shape) - 1)


def target_of(route, me, k, parts):
    swap, order = route
    step = order(k, parts) if k else 0
    if swap and parts & (parts - 1) == 0:
        return me ^ step
    return (me + step) % parts if isinstance(me, int) else lax.rem(me + step, parts)


def origin_of(route, me, k, parts):
    swap, order = route
    step = order(k, parts) if k else 0
    if swap and parts & (parts - 1) == 0:
        return me ^ step
    return lax.rem(me + (parts - step), parts)


def upward(k, parts):
    return k


def longest_first(k, parts):
    return (k - 2) % (parts - 1) + 1


def longest_last(k, parts):
    return parts - 1 - k if k < parts - 1 else k


W_ROUTE = (True, longest_first)
R_ROUTE = (True, longest_last)
B_ROUTE = (False, upward)
H_ROUTE = (False, longest_last)


def load_group(ref, group, modes, groups):
    spare = modes % SUB
    main = modes - spare
    if not spare:
        return ref[pl.ds(group, modes, stride=groups), :]
    last = ref[pl.ds((modes - SUB) * groups + group, SUB, stride=groups), :]
    row = lax.broadcasted_iota(jnp.int32, last.shape, 0)
    last = jnp.where(row < spare, pltpu.roll(last, spare, 0), 0.0)
    return jnp.concatenate([ref[pl.ds(group, main, stride=groups), :], last], axis=0)


def emit_slots(route, me, parts, grouped, outs, padded):
    groups = grouped.shape[0] // padded
    per = groups // parts
    lane = lane_ids((padded, LANES))
    for k, out in enumerate(outs):
        q = target_of(route, me, k, parts)
        start = pl.multiple_of(q * (per * padded), SUB)
        out[: per * padded, :] = grouped[pl.ds(start, per * padded), :]
        before = pl.multiple_of(jnp.maximum(q * per - 1, 0) * padded, SUB)
        after = pl.multiple_of(jnp.minimum(q * per + per, groups - 1) * padded, SUB)
        low = pltpu.roll(grouped[pl.ds(before, padded), :], NZ, 1)
        high = pltpu.roll(grouped[pl.ds(after, padded), :], NZ, 1)
        rim = jnp.where((lane < NZ) & (q > 0), low, 0.0)
        rim = jnp.where((lane >= NZ) & (lane < 2 * NZ) & (q < parts - 1), high, rim)
        packed = rim[:SUB]
        for tile in range(1, padded // SUB):
            packed = packed + pltpu.roll(rim[tile * SUB : (tile + 1) * SUB], 2 * NZ * tile, 1)
        out[per * padded :, :] = packed


def source_kernel(parts, modes, padded, v_hbm, j_hbm, a_hbm, *rest):
    outs, (grouped, v_ref, j_ref, a_ref, sems) = rest[:-5], rest[-5:]
    groups = a_ref.shape[0]
    starts = range(0, modes, SUB)
    pairs = [(a_hbm, a_ref)]
    for start in starts:
        rows = pl.ds(start * groups, min(SUB, modes - start) * groups)
        pairs += [(v_hbm.at[rows], v_ref.at[rows]), (j_hbm.at[rows], j_ref.at[rows])]
    copies = [pltpu.make_async_copy(x, y, sems.at[i]) for i, (x, y) in enumerate(pairs)]
    for copy in copies:
        copy.start()
    me = lax.axis_index("modes")
    row = lax.broadcasted_iota(jnp.int32, (SUB, LANES), 0)
    copies[0].wait()
    factor = 0.8 / (6.0 * a_ref[...])
    for tile, start in enumerate(starts):
        copies[2 * tile + 1].wait()
        copies[2 * tile + 2].wait()
        count = min(SUB, modes - start)
        for g in range(groups):
            rows = pl.ds(start * groups + g, SUB, stride=groups)
            w = v_ref[rows, :] + j_ref[rows, :] * factor[g : g + 1]
            if count < SUB:
                w = jnp.where(row < count, w, 0.0)
            grouped[g * padded + start : g * padded + start + SUB, :] = w
    emit_slots(W_ROUTE, me, parts, grouped, outs, padded)


def stencil_groups(x_ref, near_ref, far_ref, modes, groups, padded, emit):
    lane = lane_ids((padded, LANES))
    depth = lane % NZ
    fields = [load_group(x_ref, g, modes, groups) for g in range(groups)]
    for g in range(groups):
        x = fields[g]
        total = 6.0 * x - load_group(near_ref, g, modes, groups)
        total = total - load_group(far_ref, g, modes, groups)
        total = total - jnp.where(depth < NZ - 1, pltpu.roll(x, LANES - 1, 1), 0.0)
        total = total - jnp.where(depth > 0, pltpu.roll(x, 1, 1), 0.0)
        right = fields[g + 1] if g + 1 < groups else jnp.zeros_like(x)
        left = fields[g - 1] if g > 0 else jnp.zeros_like(x)
        total = total - pltpu.roll(jnp.where(lane < NZ, right, x), LANES - NZ, 1)
        total = total - pltpu.roll(jnp.where(lane >= LANES - NZ, left, x), NZ, 1)
        emit(g, x, total)


def rough_kernel(parts, modes, padded, groups, v_ref, near_ref, far_ref, *rest):
    outs, grouped = rest[:-1], rest[-1]
    me = lax.axis_index("modes")

    def emit(g, _, total):
        grouped[g * padded : (g + 1) * padded, :] = total

    stencil_groups(v_ref, near_ref, far_ref, modes, groups, padded, emit)
    emit_slots(R_ROUTE, me, parts, grouped, outs, padded)


def thermal_kernel(modes, padded, groups, t_ref, near_ref, far_ref, out_ref):
    def emit(g, x, total):
        out_ref[g * padded : (g + 1) * padded, :] = x - 0.15 * total

    stencil_groups(t_ref, near_ref, far_ref, modes, groups, padded, emit)


def tables_kernel(
    parts, modes, padded, table_ref, nodes_ref, share_ref, z_ref, zone_ref,
    ah_ref, al_ref, bh_ref, bl_ref, wh_ref, wl_ref, lift_ref, zones_ref,
    cols, basis_t,
):
    nreg, npar = z_ref.shape
    all_modes = parts * modes
    rows = parts * padded
    points = nodes_ref.shape[1]
    me = lax.axis_index("modes")
    kinds = 4 * TILE16

    slot = lax.broadcasted_iota(jnp.int32, (rows, all_modes), 0)
    mode = lax.broadcasted_iota(jnp.int32, (rows, all_modes), 1)
    within = slot % padded
    pick = (within < modes) & (mode == slot // padded * modes + within)
    pick = jnp.where(pick, 1.0, 0.0).astype(BF16)
    table = table_ref[...].astype(F32).astype(BF16)
    spread = lax.broadcasted_iota(jnp.int32, (kinds, npar), 0) % TILE16
    spread = spread == lax.broadcasted_iota(jnp.int32, (kinds, npar), 1)
    table = dot(jnp.where(spread, 1.0, 0.0).astype(BF16), table).astype(BF16)
    along = dot_nt(table, pick)
    down = dot_nt(pick, table)
    cols[...] = down

    def one_hot(values, axis):
        kind = lax.broadcasted_iota(jnp.int32, values.shape, axis)
        row = lax.broadcasted_iota(jnp.int32, values.shape, 1 - axis)
        hit = (values == (kind // TILE16).astype(F32)) & (kind % TILE16 < npar)
        return jnp.where(hit & (row % padded < modes), 1.0, 0.0).astype(BF16)

    hot_down, hot_along = one_hot(down, 1), one_hot(along, 0)
    agree = dot(hot_down, hot_along)
    degree_down = jnp.sum(down[:, :TILE16], axis=1, keepdims=True)
    degree_along = jnp.sum(along[:TILE16], axis=0, keepdims=True)
    linked = (agree == npar - 1.0) & (jnp.abs(degree_down - degree_along) == 1.0)
    same = agree == float(npar)
    left = lax.broadcasted_iota(jnp.int32, (kinds, kinds), 0)
    right = lax.broadcasted_iota(jnp.int32, (kinds, kinds), 1)
    step = (left % TILE16 == right % TILE16) & (jnp.abs(left // TILE16 - right // TILE16) == 1)
    root = jnp.where(step, jnp.sqrt((jnp.maximum(left, right) // TILE16).astype(F32)), 0.0)
    param = lax.broadcasted_iota(jnp.int32, (1, kinds), 1) % TILE16
    hot3 = jnp.concatenate([hot_along] * 3, axis=0)
    matrices = []
    for r in range(nreg):
        weight = jnp.zeros((1, kinds), F32)
        for m in range(npar):
            weight = jnp.where(param == m, z_ref[r, m], weight)
        link = root * weight
        high = link.astype(BF16)
        mid = (link - high.astype(F32)).astype(BF16)
        low = (link - high.astype(F32) - mid.astype(F32)).astype(BF16)
        part = dot(hot_down, jnp.concatenate([high, mid, low], axis=1)).astype(BF16)
        matrices.append(jnp.where(linked, dot(part, hot3), jnp.where(same, 1.0, 0.0)))
    for source in range(parts):
        columns = slice(source * padded, (source + 1) * padded)
        high, low = split2(jnp.concatenate([x[:, columns] for x in matrices], axis=1))
        ah_ref[source] = high
        al_ref[source] = low

    nodes = nodes_ref[...]
    t = jnp.zeros(nodes.shape, F32)
    for which in range(1, len(HERMITE_NODES)):
        t = jnp.where(nodes == which, HERMITE_NODES[which], t)
    h2 = (t * t - 1.0) * (1.0 / 2.0**0.5)
    h3 = (t * t * t - 3.0 * t) * (1.0 / 6.0**0.5)
    share = share_ref[...].astype(F32) * (0.25 / (512.0 * points * all_modes))
    tiles = points // LANES

    def block(b, carry):
        at = pl.multiple_of(b * TILE16, TILE16)
        mine = cols[pl.ds(at, TILE16), :]
        row = lax.broadcasted_iota(jnp.int32, (TILE16, LANES), 0) + at
        basis = [jnp.where(row % padded < modes, 1.0, 0.0)] * tiles
        for m in range(npar):
            own = jnp.broadcast_to(mine[:, m : m + 1], (TILE16, LANES))
            is0, is1, is2 = own == 0.0, own == 1.0, own == 2.0
            for i in range(tiles):
                lanes = slice(i * LANES, (i + 1) * LANES)
                factor = jnp.where(is2, h2[m : m + 1, lanes], h3[m : m + 1, lanes])
                factor = jnp.where(is1, t[m : m + 1, lanes], factor)
                basis[i] = basis[i] * jnp.where(is0, 1.0, factor)
        for i in range(tiles):
            lanes = slice(i * LANES, (i + 1) * LANES)
            basis_t[pl.ds(at, TILE16), lanes] = basis[i]
            high, low = split2(basis[i] * share[:, lanes])
            wh_ref[pl.ds(at, TILE16), lanes] = high
            wl_ref[pl.ds(at, TILE16), lanes] = low
        return carry

    lax.fori_loop(0, rows // TILE16, block, 0)
    high, low = split2(basis_t[...].T)
    bh_ref[...] = high
    bl_ref[...] = low

    terms = []
    for r in range(nreg):
        lift = jnp.ones((1, points), F32)
        for m in range(npar):
            lift = lift + z_ref[r, m] * t[m : m + 1]
        terms.append(lift)
    lift = jnp.concatenate(terms, axis=0)
    high = lift.astype(BF16).astype(F32)
    mid = (lift - high).astype(BF16).astype(F32)
    low = lift - high - mid
    stacked = jnp.concatenate(
        [high, mid, low, jnp.zeros((LANES - 3 * nreg, points), F32)], axis=0
    )
    lift_ref[...] = stacked.T.astype(BF16)

    groups = zone_ref.shape[0]
    per = groups // parts
    zone = zone_ref[...]
    row = lax.broadcasted_iota(jnp.int32, zone.shape, 0)

    def pick_row(g):
        return jnp.sum(jnp.where(row == g, zone, 0), axis=0, keepdims=True)

    for s in range(per):
        zones_ref[:, s * LANES : (s + 1) * LANES] = pick_row(me * per + s)
    low = pltpu.roll(pick_row(jnp.maximum(me * per - 1, 0)), NZ, 1)
    high = pltpu.roll(pick_row(jnp.minimum(me * per + per, groups - 1)), NZ, 1)
    zones_ref[:, per * LANES :] = jnp.where(lane_ids(low.shape) < NZ, low, high)


def unpack(chunk, padded, per):
    packed = chunk[per * padded :, :]
    rims = [packed]
    for tile in range(1, padded // SUB):
        rims.append(pltpu.roll(packed, LANES - 2 * NZ * tile, 1))
    columns = [chunk[s * padded : (s + 1) * padded, :] for s in range(per)]
    return jnp.concatenate(columns + [jnp.concatenate(rims, axis=0)], axis=1)


def coupled(chunk, source, ah_ref, al_ref, zones, nreg, padded, per):
    field = unpack(chunk, padded, per)
    stacked = jnp.concatenate([jnp.where(zones == r, field, 0.0) for r in range(nreg)], axis=0)
    high, low = split2(stacked)
    return dot3(ah_ref[source], al_ref[source], high, low)


def couple_kernel(parts, padded, per, nreg, count, *refs):
    w_refs, r_refs = refs[:parts], refs[parts : parts + count]
    ah_ref, al_ref, zones_ref, out_ref = refs[parts + count :]
    me = lax.axis_index("modes")
    zones = zones_ref[...]
    applied = None
    for k in range(count):
        source = origin_of(R_ROUTE, me, k, parts)
        part = coupled(r_refs[k], source, ah_ref, al_ref, zones, nreg, padded, per)
        applied = part if applied is None else applied + part
    for k in range(parts):
        at = pl.multiple_of(origin_of(W_ROUTE, me, k, parts) * padded, SUB)
        out_ref[pl.ds(at, padded), :] = unpack(w_refs[k], padded, per)
    out_ref[...] = out_ref[...] - (0.8 / 6.0) * applied


def relax_kernel(parts, padded, per, nreg, count, *refs):
    r_refs = refs[: parts - count]
    most_ref, ah_ref, al_ref, zones_ref, rel_ref, rim_ref, *outs, all_ref = refs[parts - count :]
    me = lax.axis_index("modes")
    width = per * LANES
    zones = zones_ref[...]
    applied = None
    for k in range(count, parts):
        source = origin_of(R_ROUTE, me, k, parts)
        part = coupled(r_refs[k - count], source, ah_ref, al_ref, zones, nreg, padded, per)
        applied = part if applied is None else applied + part
    relaxed = most_ref[...] - (0.8 / 6.0) * applied
    rel_ref[...] = relaxed[:, :width]
    rim_ref[...] = relaxed[:, width:]
    all_ref[...] = relaxed[:, :width]
    for k, out in enumerate(outs):
        at = pl.multiple_of(target_of(B_ROUTE, me, k, parts) * padded, SUB)
        for s in range(per):
            out[s * padded : (s + 1) * padded, :] = all_ref[
                pl.ds(at, padded), s * LANES : (s + 1) * LANES
            ]


def plane_kernel(nreg, halves, *refs):
    rel_refs, (rim_ref, zones_ref, bh_ref, bl_ref, lift_ref, part_ref, spread_ref) = (
        refs[:halves], refs[halves:],
    )
    width = sum(ref.shape[1] for ref in rel_refs)
    rel = jnp.concatenate([ref[...] for ref in rel_refs], axis=1)
    rim = rim_ref[...]
    lane = lane_ids(rel.shape)
    depth = lane % NZ
    wide = jnp.concatenate([rim, jnp.zeros((rim.shape[0], width - LANES), F32)], axis=1)
    along_z = jnp.where(depth < NZ - 1, pltpu.roll(rel, width - 1, 1), 0.0)
    along_z = along_z - jnp.where(depth > 0, pltpu.roll(rel, 1, 1), 0.0)
    after = pltpu.roll(wide, width - 2 * NZ, 1)
    along_y = jnp.where(lane >= width - NZ, after, pltpu.roll(rel, width - NZ, 1))
    along_y = along_y - jnp.where(lane < NZ, wide, pltpu.roll(rel, NZ, 1))
    b_high, b_low = bh_ref[...], bl_ref[...]
    total = None
    for grad in (along_y, along_z):
        g_high, g_low = split2(grad)
        at_point = dot3(b_high, b_low, g_high, g_low)
        total = at_point * at_point if total is None else total + at_point * at_point
    row = lax.broadcasted_iota(jnp.int32, (LANES, width), 0)
    hot = (row < 3 * nreg) & (row % nreg == zones_ref[:, :width])
    spread = dot(lift_ref[...], jnp.where(hot, 1.0, 0.0).astype(BF16))
    spread_ref[...] = spread
    part_ref[...] = spread * total


def joule_kernel(
    parts, padded, per, halves, half, near_ref, far_ref, part_ref, spread_ref, a_ref,
    bh_ref, bl_ref, wh_ref, wl_ref, *rest,
):
    outs, heat_ref = rest[:-1], rest[-1]
    me = lax.axis_index("modes")
    own = per // halves
    lanes = slice(half * own * LANES, (half + 1) * own * LANES)
    g_high, g_low = split2(far_ref[...] - near_ref[...])
    at_point = dot3(bh_ref[...], bl_ref[...], g_high, g_low)
    joule = part_ref[:, lanes] + spread_ref[:, lanes] * (at_point * at_point)
    j_high, j_low = split2(joule)
    heat = dot3(wh_ref[...], wl_ref[...], j_high, j_low)
    for s in range(own):
        heat_ref[:, s * LANES : (s + 1) * LANES] = (
            heat[:, s * LANES : (s + 1) * LANES] * a_ref[pl.ds(me * per + half * own + s, 1), :]
        )
    for k, out in enumerate(outs):
        target = target_of(H_ROUTE, me, k, parts)
        at = pl.multiple_of(target * padded, SUB)
        for s in range(own):
            out[s * padded : (s + 1) * padded, :] = heat_ref[
                pl.ds(at, padded), s * LANES : (s + 1) * LANES
            ]


def flat_tiles(modes, groups, write, out_hbm, buffer, sems):
    copies = []
    for tile, start in enumerate(range(0, modes, SUB)):
        count = min(SUB, modes - start)
        write(start)
        rows = pl.ds(start * groups, count * groups)
        copy = pltpu.make_async_copy(buffer.at[rows], out_hbm.at[rows], sems.at[tile])
        copy.start()
        copies.append(copy)
    for copy in copies:
        copy.wait()


def gather_kernel(parts, modes, padded, per, *refs):
    chunks, (out_hbm, buffer, sems) = refs[:parts], refs[parts:]
    me = lax.axis_index("modes")
    groups = parts * per

    def write(start):
        for k in range(parts):
            q = origin_of(B_ROUTE, me, k, parts)
            for s in range(per):
                at = pl.ds(start * groups + q * per + s, SUB, stride=groups)
                buffer[at, :] = chunks[k][s * padded + start : s * padded + start + SUB, :]

    flat_tiles(modes, groups, write, out_hbm, buffer, sems)


def final_kernel(parts, modes, padded, per, *refs):
    chunks, (base, out_hbm, buffer, sems) = refs[:parts], refs[parts:]
    me = lax.axis_index("modes")
    groups = parts * per

    def write(start):
        for k in range(parts):
            q = origin_of(H_ROUTE, me, k, parts)
            for s in range(per):
                at = pl.multiple_of((q * per + s) * padded + start, SUB)
                within = s * padded + start
                rows = base[pl.ds(at, SUB), :] + 0.1 * chunks[k][within : within + SUB, :]
                buffer[pl.ds(start * groups + q * per + s, SUB, stride=groups), :] = rows

    flat_tiles(modes, groups, write, out_hbm, buffer, sems)


def call(kernel, out_shape, args, scratch=(), smem=(), hbm=(), limit=VMEM_LIMIT, out_hbm=False):
    specs = [
        pl.BlockSpec(
            memory_space=pltpu.SMEM if i in smem else pltpu.HBM if i in hbm else pltpu.VMEM
        )
        for i in range(len(args))
    ]
    many = isinstance(out_shape, (list, tuple))
    where = pl.BlockSpec(memory_space=pltpu.HBM if out_hbm else pltpu.VMEM)
    nbytes = sum(x.size * x.dtype.itemsize for x in args)
    return pl.pallas_call(
        kernel,
        out_shape=out_shape,
        in_specs=specs,
        out_specs=[where] * len(out_shape) if many else where,
        scratch_shapes=list(scratch),
        compiler_params=pltpu.CompilerParams(vmem_limit_bytes=limit),
        cost_estimate=pl.CostEstimate(flops=0, bytes_accessed=nbytes, transcendentals=0),
    )(*args)


def exchange(chunks, route):
    parts = lax.axis_size("modes")
    received = list(chunks)
    for k in range(1, parts):
        pairs = [(i, target_of(route, i, k, parts)) for i in range(parts)]
        received[k] = lax.ppermute(chunks[k], "modes", pairs)
    return received


def halo(x):
    count = lax.axis_size("space")
    near = [(i, i ^ 1) for i in range(count) if i ^ 1 < count]
    far = [(i, ((i - 1) ^ 1) + 1) for i in range(1, count) if ((i - 1) ^ 1) + 1 < count]
    far = lax.ppermute(x, "space", far)
    return lax.ppermute(x, "space", near), far


def on_device(
    voltage_expansion,
    current_injection,
    thermal_state,
    average_electric_transport,
    material_zone,
    zone_relative_response,
    polynomial_exponent_rows,
    quadrature_abscissa_choice,
    quadrature_integer_share,
):
    parts = lax.axis_size("modes")
    modes, planes, columns = voltage_expansion.shape
    nreg = zone_relative_response.shape[0]
    points = quadrature_integer_share.shape[0]
    groups = columns // LANES
    per = groups // parts
    padded = -(-modes // SUB) * SUB
    halves = 1
    rows = parts * padded
    assert modes > SUB and planes == 1 and groups * LANES == columns and per * parts == groups
    assert polynomial_exponent_rows.shape[1] <= TILE16 and points % LANES == 0
    assert rows % TILE16 == 0 and 2 * NZ * padded <= SUB * LANES and 3 * nreg <= LANES

    def flat(x):
        return x.reshape(modes * groups, LANES)

    def struct(*shape, dtype=F32):
        return jax.ShapeDtypeStruct(shape, dtype)

    v, cur, temp = flat(voltage_expansion), flat(current_injection), flat(thermal_state)
    avg = average_electric_transport.reshape(groups, LANES)
    zone = material_zone.reshape(groups, LANES)
    rimmed = struct(per * padded + SUB, LANES)
    grouped = pltpu.VMEM((groups * padded, LANES), F32)

    fields = pltpu.VMEM((padded * groups, LANES), F32)
    v_near, v_far = halo(v)
    source = call(
        functools.partial(source_kernel, parts, modes, padded),
        [rimmed] * parts,
        [v, cur, avg],
        [grouped, fields, fields, pltpu.VMEM((groups, LANES), F32), pltpu.SemaphoreType.DMA((1 + 2 * (padded // SUB),))],
        hbm=(0, 1, 2),
        limit=62 * 1024 * 1024,
    )
    source = exchange(source, W_ROUTE)
    temp, source[1] = lax.optimization_barrier((temp, source[1]))
    a_high, a_low, b_high, b_low, w_high, w_low, lift, zones = call(
        functools.partial(tables_kernel, parts, modes, padded),
        [
            struct(parts, rows, nreg * padded, dtype=BF16),
            struct(parts, rows, nreg * padded, dtype=BF16),
            struct(points, rows, dtype=BF16),
            struct(points, rows, dtype=BF16),
            struct(rows, points, dtype=BF16),
            struct(rows, points, dtype=BF16),
            struct(points, LANES, dtype=BF16),
            struct(1, (per + 1) * LANES, dtype=jnp.int32),
        ],
        [
            polynomial_exponent_rows.T,
            quadrature_abscissa_choice.T,
            quadrature_integer_share.reshape(1, points),
            zone_relative_response,
            zone,
        ],
        [pltpu.VMEM((rows, 4 * TILE16), F32), pltpu.VMEM((rows, points), F32)],
        smem=(3,),
    )
    v, zones = lax.optimization_barrier((v, zones))
    rough = call(
        functools.partial(rough_kernel, parts, modes, padded, groups),
        [rimmed] * parts, [v, v_near, v_far], [grouped],
    )
    rough = exchange(rough, R_ROUTE)
    t_near, t_far = halo(temp)
    base = call(
        functools.partial(thermal_kernel, modes, padded, groups),
        struct(groups * padded, LANES), [temp, t_near, t_far],
    )
    wide = (per + 1) * LANES
    count = max(1, parts // 2)
    most = call(
        functools.partial(couple_kernel, parts, padded, per, nreg, count),
        struct(rows, wide), [*source, *rough[:count], a_high, a_low, zones],
    )
    relaxed, rim, *back = call(
        functools.partial(relax_kernel, parts, padded, per, nreg, count),
        [struct(rows, per * LANES), struct(rows, LANES)]
        + [struct(per * padded, LANES)] * parts,
        [*rough[count:], most, a_high, a_low, zones],
        [pltpu.VMEM((rows, per * LANES), F32)],
    )
    relaxed = [relaxed]
    beside = [halo(x) for x in relaxed]
    base, back[2] = lax.optimization_barrier((base, back[2]))
    back = exchange(back, B_ROUTE)
    part, spread = call(
        functools.partial(plane_kernel, nreg, halves),
        [struct(points, per * LANES)] * 2,
        [*relaxed, rim, zones, b_high, b_low, lift],
    )
    heat = []
    for half in range(halves):
        pieces = call(
            functools.partial(joule_kernel, parts, padded, per, halves, half),
            [struct(per // halves * padded, LANES)] * parts,
            [*beside[half], part, spread, avg, b_high, b_low, w_high, w_low],
            [pltpu.VMEM((rows, per * LANES // halves), F32)],
        )
        heat += exchange(pieces, H_ROUTE)
    tiled = [fields, pltpu.SemaphoreType.DMA((padded // SUB,))]
    relaxed_voltage = call(
        functools.partial(gather_kernel, parts, modes, padded, per),
        struct(modes * groups, LANES), back, tiled, out_hbm=True,
    )
    advanced = call(
        functools.partial(final_kernel, parts, modes, padded, per),
        struct(modes * groups, LANES), [*heat, base], tiled, out_hbm=True,
    )
    shape = voltage_expansion.shape
    return relaxed_voltage.reshape(shape), advanced.reshape(shape)


def solution(mesh):
    in_specs = (
        P("modes", "space", None),
        P("modes", "space", None),
        P("modes", "space", None),
        P("space", None),
        P("space", None),
        P(),
        P(),
        P(),
        P(),
    )
    out_specs = (P("modes", "space", None), P("modes", "space", None))
    return jax.shard_map(
        on_device, mesh=mesh, in_specs=in_specs, out_specs=out_specs, check_vma=False
    )
```

```python
import functools

import jax
import jax.numpy as jnp
from jax import lax
from jax.experimental import pallas as pl
from jax.experimental.pallas import tpu as pltpu
from jax.sharding import PartitionSpec as P

NZ = 8
LANES = 128
SUB = 8
TILE16 = 16
VMEM_LIMIT = 40 * 1024 * 1024

HERMITE_NODES = (
    0.0,
    1.355626179974266,
    -1.355626179974266,
    2.8569700138728056,
    -2.8569700138728056,
)

F32 = jnp.float32
BF16 = jnp.bfloat16


def split2(x):
    high = x.astype(BF16)
    return high, (x - high.astype(F32)).astype(BF16)


def dot(a, b):
    return jnp.dot(a, b, preferred_element_type=F32)


def dot_nt(a, b):
    return lax.dot_general(a, b, (((1,), (1,)), ((), ())), preferred_element_type=F32)


def dot3(a_high, a_low, b_high, b_low):
    return dot(a_high, b_high) + (dot(a_high, b_low) + dot(a_low, b_high))


def lane_ids(shape):
    return lax.broadcasted_iota(jnp.int32, shape, len(shape) - 1)


def target_of(route, me, k, parts):
    swap, order = route
    step = order(k, parts) if k else 0
    if swap and parts & (parts - 1) == 0:
        return me ^ step
    return (me + step) % parts if isinstance(me, int) else lax.rem(me + step, parts)


def origin_of(route, me, k, parts):
    swap, order = route
    step = order(k, parts) if k else 0
    if swap and parts & (parts - 1) == 0:
        return me ^ step
    return lax.rem(me + (parts - step), parts)


def upward(k, parts):
    return k


def longest_first(k, parts):
    return (k - 2) % (parts - 1) + 1


def longest_last(k, parts):
    return parts - 1 - k if k < parts - 1 else k


W_ROUTE = (True, longest_first)
R_ROUTE = (True, longest_last)
B_ROUTE = (False, upward)
H_ROUTE = (False, longest_last)


def load_group(ref, group, modes, groups):
    spare = modes % SUB
    main = modes - spare
    if not spare:
        return ref[pl.ds(group, modes, stride=groups), :]
    last = ref[pl.ds((modes - SUB) * groups + group, SUB, stride=groups), :]
    row = lax.broadcasted_iota(jnp.int32, last.shape, 0)
    last = jnp.where(row < spare, pltpu.roll(last, spare, 0), 0.0)
    return jnp.concatenate([ref[pl.ds(group, main, stride=groups), :], last], axis=0)


def emit_slots(route, me, parts, grouped, outs, padded):
    groups = grouped.shape[0] // padded
    per = groups // parts
    lane = lane_ids((padded, LANES))
    for k, out in enumerate(outs):
        q = target_of(route, me, k, parts)
        start = pl.multiple_of(q * (per * padded), SUB)
        out[: per * padded, :] = grouped[pl.ds(start, per * padded), :]
        before = pl.multiple_of(jnp.maximum(q * per - 1, 0) * padded, SUB)
        after = pl.multiple_of(jnp.minimum(q * per + per, groups - 1) * padded, SUB)
        low = pltpu.roll(grouped[pl.ds(before, padded), :], NZ, 1)
        high = pltpu.roll(grouped[pl.ds(after, padded), :], NZ, 1)
        rim = jnp.where((lane < NZ) & (q > 0), low, 0.0)
        rim = jnp.where((lane >= NZ) & (lane < 2 * NZ) & (q < parts - 1), high, rim)
        packed = rim[:SUB]
        for tile in range(1, padded // SUB):
            packed = packed + pltpu.roll(rim[tile * SUB : (tile + 1) * SUB], 2 * NZ * tile, 1)
        out[per * padded :, :] = packed


def source_kernel(parts, modes, padded, v_hbm, j_hbm, a_hbm, *rest):
    outs, (grouped, v_ref, j_ref, a_ref, sems) = rest[:-5], rest[-5:]
    groups = a_ref.shape[0]
    starts = range(0, modes, SUB)
    pairs = [(a_hbm, a_ref)]
    for start in starts:
        rows = pl.ds(start * groups, min(SUB, modes - start) * groups)
        pairs += [(v_hbm.at[rows], v_ref.at[rows]), (j_hbm.at[rows], j_ref.at[rows])]
    copies = [pltpu.make_async_copy(x, y, sems.at[i]) for i, (x, y) in enumerate(pairs)]
    for copy in copies:
        copy.start()
    me = lax.axis_index("modes")
    row = lax.broadcasted_iota(jnp.int32, (SUB, LANES), 0)
    copies[0].wait()
    factor = 0.8 / (6.0 * a_ref[...])
    for tile, start in enumerate(starts):
        copies[2 * tile + 1].wait()
        copies[2 * tile + 2].wait()
        count = min(SUB, modes - start)
        for g in range(groups):
            rows = pl.ds(start * groups + g, SUB, stride=groups)
            w = v_ref[rows, :] + j_ref[rows, :] * factor[g : g + 1]
            if count < SUB:
                w = jnp.where(row < count, w, 0.0)
            grouped[g * padded + start : g * padded + start + SUB, :] = w
    emit_slots(W_ROUTE, me, parts, grouped, outs, padded)


def stencil_groups(x_ref, near_ref, far_ref, modes, groups, padded, emit):
    lane = lane_ids((padded, LANES))
    depth = lane % NZ
    fields = [load_group(x_ref, g, modes, groups) for g in range(groups)]
    for g in range(groups):
        x = fields[g]
        total = 6.0 * x - load_group(near_ref, g, modes, groups)
        total = total - load_group(far_ref, g, modes, groups)
        total = total - jnp.where(depth < NZ - 1, pltpu.roll(x, LANES - 1, 1), 0.0)
        total = total - jnp.where(depth > 0, pltpu.roll(x, 1, 1), 0.0)
        right = fields[g + 1] if g + 1 < groups else jnp.zeros_like(x)
        left = fields[g - 1] if g > 0 else jnp.zeros_like(x)
        total = total - pltpu.roll(jnp.where(lane < NZ, right, x), LANES - NZ, 1)
        total = total - pltpu.roll(jnp.where(lane >= LANES - NZ, left, x), NZ, 1)
        emit(g, x, total)


def rough_kernel(parts, modes, padded, groups, v_ref, near_ref, far_ref, *rest):
    outs, grouped = rest[:-1], rest[-1]
    me = lax.axis_index("modes")

    def emit(g, _, total):
        grouped[g * padded : (g + 1) * padded, :] = total

    stencil_groups(v_ref, near_ref, far_ref, modes, groups, padded, emit)
    emit_slots(R_ROUTE, me, parts, grouped, outs, padded)


def thermal_kernel(modes, padded, groups, t_ref, near_ref, far_ref, out_ref):
    def emit(g, x, total):
        out_ref[g * padded : (g + 1) * padded, :] = x - 0.15 * total

    stencil_groups(t_ref, near_ref, far_ref, modes, groups, padded, emit)


def tables_kernel(
    parts, modes, padded, table_ref, nodes_ref, share_ref, z_ref, zone_ref,
    ah_ref, al_ref, bh_ref, bl_ref, wh_ref, wl_ref, lift_ref, zones_ref,
    cols, basis_t,
):
    nreg, npar = z_ref.shape
    all_modes = parts * modes
    rows = parts * padded
    points = nodes_ref.shape[1]
    me = lax.axis_index("modes")
    kinds = 4 * TILE16

    slot = lax.broadcasted_iota(jnp.int32, (rows, all_modes), 0)
    mode = lax.broadcasted_iota(jnp.int32, (rows, all_modes), 1)
    within = slot % padded
    pick = (within < modes) & (mode == slot // padded * modes + within)
    pick = jnp.where(pick, 1.0, 0.0).astype(BF16)
    table = table_ref[...].astype(F32).astype(BF16)
    spread = lax.broadcasted_iota(jnp.int32, (kinds, npar), 0) % TILE16
    spread = spread == lax.broadcasted_iota(jnp.int32, (kinds, npar), 1)
    table = dot(jnp.where(spread, 1.0, 0.0).astype(BF16), table).astype(BF16)
    along = dot_nt(table, pick)
    down = dot_nt(pick, table)
    cols[...] = down

    def one_hot(values, axis):
        kind = lax.broadcasted_iota(jnp.int32, values.shape, axis)
        row = lax.broadcasted_iota(jnp.int32, values.shape, 1 - axis)
        hit = (values == (kind // TILE16).astype(F32)) & (kind % TILE16 < npar)
        return jnp.where(hit & (row % padded < modes), 1.0, 0.0).astype(BF16)

    hot_down, hot_along = one_hot(down, 1), one_hot(along, 0)
    agree = dot(hot_down, hot_along)
    degree_down = jnp.sum(down[:, :TILE16], axis=1, keepdims=True)
    degree_along = jnp.sum(along[:TILE16], axis=0, keepdims=True)
    linked = (agree == npar - 1.0) & (jnp.abs(degree_down - degree_along) == 1.0)
    same = agree == float(npar)
    left = lax.broadcasted_iota(jnp.int32, (kinds, kinds), 0)
    right = lax.broadcasted_iota(jnp.int32, (kinds, kinds), 1)
    step = (left % TILE16 == right % TILE16) & (jnp.abs(left // TILE16 - right // TILE16) == 1)
    root = jnp.where(step, jnp.sqrt((jnp.maximum(left, right) // TILE16).astype(F32)), 0.0)
    param = lax.broadcasted_iota(jnp.int32, (1, kinds), 1) % TILE16
    hot3 = jnp.concatenate([hot_along] * 3, axis=0)
    matrices = []
    for r in range(nreg):
        weight = jnp.zeros((1, kinds), F32)
        for m in range(npar):
            weight = jnp.where(param == m, z_ref[r, m], weight)
        link = root * weight
        high = link.astype(BF16)
        mid = (link - high.astype(F32)).astype(BF16)
        low = (link - high.astype(F32) - mid.astype(F32)).astype(BF16)
        part = dot(hot_down, jnp.concatenate([high, mid, low], axis=1)).astype(BF16)
        matrices.append(jnp.where(linked, dot(part, hot3), jnp.where(same, 1.0, 0.0)))
    for source in range(parts):
        columns = slice(source * padded, (source + 1) * padded)
        high, low = split2(jnp.concatenate([x[:, columns] for x in matrices], axis=1))
        ah_ref[source] = high
        al_ref[source] = low

    nodes = nodes_ref[...]
    t = jnp.zeros(nodes.shape, F32)
    for which in range(1, len(HERMITE_NODES)):
        t = jnp.where(nodes == which, HERMITE_NODES[which], t)
    h2 = (t * t - 1.0) * (1.0 / 2.0**0.5)
    h3 = (t * t * t - 3.0 * t) * (1.0 / 6.0**0.5)
    share = share_ref[...].astype(F32) * (0.25 / (512.0 * points * all_modes))
    tiles = points // LANES

    def block(b, carry):
        at = pl.multiple_of(b * TILE16, TILE16)
        mine = cols[pl.ds(at, TILE16), :]
        row = lax.broadcasted_iota(jnp.int32, (TILE16, LANES), 0) + at
        basis = [jnp.where(row % padded < modes, 1.0, 0.0)] * tiles
        for m in range(npar):
            own = jnp.broadcast_to(mine[:, m : m + 1], (TILE16, LANES))
            is0, is1, is2 = own == 0.0, own == 1.0, own == 2.0
            for i in range(tiles):
                lanes = slice(i * LANES, (i + 1) * LANES)
                factor = jnp.where(is2, h2[m : m + 1, lanes], h3[m : m + 1, lanes])
                factor = jnp.where(is1, t[m : m + 1, lanes], factor)
                basis[i] = basis[i] * jnp.where(is0, 1.0, factor)
        for i in range(tiles):
            lanes = slice(i * LANES, (i + 1) * LANES)
            basis_t[pl.ds(at, TILE16), lanes] = basis[i]
            high, low = split2(basis[i] * share[:, lanes])
            wh_ref[pl.ds(at, TILE16), lanes] = high
            wl_ref[pl.ds(at, TILE16), lanes] = low
        return carry

    lax.fori_loop(0, rows // TILE16, block, 0)
    high, low = split2(basis_t[...].T)
    bh_ref[...] = high
    bl_ref[...] = low

    terms = []
    for r in range(nreg):
        lift = jnp.ones((1, points), F32)
        for m in range(npar):
            lift = lift + z_ref[r, m] * t[m : m + 1]
        terms.append(lift)
    lift = jnp.concatenate(terms, axis=0)
    high = lift.astype(BF16).astype(F32)
    mid = (lift - high).astype(BF16).astype(F32)
    low = lift - high - mid
    stacked = jnp.concatenate(
        [high, mid, low, jnp.zeros((LANES - 3 * nreg, points), F32)], axis=0
    )
    lift_ref[...] = stacked.T.astype(BF16)

    groups = zone_ref.shape[0]
    per = groups // parts
    zone = zone_ref[...]
    row = lax.broadcasted_iota(jnp.int32, zone.shape, 0)

    def pick_row(g):
        return jnp.sum(jnp.where(row == g, zone, 0), axis=0, keepdims=True)

    for s in range(per):
        zones_ref[:, s * LANES : (s + 1) * LANES] = pick_row(me * per + s)
    low = pltpu.roll(pick_row(jnp.maximum(me * per - 1, 0)), NZ, 1)
    high = pltpu.roll(pick_row(jnp.minimum(me * per + per, groups - 1)), NZ, 1)
    zones_ref[:, per * LANES :] = jnp.where(lane_ids(low.shape) < NZ, low, high)


def unpack(chunk, padded, per):
    packed = chunk[per * padded :, :]
    rims = [packed]
    for tile in range(1, padded // SUB):
        rims.append(pltpu.roll(packed, LANES - 2 * NZ * tile, 1))
    columns = [chunk[s * padded : (s + 1) * padded, :] for s in range(per)]
    return jnp.concatenate(columns + [jnp.concatenate(rims, axis=0)], axis=1)


def coupled(chunk, source, ah_ref, al_ref, zones, nreg, padded, per):
    field = unpack(chunk, padded, per)
    stacked = jnp.concatenate([jnp.where(zones == r, field, 0.0) for r in range(nreg)], axis=0)
    high, low = split2(stacked)
    return dot3(ah_ref[source], al_ref[source], high, low)


def couple_kernel(parts, padded, per, nreg, count, *refs):
    w_refs, r_refs = refs[:parts], refs[parts : parts + count]
    ah_ref, al_ref, zones_ref, out_ref = refs[parts + count :]
    me = lax.axis_index("modes")
    zones = zones_ref[...]
    applied = None
    for k in range(count):
        source = origin_of(R_ROUTE, me, k, parts)
        part = coupled(r_refs[k], source, ah_ref, al_ref, zones, nreg, padded, per)
        applied = part if applied is None else applied + part
    for k in range(parts):
        at = pl.multiple_of(origin_of(W_ROUTE, me, k, parts) * padded, SUB)
        out_ref[pl.ds(at, padded), :] = unpack(w_refs[k], padded, per)
    out_ref[...] = out_ref[...] - (0.8 / 6.0) * applied


def relax_kernel(parts, padded, per, nreg, count, *refs):
    r_refs = refs[: parts - count]
    most_ref, ah_ref, al_ref, zones_ref, rel_ref, rim_ref, *outs = refs[parts - count :]
    me = lax.axis_index("modes")
    width = per * LANES
    zones = zones_ref[...]
    applied = None
    for k in range(count, parts):
        source = origin_of(R_ROUTE, me, k, parts)
        part = coupled(r_refs[k - count], source, ah_ref, al_ref, zones, nreg, padded, per)
        applied = part if applied is None else applied + part
    relaxed = most_ref[...] - (0.8 / 6.0) * applied
    rel_ref[...] = relaxed[:, :width]
    rim_ref[...] = relaxed[:, width:]
    for k, out in enumerate(outs):
        at = pl.multiple_of(target_of(B_ROUTE, me, k, parts) * padded, SUB)
        for s in range(per):
            out[s * padded : (s + 1) * padded, :] = rel_ref[
                pl.ds(at, padded), s * LANES : (s + 1) * LANES
            ]


def plane_kernel(nreg, halves, *refs):
    rel_refs, (rim_ref, zones_ref, bh_ref, bl_ref, lift_ref, part_ref, spread_ref) = (
        refs[:halves], refs[halves:],
    )
    width = sum(ref.shape[1] for ref in rel_refs)
    rel = jnp.concatenate([ref[...] for ref in rel_refs], axis=1)
    rim = rim_ref[...]
    lane = lane_ids(rel.shape)
    depth = lane % NZ
    wide = jnp.concatenate([rim, jnp.zeros((rim.shape[0], width - LANES), F32)], axis=1)
    along_z = jnp.where(depth < NZ - 1, pltpu.roll(rel, width - 1, 1), 0.0)
    along_z = along_z - jnp.where(depth > 0, pltpu.roll(rel, 1, 1), 0.0)
    after = pltpu.roll(wide, width - 2 * NZ, 1)
    along_y = jnp.where(lane >= width - NZ, after, pltpu.roll(rel, width - NZ, 1))
    along_y = along_y - jnp.where(lane < NZ, wide, pltpu.roll(rel, NZ, 1))
    b_high, b_low = bh_ref[...], bl_ref[...]
    total = None
    for grad in (along_y, along_z):
        g_high, g_low = split2(grad)
        at_point = dot3(b_high, b_low, g_high, g_low)
        total = at_point * at_point if total is None else total + at_point * at_point
    row = lax.broadcasted_iota(jnp.int32, (LANES, width), 0)
    hot = (row < 3 * nreg) & (row % nreg == zones_ref[:, :width])
    spread = dot(lift_ref[...], jnp.where(hot, 1.0, 0.0).astype(BF16))
    spread_ref[...] = spread
    part_ref[...] = spread * total


def joule_kernel(
    parts, padded, per, halves, half, near_ref, far_ref, part_ref, spread_ref, a_ref,
    bh_ref, bl_ref, wh_ref, wl_ref, *rest,
):
    outs, heat_ref = rest[:-1], rest[-1]
    me = lax.axis_index("modes")
    own = per // halves
    lanes = slice(half * own * LANES, (half + 1) * own * LANES)
    g_high, g_low = split2(far_ref[...] - near_ref[...])
    at_point = dot3(bh_ref[...], bl_ref[...], g_high, g_low)
    joule = part_ref[:, lanes] + spread_ref[:, lanes] * (at_point * at_point)
    j_high, j_low = split2(joule)
    heat = dot3(wh_ref[...], wl_ref[...], j_high, j_low)
    for s in range(own):
        heat_ref[:, s * LANES : (s + 1) * LANES] = (
            heat[:, s * LANES : (s + 1) * LANES] * a_ref[pl.ds(me * per + half * own + s, 1), :]
        )
    for k, out in enumerate(outs):
        target = target_of(H_ROUTE, me, k, parts)
        at = pl.multiple_of(target * padded, SUB)
        for s in range(own):
            out[s * padded : (s + 1) * padded, :] = heat_ref[
                pl.ds(at, padded), s * LANES : (s + 1) * LANES
            ]


def flat_tiles(modes, groups, write, out_hbm, buffer, sems):
    copies = []
    for tile, start in enumerate(range(0, modes, SUB)):
        count = min(SUB, modes - start)
        write(start)
        rows = pl.ds(start * groups, count * groups)
        copy = pltpu.make_async_copy(buffer.at[rows], out_hbm.at[rows], sems.at[tile])
        copy.start()
        copies.append(copy)
    for copy in copies:
        copy.wait()


def gather_kernel(parts, modes, padded, per, *refs):
    chunks, (out_hbm, buffer, sems) = refs[:parts], refs[parts:]
    me = lax.axis_index("modes")
    groups = parts * per

    def write(start):
        for k in range(parts):
            q = origin_of(B_ROUTE, me, k, parts)
            for s in range(per):
                at = pl.ds(start * groups + q * per + s, SUB, stride=groups)
                buffer[at, :] = chunks[k][s * padded + start : s * padded + start + SUB, :]

    flat_tiles(modes, groups, write, out_hbm, buffer, sems)


def final_kernel(parts, modes, padded, per, *refs):
    chunks, (base, out_hbm, buffer, sems) = refs[:parts], refs[parts:]
    me = lax.axis_index("modes")
    groups = parts * per

    def write(start):
        for k in range(parts):
            q = origin_of(H_ROUTE, me, k, parts)
            for s in range(per):
                at = pl.multiple_of((q * per + s) * padded + start, SUB)
                within = s * padded + start
                rows = base[pl.ds(at, SUB), :] + 0.1 * chunks[k][within : within + SUB, :]
                buffer[pl.ds(start * groups + q * per + s, SUB, stride=groups), :] = rows

    flat_tiles(modes, groups, write, out_hbm, buffer, sems)


def call(kernel, out_shape, args, scratch=(), smem=(), hbm=(), limit=VMEM_LIMIT, out_hbm=False):
    specs = [
        pl.BlockSpec(
            memory_space=pltpu.SMEM if i in smem else pltpu.HBM if i in hbm else pltpu.VMEM
        )
        for i in range(len(args))
    ]
    many = isinstance(out_shape, (list, tuple))
    where = pl.BlockSpec(memory_space=pltpu.HBM if out_hbm else pltpu.VMEM)
    nbytes = sum(x.size * x.dtype.itemsize for x in args)
    return pl.pallas_call(
        kernel,
        out_shape=out_shape,
        in_specs=specs,
        out_specs=[where] * len(out_shape) if many else where,
        scratch_shapes=list(scratch),
        compiler_params=pltpu.CompilerParams(vmem_limit_bytes=limit),
        cost_estimate=pl.CostEstimate(flops=0, bytes_accessed=nbytes, transcendentals=0),
    )(*args)


def exchange(chunks, route):
    parts = lax.axis_size("modes")
    received = list(chunks)
    for k in range(1, parts):
        pairs = [(i, target_of(route, i, k, parts)) for i in range(parts)]
        received[k] = lax.ppermute(chunks[k], "modes", pairs)
    return received


def halo(x):
    count = lax.axis_size("space")
    near = [(i, i ^ 1) for i in range(count) if i ^ 1 < count]
    far = [(i, ((i - 1) ^ 1) + 1) for i in range(1, count) if ((i - 1) ^ 1) + 1 < count]
    far = lax.ppermute(x, "space", far)
    return lax.ppermute(x, "space", near), far


def on_device(
    voltage_expansion,
    current_injection,
    thermal_state,
    average_electric_transport,
    material_zone,
    zone_relative_response,
    polynomial_exponent_rows,
    quadrature_abscissa_choice,
    quadrature_integer_share,
):
    parts = lax.axis_size("modes")
    modes, planes, columns = voltage_expansion.shape
    nreg = zone_relative_response.shape[0]
    points = quadrature_integer_share.shape[0]
    groups = columns // LANES
    per = groups // parts
    padded = -(-modes // SUB) * SUB
    halves = 1
    rows = parts * padded
    assert modes > SUB and planes == 1 and groups * LANES == columns and per * parts == groups
    assert polynomial_exponent_rows.shape[1] <= TILE16 and points % LANES == 0
    assert rows % TILE16 == 0 and 2 * NZ * padded <= SUB * LANES and 3 * nreg <= LANES

    def flat(x):
        return x.reshape(modes * groups, LANES)

    def struct(*shape, dtype=F32):
        return jax.ShapeDtypeStruct(shape, dtype)

    v, cur, temp = flat(voltage_expansion), flat(current_injection), flat(thermal_state)
    avg = average_electric_transport.reshape(groups, LANES)
    zone = material_zone.reshape(groups, LANES)
    rimmed = struct(per * padded + SUB, LANES)
    grouped = pltpu.VMEM((groups * padded, LANES), F32)

    fields = pltpu.VMEM((padded * groups, LANES), F32)
    v_near, v_far = halo(v)
    source = call(
        functools.partial(source_kernel, parts, modes, padded),
        [rimmed] * parts,
        [v, cur, avg],
        [grouped, fields, fields, pltpu.VMEM((groups, LANES), F32), pltpu.SemaphoreType.DMA((1 + 2 * (padded // SUB),))],
        hbm=(0, 1, 2),
        limit=62 * 1024 * 1024,
    )
    source = exchange(source, W_ROUTE)
    temp, source[1] = lax.optimization_barrier((temp, source[1]))
    a_high, a_low, b_high, b_low, w_high, w_low, lift, zones = call(
        functools.partial(tables_kernel, parts, modes, padded),
        [
            struct(parts, rows, nreg * padded, dtype=BF16),
            struct(parts, rows, nreg * padded, dtype=BF16),
            struct(points, rows, dtype=BF16),
            struct(points, rows, dtype=BF16),
            struct(rows, points, dtype=BF16),
            struct(rows, points, dtype=BF16),
            struct(points, LANES, dtype=BF16),
            struct(1, (per + 1) * LANES, dtype=jnp.int32),
        ],
        [
            polynomial_exponent_rows.T,
            quadrature_abscissa_choice.T,
            quadrature_integer_share.reshape(1, points),
            zone_relative_response,
            zone,
        ],
        [pltpu.VMEM((rows, 4 * TILE16), F32), pltpu.VMEM((rows, points), F32)],
        smem=(3,),
    )
    v, zones = lax.optimization_barrier((v, zones))
    rough = call(
        functools.partial(rough_kernel, parts, modes, padded, groups),
        [rimmed] * parts, [v, v_near, v_far], [grouped],
    )
    rough = exchange(rough, R_ROUTE)
    t_near, t_far = halo(temp)
    base = call(
        functools.partial(thermal_kernel, modes, padded, groups),
        struct(groups * padded, LANES), [temp, t_near, t_far],
    )
    wide = (per + 1) * LANES
    count = parts - 1
    most = call(
        functools.partial(couple_kernel, parts, padded, per, nreg, count),
        struct(rows, wide), [*source, *rough[:count], a_high, a_low, zones],
    )
    relaxed, rim, *back = call(
        functools.partial(relax_kernel, parts, padded, per, nreg, count),
        [struct(rows, per * LANES), struct(rows, LANES)]
        + [struct(per * padded, LANES)] * parts,
        [*rough[count:], most, a_high, a_low, zones],
    )
    relaxed = [relaxed]
    beside = [halo(x) for x in relaxed]
    base, back[2] = lax.optimization_barrier((base, back[2]))
    back = exchange(back, B_ROUTE)
    part, spread = call(
        functools.partial(plane_kernel, nreg, halves),
        [struct(points, per * LANES)] * 2,
        [*relaxed, rim, zones, b_high, b_low, lift],
    )
    heat = []
    for half in range(halves):
        pieces = call(
            functools.partial(joule_kernel, parts, padded, per, halves, half),
            [struct(per // halves * padded, LANES)] * parts,
            [*beside[half], part, spread, avg, b_high, b_low, w_high, w_low],
            [pltpu.VMEM((rows, per * LANES // halves), F32)],
        )
        heat += exchange(pieces, H_ROUTE)
    tiled = [fields, pltpu.SemaphoreType.DMA((padded // SUB,))]
    relaxed_voltage = call(
        functools.partial(gather_kernel, parts, modes, padded, per),
        struct(modes * groups, LANES), back, tiled, out_hbm=True,
    )
    advanced = call(
        functools.partial(final_kernel, parts, modes, padded, per),
        struct(modes * groups, LANES), [*heat, base], tiled, out_hbm=True,
    )
    shape = voltage_expansion.shape
    return relaxed_voltage.reshape(shape), advanced.reshape(shape)


def solution(mesh):
    in_specs = (
        P("modes", "space", None),
        P("modes", "space", None),
        P("modes", "space", None),
        P("space", None),
        P("space", None),
        P(),
        P(),
        P(),
        P(),
    )
    out_specs = (P("modes", "space", None), P("modes", "space", None))
    return jax.shard_map(
        on_device, mesh=mesh, in_specs=in_specs, out_specs=out_specs, check_vma=False
    )
```
